128 devices in a mesh: pipe: 2 (over core), dp: 32 (over x_hi, z, y), seq: 2 (over x_lo).
Axes of the slice: x: 4 (x_hi: 2, x_lo: 2; x = x_hi * 2 + x_lo), y: 4, z: 4, core: 2. Of those that a mesh axis runs over, the one named last changes fastest.
Arguments:
- activations: float32 [4, 32768, 256], P(None, ('dp', 'seq')), may hold values from -6 to 6
- cotangent: float32 [4, 32768, 256], P(None, ('dp', 'seq')), may hold values from -6 to 6
- cell_lengths: int32 [4, 32, 3], P(None, 'dp'), may hold values from 0 to 1023, as said below
- w_qkv: float32 [2, 256, 768], P('pipe'), may hold values from -0.375 to 0.375
- b_qv: float32 [2, 512], P('pipe'), may hold values from -3 to 3
- w_out: float32 [2, 256, 256], P('pipe'), may hold values from -1.5 to 1.5
- b_out: float32 [2, 256], P('pipe'), may hold values from -3 to 3
- gain_one: float32 [2, 256], P('pipe'), may hold values from 0.5 to 1.5
- shift_one: float32 [2, 256], P('pipe'), may hold values from -3 to 3
- w_in: float32 [2, 256, 512], P('pipe'), may hold values from -0.375 to 0.375
- b_in: float32 [2, 512], P('pipe'), may hold values from -3 to 3
- w_back: float32 [2, 512, 256], P('pipe'), may hold values from -0.25 to 0.25
- b_back: float32 [2, 256], P('pipe'), may hold values from -3 to 3
- gain_two: float32 [2, 256], P('pipe'), may hold values from 0.5 to 1.5
- shift_two: float32 [2, 256], P('pipe'), may hold values from -3 to 3
Outputs:
- final_output: float32 [4, 32768, 256], P('pipe', ('dp', 'seq'))
- input_grad: float32 [4, 32768, 256], P('pipe', ('dp', 'seq'))
- grad_w_qkv: float32 [2, 256, 768], P('pipe')
- grad_b_qv: float32 [2, 512], P('pipe')
- grad_w_out: float32 [2, 256, 256], P('pipe')
- grad_b_out: float32 [2, 256], P('pipe')
- grad_gain_one: float32 [2, 256], P('pipe')
- grad_shift_one: float32 [2, 256], P('pipe')
- grad_w_in: float32 [2, 256, 512], P('pipe')
- grad_b_in: float32 [2, 512], P('pipe')
- grad_w_back: float32 [2, 512, 256], P('pipe')
- grad_b_back: float32 [2, 256], P('pipe')
- grad_gain_two: float32 [2, 256], P('pipe')
- grad_shift_two: float32 [2, 256], P('pipe')
The draws below stay inside these ranges and needn't reach their ends.
Inputs may be any that keep to these rules, and one draw needn't show every extreme that they name: cell_lengths[m, g] lists three cells packed from the start of group g's slot of micro-batch m: the first has 1 to 256 tokens, the last 0 to 256, the middle one the rest, and the middle one always covers place 512 of the slot. Together they fill 512 + 512 // 8 to 1024 places. In every micro-batch one group fills exactly 1024 places with a middle cell of 1023 tokens and an empty last cell.
All inputs are finite; a program needn't handle non-finite values.
Results may differ from the reference program's by a relative error of at most 0.0003.
Values sent between devices are 32-bit elements; how exact they have to be, the bound alone decides.
A program may use at most 256 MiB of HBM per device.

```python
import math
import jax
import jax.numpy as jnp
from jax import lax

D = 256
HEADS = 4
FF = 512
ROWS = 512
MICRO = 4
CELLS = 3
SHORT = 256
SLOT = 1024
GROUPS = 32
TOKENS = 32768
SECTIONS = 2


def draw_cell_lengths(key, part):
    key = jax.random.fold_in(key, 7)
    fill_key, full_key, first_key, last_key = jax.random.split(key, 4)
    filled = jax.random.randint(fill_key, (MICRO, GROUPS), ROWS + ROWS // 8, SLOT + 1)
    fullest = jax.random.randint(full_key, (MICRO, 1), 0, GROUPS)
    is_full = jnp.arange(GROUPS)[None, :] == fullest
    filled = jnp.where(is_full, SLOT, filled)
    first_cell = jax.random.randint(first_key, (MICRO, GROUPS), 1, SHORT + 1)
    first_cell = jnp.where(is_full, 1, first_cell)
    last_room = jnp.minimum(SHORT, filled - ROWS - 1)
    last_cell = jax.random.randint(last_key, (MICRO, GROUPS), 0, last_room + 1)
    last_cell = jnp.where(is_full, 0, last_cell)
    middle_cell = filled - first_cell - last_cell
    return jnp.stack([first_cell, middle_cell, last_cell], axis=-1).astype(jnp.int32)


def steps_of(own_key, dims, cuts, low, top_value):
    def one(position, shards_of):
        heights = jax.random.uniform(jax.random.fold_in(jax.random.fold_in(own_key, 6), position), (shards_of,), jnp.float32, low / len(cuts), top_value / len(cuts))
        return jnp.repeat(jnp.exp(heights), dims[position] // shards_of).reshape((-1,) + (1,) * (len(dims) - position - 1))

    gain = one(*cuts[0])
    for cut in cuts[1:]:
        gain = gain * one(*cut)
    return gain


def normal_values(own_key, dims, scale, reach, cuts=(), dtype=jnp.bfloat16):
    drawn = jax.random.normal(own_key, dims, jnp.float32) * scale
    if len(cuts) > 0:
        drawn = steps_of(own_key, dims, cuts, -0.22, 0.18) * drawn
    return jnp.clip(drawn, min=-reach, max=reach).astype(dtype)


def setup_inputs(seed: int = 0) -> dict:
    key_list = jax.random.split(jax.random.key(seed), 16)
    return {
        "activations": normal_values(key_list[0], (MICRO, TOKENS, D), 1.0, 6.0, ((1, 64),), jnp.float32),
        "cotangent": normal_values(key_list[1], (MICRO, TOKENS, D), 1.0, 6.0, ((1, 64),), jnp.float32),
        "cell_lengths": draw_cell_lengths(jax.random.fold_in(key_list[15], 71), 0),
        "w_qkv": normal_values(key_list[3], (SECTIONS, D, 3 * D), D ** -0.5, 0.375, ((0, 2),), jnp.float32),
        "b_qv": normal_values(key_list[4], (SECTIONS, 2 * D), 0.5, 3.0, ((0, 2),), jnp.float32),
        "w_out": normal_values(key_list[5], (SECTIONS, D, D), (D // 16) ** -0.5, 1.5, ((0, 2),), jnp.float32),
        "b_out": normal_values(key_list[6], (SECTIONS, D), 0.5, 3.0, ((0, 2),), jnp.float32),
        "gain_one": jnp.clip(1.0 + 0.1 * jax.random.normal(key_list[7], (SECTIONS, D), jnp.float32), 0.5, 1.5),
        "shift_one": normal_values(key_list[8], (SECTIONS, D), 0.5, 3.0, ((0, 2),), jnp.float32),
        "w_in": normal_values(key_list[9], (SECTIONS, D, FF), D ** -0.5, 0.375, ((0, 2),), jnp.float32),
        "b_in": normal_values(key_list[10], (SECTIONS, FF), 0.5, 3.0, ((0, 2),), jnp.float32),
        "w_back": normal_values(key_list[11], (SECTIONS, FF, D), FF ** -0.5, 0.25, ((0, 2),), jnp.float32),
        "b_back": normal_values(key_list[12], (SECTIONS, D), 0.5, 3.0, ((0, 2),), jnp.float32),
        "gain_two": jnp.clip(1.0 + 0.1 * jax.random.normal(key_list[13], (SECTIONS, D), jnp.float32), 0.5, 1.5),
        "shift_two": normal_values(key_list[14], (SECTIONS, D), 0.5, 3.0, ((0, 2),), jnp.float32),
    }


PRECISE = lax.Precision.HIGHEST
EPSILON = 1e-06
NEGATIVE = -1e+30

def layer_norm(values, gain_vector, bias_vector):
    center = values - lax.optimization_barrier(jnp.mean(values, axis=-1, keepdims=True))
    spread = lax.optimization_barrier(jnp.mean(center * center, axis=-1, keepdims=True))
    return center * lax.rsqrt(spread + EPSILON) * gain_vector + bias_vector

def segments(positions, cell_ends):
    return lax.optimization_barrier(jnp.sum((positions[:, None] >= cell_ends[None, :]).astype(jnp.int32), axis=1)).astype(jnp.int32)

def one_layer(layer_in, cell_ids, live_rows, params):
    w_qkv, b_qv, w_out, b_out, gain_one, shift_one, w_in, b_in, w_back, b_back, gain_two, shift_two = params
    row_count = layer_in.shape[0]
    model_width = layer_in.shape[1]
    head_size = model_width // HEADS
    joined = jnp.dot(layer_in, w_qkv, precision=PRECISE)
    queries = (joined[:, :model_width] + b_qv[:model_width]).reshape(row_count, HEADS, head_size)
    key_rows = joined[:, model_width:2 * model_width].reshape(row_count, HEADS, head_size)
    value_rows = (joined[:, 2 * model_width:] + b_qv[model_width:]).reshape(row_count, HEADS, head_size)
    scores = jnp.einsum('qhd,khd->hqk', queries, key_rows, precision=PRECISE) * (1.0 / math.sqrt(head_size))
    allowed = (cell_ids[:, None] == cell_ids[None, :])[None]
    masked = jnp.where(allowed, scores, NEGATIVE)
    row_max = lax.optimization_barrier(jnp.max(masked, axis=2, keepdims=True))
    weights = jnp.where(allowed, jnp.exp(masked - row_max), 0.0)
    probabilities = weights / lax.optimization_barrier(jnp.sum(weights, axis=2, keepdims=True))
    context = jnp.einsum('hqk,khd->qhd', probabilities, value_rows, precision=PRECISE).reshape(row_count, model_width)
    upper_sum = layer_in + jnp.dot(context, w_out, precision=PRECISE) + b_out
    hidden = layer_norm(upper_sum, gain_one, shift_one)
    inner_act = jax.nn.gelu(jnp.dot(hidden, w_in, precision=PRECISE) + b_in, approximate=False)
    lower_sum = hidden + jnp.dot(inner_act, w_back, precision=PRECISE) + b_back
    return layer_norm(lower_sum, gain_two, shift_two) * live_rows[:, None]

def slot_forward(slot_rows, slot_lengths, stacked):
    cell_ends = jnp.cumsum(slot_lengths).astype(jnp.int32)
    cell_ids = segments(jnp.arange(slot_rows.shape[0]).astype(jnp.int32), cell_ends)
    live_rows = (cell_ids < slot_lengths.shape[0]).astype(jnp.float32)
    for layer_index in range(SECTIONS):
        slot_rows = one_layer(slot_rows, cell_ids, live_rows, tuple((weight[layer_index] for weight in stacked)))
    return slot_rows

def forward(activations, stacked, cell_lengths):
    micro_count = activations.shape[0]
    slot_rows = activations.reshape(micro_count * GROUPS, SLOT, activations.shape[2])
    slot_lengths = cell_lengths.reshape(micro_count * GROUPS, CELLS)
    checked = jax.checkpoint(slot_forward)

    def run_slot(slot_pair):
        return checked(slot_pair[0], slot_pair[1], stacked)
    outputs = lax.map(run_slot, (slot_rows, slot_lengths))
    return outputs.reshape(activations.shape)

def reference(activations, cotangent, cell_lengths, w_qkv, b_qv, w_out, b_out, gain_one, shift_one, w_in, b_in, w_back, b_back, gain_two, shift_two):
    stacked = (w_qkv, b_qv, w_out, b_out, gain_one, shift_one, w_in, b_in, w_back, b_back, gain_two, shift_two)

    def apply_all(given_acts, given_weights):
        return forward(given_acts, given_weights, cell_lengths)
    final_output, pullback = jax.vjp(apply_all, activations, stacked)
    input_grad, weight_grads = pullback(cotangent)
    grad_w_qkv, grad_b_qv, grad_w_out, grad_b_out, grad_gain_one, grad_shift_one, grad_w_in, grad_b_in, grad_w_back, grad_b_back, grad_gain_two, grad_shift_two = weight_grads
    return (final_output, input_grad, grad_w_qkv, grad_b_qv, grad_w_out, grad_b_out, grad_gain_one, grad_shift_one, grad_w_in, grad_b_in, grad_w_back, grad_b_back, grad_gain_two, grad_shift_two)
```

```python
import math

import jax
import jax.numpy as jnp
from jax import lax
from jax.experimental import pallas as pl
from jax.experimental.pallas import tpu as pltpu
from jax.sharding import PartitionSpec as P

MESH = pl.DeviceIdType.MESH
F32 = jnp.float32
BF16 = jnp.bfloat16

HEADS = 4
HEAD = 64
WIDTH = 256
INNER = 512
HALF = 512
SLOT = 1024
BLOCK = 256
BLOCKS = SLOT // BLOCK
EPSILON = 1e-06
APART = -1e30
LOG2E = math.log2(math.e)
LN2 = math.log(2.0)
QUERY_SCALE = LOG2E / math.sqrt(HEAD)
KEY_SCALE = 1.0 / math.sqrt(HEAD)

AT_QKV, AT_OUT, AT_IN, AT_BACK, AT_SMALL = 0, 768, 1024, 1536, 2048
MATRIX_ROWS = 2048
SMALL_ROWS = 16
PACKED_ROWS = MATRIX_ROWS + SMALL_ROWS
V_Q, V_V, V_OUT, V_GAIN1, V_SHIFT1, V_IN, V_BACK, V_GAIN2, V_SHIFT2 = 0, 1, 2, 3, 4, 5, 7, 8, 9


def dot(left, right, left_t=False, right_t=False):
    dims = (((0 if left_t else 1,), (1 if right_t else 0,)), ((), ()))
    return lax.dot_general(left, right, dims, preferred_element_type=F32)


def split(values):
    high = values.astype(BF16)
    return high, (values - high.astype(F32)).astype(BF16)


def dot3(left_high, left_low, right_high, right_low, right_t=False):
    return (
        dot(left_high, right_high, right_t=right_t)
        + dot(left_high, right_low, right_t=right_t)
        + dot(left_low, right_high, right_t=right_t)
    )


def col_mean(values):
    return jnp.mean(values, axis=0, keepdims=True)


def norm_rows(values):
    center = values - col_mean(values)
    spread = col_mean(center * center)
    inverse = lax.rsqrt(spread + EPSILON)
    return center * inverse, inverse


def norm_back(grad, normed, inverse):
    return (grad - col_mean(grad) - normed * col_mean(grad * normed)) * inverse


def feature_tile(base, values, first):
    high = values.astype(BF16).astype(F32)
    rest = values - high
    middle = rest.astype(BF16).astype(F32)
    low = rest - middle
    row = lax.broadcasted_iota(jnp.int32, base.shape, 0)
    tile = jnp.where(row == first, high, base)
    tile = jnp.where(row == first + 1, middle, tile)
    return jnp.where(row == first + 2, low, tile).astype(BF16)


def lane_fold(values):
    folded = values[:, :128]
    for first in range(128, values.shape[1], 128):
        folded = folded + values[:, first:first + 128]
    return folded


def relay_kernel(
    act_ref, cot_ref, len_ref, w_qkv_ref, w_out_ref, w_in_ref, w_back_ref, vec_ref,
    final_ref, grad_ref, packed_ref,
    x_in, c_in, w_qkv, w_out, w_in, w_back, vecs,
    fq, fo, fi, fb, nq, no, ni, nb, cols,
    marks, live, x_now, x_parts, q_all, k_all, v_all, ctx_parts,
    n_one, r_one, hid_parts, slope, inner_parts, n_two, r_two,
    d_now, dl_parts, dp_parts, du_now, du_parts, do_all, dkv, dqkv, sums, packed,
    local_sem, send_sem, recv_sem,
):
    core = lax.axis_index("pipe")
    half = lax.axis_index("seq")
    sibling = {"pipe": 1 - core}
    partner = {"seq": 1 - half}

    barrier = pltpu.get_barrier_semaphore()
    pl.semaphore_signal(barrier, inc=1, device_id=sibling, device_id_type=MESH)
    pl.semaphore_signal(barrier, inc=1, device_id=partner, device_id_type=MESH)
    pl.semaphore_wait(barrier, 2)

    def remote(src, dst, index, device):
        return pltpu.make_async_remote_copy(
            src_ref=src, dst_ref=dst, send_sem=send_sem.at[index], recv_sem=recv_sem.at[index],
            device_id=device, device_id_type=MESH,
        )

    mine = 2 * core + half
    theirs = 2 * core + 1 - half
    weight_pairs = (
        (w_qkv_ref, w_qkv), (w_out_ref, w_out), (w_in_ref, w_in), (w_back_ref, w_back), (vec_ref, vecs),
    )
    x_send = remote(act_ref.at[theirs], x_in.at[1], 0, partner)
    c_send = remote(cot_ref.at[theirs], c_in.at[1], 1, partner)
    w_sends = [remote(src.at[0], dst.at[core], 2 + i, sibling) for i, (src, dst) in enumerate(weight_pairs)]
    x_own = pltpu.make_async_copy(act_ref.at[mine], x_in.at[0], local_sem.at[0])
    c_own = pltpu.make_async_copy(cot_ref.at[mine], c_in.at[0], local_sem.at[1])
    w_owns = [
        pltpu.make_async_copy(src.at[0], dst.at[core], local_sem.at[2 + i])
        for i, (src, dst) in enumerate(weight_pairs)
    ]
    x_send.start()
    for copy in w_sends:
        copy.start()
    x_own.start()
    for copy in w_owns:
        copy.start()
    c_own.start()

    lane = lax.broadcasted_iota(jnp.int32, (16, SLOT), 1)
    row = lax.broadcasted_iota(jnp.int32, (16, SLOT), 0)
    place = jnp.where(lane < HALF, half * HALF + lane, (1 - half) * HALF + lane - HALF)
    end_0 = len_ref[mine, 0, 0]
    end_1 = end_0 + len_ref[mine, 0, 1]
    end_2 = end_1 + len_ref[mine, 0, 2]
    one = jnp.ones_like(place)
    none = jnp.zeros_like(place)
    cell = (
        jnp.where(place >= end_0, one, none)
        + jnp.where(place >= end_1, one, none)
        + jnp.where(place >= end_2, one, none)
    )
    same = jnp.where(cell == row, 1.0, 0.0)
    marks[...] = same
    live[...] = jnp.where(cell < 3, 1.0, 0.0)[:8]
    key_marks = jnp.where(row < 4, (1.0 - same) * APART, jnp.where(row < 7, 1.0, 0.0)).astype(BF16)
    value_marks = jnp.where(row < 3, 1.0, 0.0).astype(BF16)
    query_marks = same.astype(BF16)
    blank = jnp.zeros((48, SLOT), BF16)
    for layer in range(2):
        for head in range(HEADS):
            q_all[layer, head, 192:208, :] = query_marks
            k_all[layer, head, 192:208, :] = key_marks
            v_all[layer, head, 192:208, :] = value_marks
            q_all[layer, head, 208:256, :] = blank
            k_all[layer, head, 208:256, :] = blank
            v_all[layer, head, 208:256, :] = blank
    for head in range(HEADS):
        do_all[head, 208:256, :] = blank

    for copy in w_owns:
        copy.wait()
    for copy in w_sends:
        copy.wait()
    x_own.wait()
    x_send.wait()
    c_send.start()

    first_x = jnp.concatenate([x_in[0].T, x_in[1].T], axis=1)
    x_now[...] = first_x

    def forward(layer, carry):
        cols[...] = jnp.concatenate([vecs[layer].T, jnp.zeros((WIDTH, 128 - SMALL_ROWS), F32)], axis=1)

        def col(index):
            return cols[:, index:index + 1]

        fq[0], fq[1] = split(w_qkv[layer].T)
        fo[0], fo[1] = split(w_out[layer].T)
        fi[0], fi[1] = split(w_in[layer].T)
        fb[0], fb[1] = split(w_back[layer].T)
        x_parts[layer, 0], x_parts[layer, 1] = split(x_now[...])

        for block in range(BLOCKS):
            at = slice(block * BLOCK, (block + 1) * BLOCK)
            joined = dot3(fq[0], fq[1], x_parts[layer, 0, :, at], x_parts[layer, 1, :, at])
            q_high, q_low = split((joined[:WIDTH] + col(V_Q)) * QUERY_SCALE)
            k_high, k_low = split(joined[WIDTH:2 * WIDTH])
            v_high, v_low = split(joined[2 * WIDTH:] + col(V_V))
            for head in range(HEADS):
                rows = slice(head * HEAD, (head + 1) * HEAD)
                q_all[layer, head, 0:64, at] = q_high[rows]
                q_all[layer, head, 64:128, at] = q_high[rows]
                q_all[layer, head, 128:192, at] = q_low[rows]
                k_all[layer, head, 0:64, at] = k_high[rows]
                k_all[layer, head, 64:128, at] = k_low[rows]
                k_all[layer, head, 128:192, at] = k_high[rows]
                v_all[layer, head, 0:64, at] = v_high[rows]
                v_all[layer, head, 64:128, at] = v_low[rows]
                v_all[layer, head, 128:192, at] = v_high[rows]

        def attend(head, inside):
            rows = pl.ds(pl.multiple_of(head * HEAD, HEAD), HEAD)
            for block in range(BLOCKS):
                at = slice(block * BLOCK, (block + 1) * BLOCK)
                scores = dot(k_all[layer, head], q_all[layer, head, :, at], left_t=True)
                top = jnp.max(scores, axis=0, keepdims=True)
                weights = jnp.exp2(scores - top)
                total = jnp.sum(weights, axis=0, keepdims=True)
                high, low = split(weights)
                both = dot(v_all[layer, head, 0:128, :], high)
                context = both[:64] + both[64:] + dot(v_all[layer, head, 0:64, :], low)
                context = context / total
                ctx_parts[layer, 0, rows, at], ctx_parts[layer, 1, rows, at] = split(context)
                log_total = top + jnp.log(total) * LOG2E
                q_all[layer, head, 192:208, at] = feature_tile(marks[:, at], -log_total, 4)
            return inside

        lax.fori_loop(0, HEADS, attend, 0)

        for block in range(BLOCKS):
            at = slice(block * BLOCK, (block + 1) * BLOCK)
            upper = x_now[:, at] + dot3(fo[0], fo[1], ctx_parts[layer, 0, :, at], ctx_parts[layer, 1, :, at]) + col(V_OUT)
            normed, inverse = norm_rows(upper)
            n_one[layer, :, at] = normed
            r_one[layer, :, at] = inverse
            hidden = normed * col(V_GAIN1) + col(V_SHIFT1)
            hid_high, hid_low = split(hidden)
            hid_parts[layer, 0, :, at] = hid_high
            hid_parts[layer, 1, :, at] = hid_low
            in_bias = jnp.concatenate([col(V_IN), col(V_IN + 1)], axis=0)
            pre = dot3(fi[0], fi[1], hid_high, hid_low) + in_bias
            share = 0.5 + 0.5 * lax.erf(pre * math.sqrt(0.5))
            slope[layer, :, at] = share + pre * (jnp.exp(pre * pre * -0.5) * (1.0 / math.sqrt(2.0 * math.pi)))
            inner_high, inner_low = split(pre * share)
            inner_parts[layer, 0, :, at] = inner_high
            inner_parts[layer, 1, :, at] = inner_low
            lower = hidden + dot3(fb[0], fb[1], inner_high, inner_low) + col(V_BACK)
            normed, inverse = norm_rows(lower)
            n_two[layer, :, at] = normed
            r_two[layer, :, at] = inverse
            x_now[:, at] = live[0:1, at] * (normed * col(V_GAIN2) + col(V_SHIFT2))
        return carry

    lax.fori_loop(0, 2, forward, 0)

    x_in[0] = x_now[:, :HALF].T
    x_in[1] = x_now[:, HALF:].T
    y_send = remote(x_in.at[1], final_ref.at[half], 7, partner)
    y_own = pltpu.make_async_copy(x_in.at[0], final_ref.at[half], local_sem.at[7])
    y_send.start()
    y_own.start()

    c_own.wait()
    c_send.wait()
    first_d = jnp.concatenate([c_in[0].T, c_in[1].T], axis=1)
    d_now[...] = first_d

    def backward(step, carry):
        layer = 1 - step
        cols[...] = jnp.concatenate([vecs[layer].T, jnp.zeros((WIDTH, 128 - SMALL_ROWS), F32)], axis=1)

        def col(index):
            return cols[:, index:index + 1]

        nq[0], nq[1] = split(w_qkv[layer])
        no[0], no[1] = split(w_out[layer])
        ni[0], ni[1] = split(w_in[layer])
        nb[0], nb[1] = split(w_back[layer])
        sums[...] = jnp.zeros_like(sums)

        def add_sum(index, values):
            sums[index] += lane_fold(values)

        for block in range(BLOCKS):
            at = slice(block * BLOCK, (block + 1) * BLOCK)
            grad = live[0:1, at] * d_now[:, at]
            normed = n_two[layer, :, at]
            add_sum(V_GAIN2, grad * normed)
            add_sum(V_SHIFT2, grad)
            d_lower = norm_back(grad * col(V_GAIN2), normed, r_two[layer, :, at])
            add_sum(V_BACK, d_lower)
            high, low = split(d_lower)
            dl_parts[0, :, at] = high
            dl_parts[1, :, at] = low
            d_pre = dot3(nb[0], nb[1], high, low) * slope[layer, :, at]
            add_sum(V_IN, d_pre[:WIDTH])
            add_sum(V_IN + 1, d_pre[WIDTH:])
            high, low = split(d_pre)
            dp_parts[0, :, at] = high
            dp_parts[1, :, at] = low
            d_hidden = d_lower + dot3(ni[0], ni[1], high, low)
            normed = n_one[layer, :, at]
            add_sum(V_GAIN1, d_hidden * normed)
            add_sum(V_SHIFT1, d_hidden)
            d_upper = norm_back(d_hidden * col(V_GAIN1), normed, r_one[layer, :, at])
            add_sum(V_OUT, d_upper)
            du_now[:, at] = d_upper
            high, low = split(d_upper)
            du_parts[0, :, at] = high
            du_parts[1, :, at] = low
            d_context = dot3(no[0], no[1], high, low)
            high, low = split(d_context)
            context = ctx_parts[layer, 0, :, at].astype(F32) + ctx_parts[layer, 1, :, at].astype(F32)
            product = d_context * context
            for head in range(HEADS):
                rows = slice(head * HEAD, (head + 1) * HEAD)
                do_all[head, 0:64, at] = high[rows]
                do_all[head, 64:128, at] = high[rows]
                do_all[head, 128:192, at] = low[rows]
                row_dot = jnp.sum(product[rows], axis=0, keepdims=True)
                do_all[head, 192:208, at] = feature_tile(jnp.zeros((16, BLOCK), F32), -row_dot, 0)

        packed[layer, AT_BACK:AT_BACK + INNER, :] = dot3(
            inner_parts[layer, 0], inner_parts[layer, 1], dl_parts[0], dl_parts[1], right_t=True)
        for part in range(2):
            rows = slice(part * WIDTH, (part + 1) * WIDTH)
            packed[layer, AT_IN + part * WIDTH:AT_IN + (part + 1) * WIDTH, :] = dot3(
                hid_parts[layer, 0], hid_parts[layer, 1], dp_parts[0, rows], dp_parts[1, rows], right_t=True)
        packed[layer, AT_OUT:AT_OUT + WIDTH, :] = dot3(
            ctx_parts[layer, 0], ctx_parts[layer, 1], du_parts[0], du_parts[1], right_t=True)

        def attend_back(head, inside):
            rows = pl.ds(pl.multiple_of(head * HEAD, HEAD), HEAD)
            for block in range(2):
                at = slice(block * HALF, (block + 1) * HALF)
                probs = jnp.exp2(dot(q_all[layer, head, :, at], k_all[layer, head], left_t=True))
                d_scores = probs * dot(do_all[head, :, at], v_all[layer, head], left_t=True)
                p_high, p_low = split(probs)
                s_high, s_low = split(d_scores)
                both = dot(k_all[layer, head, 0:128, :], s_high, right_t=True)
                d_query = (both[:64] + both[64:] + dot(k_all[layer, head, 0:64, :], s_low, right_t=True)) * KEY_SCALE
                sums[V_Q, rows, :] += lane_fold(d_query)
                dqkv[0, rows, at], dqkv[1, rows, at] = split(d_query)
                both = dot(q_all[layer, head, 64:192, at], s_high)
                d_key = both[:64] + both[64:] + dot(q_all[layer, head, 64:128, at], s_low)
                both = dot(do_all[head, 64:192, at], p_high)
                d_value = both[:64] + both[64:] + dot(do_all[head, 64:128, at], p_low)
                if block == 0:
                    dkv[0:64, :] = d_key
                    dkv[64:128, :] = d_value
                else:
                    d_key = (dkv[0:64, :] + d_key) * LN2
                    d_value = dkv[64:128, :] + d_value
                    k_rows = pl.ds(pl.multiple_of(WIDTH + head * HEAD, HEAD), HEAD)
                    v_rows = pl.ds(pl.multiple_of(2 * WIDTH + head * HEAD, HEAD), HEAD)
                    dqkv[0, k_rows, :], dqkv[1, k_rows, :] = split(d_key)
                    dqkv[0, v_rows, :], dqkv[1, v_rows, :] = split(d_value)
                    sums[V_V, rows, :] += lane_fold(d_value)
            return inside

        lax.fori_loop(0, HEADS, attend_back, 0)

        for block in range(BLOCKS):
            at = slice(block * BLOCK, (block + 1) * BLOCK)
            d_now[:, at] = du_now[:, at] + dot3(nq[0], nq[1], dqkv[0, :, at], dqkv[1, :, at])
        for part in range(3):
            rows = slice(part * WIDTH, (part + 1) * WIDTH)
            packed[layer, part * WIDTH:(part + 1) * WIDTH, :] = dot3(
                x_parts[layer, 0], x_parts[layer, 1], dqkv[0, rows], dqkv[1, rows], right_t=True)
        lane_small = lax.broadcasted_iota(jnp.int32, (WIDTH, 128), 1)
        small = jnp.zeros((WIDTH, 128), F32)
        for index in range(10):
            total = jnp.sum(sums[index], axis=1, keepdims=True)
            small = jnp.where(lane_small == index, total, small)
        packed[layer, AT_SMALL:AT_SMALL + SMALL_ROWS, :] = small.T[:SMALL_ROWS]
        return carry

    lax.fori_loop(0, 2, backward, 0)

    c_in[0] = d_now[:, :HALF].T
    c_in[1] = d_now[:, HALF:].T
    d_send = remote(c_in.at[1], grad_ref.at[half], 8, partner)
    d_own = pltpu.make_async_copy(c_in.at[0], grad_ref.at[half], local_sem.at[8])
    p_own = pltpu.make_async_copy(packed, packed_ref, local_sem.at[9])
    d_send.start()
    d_own.start()
    p_own.start()
    y_own.wait()
    y_send.wait()
    d_own.wait()
    p_own.wait()
    d_send.wait()


def relay(activations, cotangent, cell_lengths, w_qkv, w_out, w_in, w_back, vectors):
    anywhere = pl.BlockSpec(memory_space=pl.ANY)
    shape = jax.ShapeDtypeStruct
    parts = lambda rows: pltpu.VMEM((2, 2, rows, SLOT), BF16)
    return pl.pallas_call(
        relay_kernel,
        out_shape=(
            shape((2, HALF, WIDTH), F32),
            shape((2, HALF, WIDTH), F32),
            shape((2, PACKED_ROWS, WIDTH), F32),
        ),
        in_specs=[anywhere, anywhere, pl.BlockSpec(memory_space=pltpu.SMEM)] + [anywhere] * 5,
        out_specs=(anywhere, anywhere, anywhere),
        scratch_shapes=[
            pltpu.VMEM((2, HALF, WIDTH), F32),
            pltpu.VMEM((2, HALF, WIDTH), F32),
            pltpu.VMEM((2, WIDTH, 3 * WIDTH), F32),
            pltpu.VMEM((2, WIDTH, WIDTH), F32),
            pltpu.VMEM((2, WIDTH, INNER), F32),
            pltpu.VMEM((2, INNER, WIDTH), F32),
            pltpu.VMEM((2, SMALL_ROWS, WIDTH), F32),
            pltpu.VMEM((2, 3 * WIDTH, WIDTH), BF16),
            pltpu.VMEM((2, WIDTH, WIDTH), BF16),
            pltpu.VMEM((2, INNER, WIDTH), BF16),
            pltpu.VMEM((2, WIDTH, INNER), BF16),
            pltpu.VMEM((2, WIDTH, 3 * WIDTH), BF16),
            pltpu.VMEM((2, WIDTH, WIDTH), BF16),
            pltpu.VMEM((2, WIDTH, INNER), BF16),
            pltpu.VMEM((2, INNER, WIDTH), BF16),
            pltpu.VMEM((WIDTH, 128), F32),
            pltpu.VMEM((16, SLOT), F32),
            pltpu.VMEM((8, SLOT), F32),
            pltpu.VMEM((WIDTH, SLOT), F32),
            parts(WIDTH),
            pltpu.VMEM((2, HEADS, 256, SLOT), BF16),
            pltpu.VMEM((2, HEADS, 256, SLOT), BF16),
            pltpu.VMEM((2, HEADS, 256, SLOT), BF16),
            parts(WIDTH),
            pltpu.VMEM((2, WIDTH, SLOT), F32),
            pltpu.VMEM((2, 1, SLOT), F32),
            parts(WIDTH),
            pltpu.VMEM((2, INNER, SLOT), F32),
            parts(INNER),
            pltpu.VMEM((2, WIDTH, SLOT), F32),
            pltpu.VMEM((2, 1, SLOT), F32),
            pltpu.VMEM((WIDTH, SLOT), F32),
            pltpu.VMEM((2, WIDTH, SLOT), BF16),
            pltpu.VMEM((2, INNER, SLOT), BF16),
            pltpu.VMEM((WIDTH, SLOT), F32),
            pltpu.VMEM((2, WIDTH, SLOT), BF16),
            pltpu.VMEM((HEADS, 256, SLOT), BF16),
            pltpu.VMEM((2 * HEAD, SLOT), F32),
            pltpu.VMEM((2, 3 * WIDTH, SLOT), BF16),
            pltpu.VMEM((10, WIDTH, 128), F32),
            pltpu.VMEM((2, PACKED_ROWS, WIDTH), F32),
            pltpu.SemaphoreType.DMA((10,)),
            pltpu.SemaphoreType.DMA((9,)),
            pltpu.SemaphoreType.DMA((9,)),
        ],
        compiler_params=pltpu.CompilerParams(
            collective_id=0, has_side_effects=True, vmem_limit_bytes=63 * 2 ** 20),
        name="relay",
    )(activations, cotangent, cell_lengths, w_qkv, w_out, w_in, w_back, vectors)


def sum_kernel(packed_ref, total_ref, small_ref, own, other, half_out, small_in, *scratch):
    (slots_x, slots_y, slots_z, sum_x, sum_y, small_slots, all_x, all_y, all_z, local_sem, send_sem, recv_sem) = scratch
    core = lax.axis_index("pipe")
    dp = lax.axis_index("dp")
    seq = lax.axis_index("seq")
    x_high, z, y = dp // 16, (dp // 4) % 4, dp % 4
    x = x_high * 2 + seq

    def at_x(index):
        return {"dp": (index // 2) * 16 + dp % 16, "seq": index % 2}

    def at_y(index):
        return {"dp": dp - y + index}

    def at_z(index):
        return {"dp": x_high * 16 + index * 4 + y}

    sibling = {"pipe": 1 - core}
    axes = ((at_x, x), (at_y, y), (at_z, z))

    barrier = pltpu.get_barrier_semaphore()
    pl.semaphore_signal(barrier, inc=1, device_id=sibling, device_id_type=MESH)
    for where, index in axes:
        for step in range(1, 4):
            pl.semaphore_signal(barrier, inc=1, device_id=where((index + step) % 4), device_id_type=MESH)
    pl.semaphore_wait(barrier, 10)

    used = [0]

    def remote(src, dst, device):
        index = used[0]
        used[0] += 1
        return pltpu.make_async_remote_copy(
            src_ref=src, dst_ref=dst, send_sem=send_sem.at[index], recv_sem=recv_sem.at[index],
            device_id=device, device_id_type=MESH,
        )

    rows = MATRIX_ROWS // 2
    sends = []
    for layer in range(2):
        sends.append(remote(
            packed_ref.at[layer, pl.ds(pl.multiple_of((1 - core) * rows, rows), rows)], other.at[layer], sibling))
    small_src = packed_ref.at[:, pl.ds(AT_SMALL, SMALL_ROWS)]
    sends.append(remote(small_src, small_slots.at[0, core], sibling))
    for copy in sends:
        copy.start()
    owns = [
        pltpu.make_async_copy(packed_ref.at[:, pl.ds(pl.multiple_of(core * rows, rows), rows)], own, local_sem.at[0]),
        pltpu.make_async_copy(small_src, small_slots.at[0, core], local_sem.at[1]),
    ]
    for copy in owns:
        copy.start()
    for copy in owns:
        copy.wait()
    for copy in sends:
        copy.wait()
    own[...] = own[...] + other[...]
    small_in[...] = small_slots[0, 0] + small_slots[0, 1]

    def chunk(ref, index, size):
        return ref.at[:, pl.ds(pl.multiple_of(index * size, size), size)]

    stages = (
        (axes[0], own, slots_x, sum_x, rows // 4),
        (axes[1], sum_x, slots_y, sum_y, rows // 16),
        (axes[2], sum_y, slots_z, None, rows // 64),
    )
    for number, ((where, index), source, slots, target, size) in enumerate(stages):
        sends = []
        small_slots[number + 1, index] = small_in[...]
        for step in range(1, 4):
            peer = (index + step) % 4
            sends.append(remote(chunk(source, peer, size), slots.at[index], where(peer)))
            sends.append(remote(small_in, small_slots.at[number + 1, index], where(peer)))
        for copy in sends:
            copy.start()
        slots[index] = source[:, pl.ds(pl.multiple_of(index * size, size), size)]
        for copy in sends:
            copy.wait()
        summed = (slots[0] + slots[1]) + (slots[2] + slots[3])
        small = (small_slots[number + 1, 0] + small_slots[number + 1, 1]) + (
            small_slots[number + 1, 2] + small_slots[number + 1, 3])
        small_in[...] = small
        if target is not None:
            target[...] = summed
        else:
            all_z[:, pl.ds(pl.multiple_of(index * size, size), size)] = summed

    whole = (all_x, all_y, all_z, None)
    for number, ((where, index), _, _, _, size) in reversed(list(enumerate(stages))):
        dest, source = whole[number], whole[number + 1]
        if source is not None:
            dest[:, pl.ds(pl.multiple_of(index * size, size), size)] = source[...]
        sends = []
        for step in range(1, 4):
            peer = (index + step) % 4
            sends.append(remote(chunk(dest, index, size), chunk(dest, index, size), where(peer)))
        for copy in sends:
            copy.start()
        for copy in sends:
            copy.wait()

    send = remote(all_x.at[1 - core], half_out, sibling)
    send.start()
    mine = pl.ds(pl.multiple_of(core * rows, rows), rows)
    theirs = pl.ds(pl.multiple_of((1 - core) * rows, rows), rows)
    keep = pltpu.make_async_copy(all_x.at[core], total_ref.at[mine], local_sem.at[2])
    keep.start()
    small_ref[...] = small_in[core]
    send.wait()
    last = pltpu.make_async_copy(half_out, total_ref.at[theirs], local_sem.at[3])
    last.start()
    keep.wait()
    last.wait()


def sum_grads(packed):
    rows = MATRIX_ROWS // 2
    count = 3 + 18 + 9 + 1
    return pl.pallas_call(
        sum_kernel,
        out_shape=(
            jax.ShapeDtypeStruct((MATRIX_ROWS, WIDTH), F32),
            jax.ShapeDtypeStruct((SMALL_ROWS, WIDTH), F32),
        ),
        in_specs=[pl.BlockSpec(memory_space=pl.ANY)],
        out_specs=(pl.BlockSpec(memory_space=pl.ANY), pl.BlockSpec(memory_space=pltpu.VMEM)),
        scratch_shapes=[
            pltpu.VMEM((2, rows, WIDTH), F32),
            pltpu.VMEM((2, rows, WIDTH), F32),
            pltpu.VMEM((rows, WIDTH), F32),
            pltpu.VMEM((2, SMALL_ROWS, WIDTH), F32),
            pltpu.VMEM((4, 2, rows // 4, WIDTH), F32),
            pltpu.VMEM((4, 2, rows // 16, WIDTH), F32),
            pltpu.VMEM((4, 2, rows // 64, WIDTH), F32),
            pltpu.VMEM((2, rows // 4, WIDTH), F32),
            pltpu.VMEM((2, rows // 16, WIDTH), F32),
            pltpu.VMEM((4, 4, 2, SMALL_ROWS, WIDTH), F32),
            pltpu.VMEM((2, rows, WIDTH), F32),
            pltpu.VMEM((2, rows // 4, WIDTH), F32),
            pltpu.VMEM((2, rows // 16, WIDTH), F32),
            pltpu.SemaphoreType.DMA((4,)),
            pltpu.SemaphoreType.DMA((count,)),
            pltpu.SemaphoreType.DMA((count,)),
        ],
        compiler_params=pltpu.CompilerParams(
            collective_id=1, has_side_effects=True, vmem_limit_bytes=48 * 2 ** 20),
        name="sum_grads",
    )(packed)


def body(
    activations, cotangent, cell_lengths, w_qkv, b_qv, w_out, b_out, gain_one, shift_one,
    w_in, b_in, w_back, b_back, gain_two, shift_two,
):
    vectors = jnp.concatenate(
        [b_qv, b_out, gain_one, shift_one, b_in, b_back, gain_two, shift_two, jnp.zeros((1, 6 * WIDTH), F32)], axis=1
    ).reshape(1, SMALL_ROWS, WIDTH)
    final_output, input_grad, packed = relay(
        activations, cotangent, cell_lengths, w_qkv, w_out, w_in, w_back, vectors)
    total, small = sum_grads(packed)

    def vector(first, count):
        return small[first:first + count].reshape(1, count * WIDTH)

    def matrix(first, count):
        blocks = [total[first + i * WIDTH:first + (i + 1) * WIDTH] for i in range(count)]
        return jnp.concatenate(blocks, axis=1)[None]

    return (
        final_output,
        input_grad,
        matrix(AT_QKV, 3),
        vector(V_Q, 2),
        matrix(AT_OUT, 1),
        vector(V_OUT, 1),
        vector(V_GAIN1, 1),
        vector(V_SHIFT1, 1),
        matrix(AT_IN, 2),
        vector(V_IN, 2),
        total[AT_BACK:AT_BACK + INNER][None],
        vector(V_BACK, 1),
        vector(V_GAIN2, 1),
        vector(V_SHIFT2, 1),
    )


def solution(mesh):
    rows = P(None, ("dp", "seq"), None)
    matrix = P("pipe", None, None)
    vector = P("pipe", None)
    in_specs = (
        rows, rows, P(None, "dp", None), matrix, vector, matrix, vector, vector, vector,
        matrix, vector, matrix, vector, vector, vector,
    )
    out_rows = P("pipe", ("dp", "seq"), None)
    out_specs = (
        out_rows, out_rows, matrix, vector, matrix, vector, vector, vector,
        matrix, vector, matrix, vector, vector, vector,
    )
    return jax.shard_map(body, mesh=mesh, in_specs=in_specs, out_specs=out_specs, check_vma=False)
```

```python
import math

import jax
import jax.numpy as jnp
from jax import lax
from jax.experimental import pallas as pl
from jax.experimental.pallas import tpu as pltpu
from jax.sharding import PartitionSpec as P

MESH = pl.DeviceIdType.MESH
F32 = jnp.float32
BF16 = jnp.bfloat16

HEADS = 4
HEAD = 64
WIDTH = 256
INNER = 512
HALF = 512
SLOT = 1024
BLOCK = 256
BLOCKS = SLOT // BLOCK
DEEP = 3 * HEAD + 16
EPSILON = 1e-06
APART = -1e30
LOG2E = math.log2(math.e)
LN2 = math.log(2.0)
QUERY_SCALE = LOG2E / math.sqrt(HEAD)
KEY_SCALE = 1.0 / math.sqrt(HEAD)

UNITS, UNIT_ROWS, UNIT_HALF = 4, 1024, 512
CHUNKS = (128, 32, 8)
SMALL_ROWS = 16
VMEM_BYTES = 64 * 2 ** 20 - 2 ** 18
V_Q, V_V, V_OUT, V_GAIN1, V_SHIFT1, V_IN, V_BACK, V_GAIN2, V_SHIFT2 = 0, 1, 2, 3, 4, 5, 7, 8, 9


def dot(left, right, left_t=False, right_t=False):
    dims = (((0 if left_t else 1,), (1 if right_t else 0,)), ((), ()))
    return lax.dot_general(left, right, dims, preferred_element_type=F32)


def split(values):
    high = values.astype(BF16)
    return high, (values - high.astype(F32)).astype(BF16)


def dot3(left_high, left_low, right_high, right_low, right_t=False):
    return (
        dot(left_high, right_high, right_t=right_t)
        + dot(left_high, right_low, right_t=right_t)
        + dot(left_low, right_high, right_t=right_t)
    )


def col_mean(values):
    return jnp.mean(values, axis=0, keepdims=True)


def norm_rows(values):
    center = values - col_mean(values)
    spread = col_mean(center * center)
    inverse = lax.rsqrt(spread + EPSILON)
    return center * inverse, inverse


def norm_back(grad, normed, inverse):
    return (grad - col_mean(grad) - normed * col_mean(grad * normed)) * inverse


def feature_tile(base, values, first):
    high = values.astype(BF16).astype(F32)
    rest = values - high
    middle = rest.astype(BF16).astype(F32)
    low = rest - middle
    row = lax.broadcasted_iota(jnp.int32, base.shape, 0)
    tile = jnp.where(row == first, high, base)
    tile = jnp.where(row == first + 1, middle, tile)
    return jnp.where(row == first + 2, low, tile).astype(BF16)


def lane_fold(values):
    folded = values[:, :128]
    for first in range(128, values.shape[1], 128):
        folded = folded + values[:, first:first + 128]
    return folded


class Torus:
    def __init__(self):
        self.core = lax.axis_index("pipe")
        self.half = lax.axis_index("seq")
        dp = lax.axis_index("dp")
        x_high, z, y = dp // 16, (dp // 4) % 4, dp % 4
        self.sibling = {"pipe": 1 - self.core}
        self.partner = {"seq": 1 - self.half}
        self.axes = {
            "x": (x_high * 2 + self.half, lambda i: {"dp": (i // 2) * 16 + dp % 16, "seq": i % 2}),
            "y": (y, lambda i: {"dp": dp - y + i}),
            "z": (z, lambda i: {"dp": x_high * 16 + i * 4 + y}),
        }

        self.near = {
            axis: [((index + step) % 4, where((index + step) % 4)) for step in (1, 2, 3)]
            for axis, (index, where) in self.axes.items()
        }

    def peer(self, axis, step):
        return self.near[axis][step - 1]

    def peers(self, axis):
        return self.near[axis]


class Sender:
    def __init__(self, send_sem, recv_sem):
        self.send_sem, self.recv_sem, self.used = send_sem, recv_sem, 0

    def take(self):
        self.used += 1
        return self.used - 1

    def __call__(self, src, dst, device):
        return self.build(self.take(), src, dst, device)

    def build(self, index, src, dst, device):
        return pltpu.make_async_remote_copy(
            src_ref=src, dst_ref=dst, send_sem=self.send_sem.at[index], recv_sem=self.recv_sem.at[index],
            device_id=device, device_id_type=MESH,
        )


def span(first, size):
    return pl.ds(pl.multiple_of(first, size), size)


class UnitSum:
    def __init__(self, torus, remote, bufs, total_ref, local_sems, layer, first, count, order):
        self.torus, self.remote, self.bufs = torus, remote, bufs
        self.total_ref, self.local_sems = total_ref, local_sems
        self.layer, self.units, self.order = layer, slice(first, first + count), order
        self.pending = []
        self.next = 0

    def send(self, makers):
        self.pending = [(self.remote.take(), maker) for maker in makers]
        for index, maker in self.pending:
            self.remote.build(index, *maker()).start()

    def settle(self):
        for index, maker in self.pending:
            self.remote.build(index, *maker()).wait()
        self.pending = []

    def offset(self, depth):
        first = 0
        for level in range(depth):
            first = first + self.torus.axes[self.order[level]][0] * CHUNKS[level]
        return first

    def step(self):
        getattr(self, "step_%d" % self.next)()
        self.next += 1

    def step_0(self):
        self.send([lambda: (
            self.bufs["grads"].at[self.layer, self.units, span((1 - self.torus.core) * UNIT_HALF, UNIT_HALF)],
            self.bufs["cores"].at[self.layer, self.units], self.torus.sibling)])

    def base(self, level):
        return self.torus.core * UNIT_HALF if level == 0 else 0

    def scatter(self, level, source):
        size = CHUNKS[level]
        slots = self.bufs["slots"][level]

        def maker(step):
            def make():
                peer, device = self.torus.peer(self.order[level], step)
                return (source.at[self.layer, self.units, span(self.base(level) + peer * size, size)],
                        slots.at[step - 1, self.layer, self.units], device)
            return make

        self.send([maker(step) for step in (1, 2, 3)])

    def gathered(self, level, source):
        size = CHUNKS[level]
        slots = self.bufs["slots"][level]
        first = self.base(level) + self.torus.axes[self.order[level]][0] * size
        own = source[self.layer, self.units, span(first, size), :]
        return (own + slots[0, self.layer, self.units]) + (
            slots[1, self.layer, self.units] + slots[2, self.layer, self.units])

    def step_1(self):
        self.settle()
        grads, cores = self.bufs["grads"], self.bufs["cores"]
        home = span(self.torus.core * UNIT_HALF, UNIT_HALF)
        grads[self.layer, self.units, home, :] += cores[self.layer, self.units]
        self.scatter(0, grads)

    def step_2(self):
        self.settle()
        partial = self.bufs["partial"][0]
        partial[self.layer, self.units] = self.gathered(0, self.bufs["grads"])
        self.scatter(1, partial)

    def step_3(self):
        self.settle()
        partial = self.bufs["partial"][1]
        partial[self.layer, self.units] = self.gathered(1, self.bufs["partial"][0])
        self.scatter(2, partial)

    def spread(self, level):
        size = CHUNKS[level]

        def maker(step):
            def make():
                chunk = self.bufs["done"].at[self.layer, self.units, span(self.offset(level + 1), size)]
                return chunk, chunk, self.torus.peer(self.order[level], step)[1]
            return make

        self.send([maker(step) for step in (1, 2, 3)])

    def step_4(self):
        self.settle()
        rows = span(self.offset(3), CHUNKS[2])
        self.bufs["done"][self.layer, self.units, rows, :] = self.gathered(2, self.bufs["partial"][1])
        self.spread(2)

    def step_5(self):
        self.settle()
        self.spread(1)

    def step_6(self):
        self.settle()
        self.spread(0)

    def away_copy(self):
        return self.remote.build(
            self.away, self.bufs["done"].at[self.layer, self.units], self.bufs["far"].at[self.units], self.torus.sibling)

    def near_copy(self):
        return pltpu.make_async_copy(
            self.bufs["done"].at[self.layer, self.units],
            self.total_ref.at[self.units, span(self.torus.core * UNIT_HALF, UNIT_HALF)], self.local_sems.at[0])

    def far_copy(self):
        return pltpu.make_async_copy(
            self.bufs["far"].at[self.units],
            self.total_ref.at[self.units, span((1 - self.torus.core) * UNIT_HALF, UNIT_HALF)], self.local_sems.at[1])

    def step_7(self):
        self.settle()
        self.away = self.remote.take()

        @pl.when(self.torus.core == self.layer)
        def _():
            self.near_copy().start()

        @pl.when(self.torus.core != self.layer)
        def _():
            self.away_copy().start()

    def step_8(self):
        @pl.when(self.torus.core == self.layer)
        def _():
            self.away_copy().wait_recv()
            self.far_copy().start()
            self.near_copy().wait()
            self.far_copy().wait()

        @pl.when(self.torus.core != self.layer)
        def _():
            self.away_copy().wait_send()


def relay_kernel(
    act_ref, cot_ref, len_ref, w_qkv_ref, w_out_ref, w_in_ref, w_back_ref,
    b_qv_ref, b_out_ref, gain_one_ref, shift_one_ref, b_in_ref, b_back_ref, gain_two_ref, shift_two_ref,
    final_ref, grad_ref, total_ref, small_ref,
    x_in, lengths, w_qkv, w_out, w_in, w_back, vecs,
    parts_q, half_o, half_a, half_b, cols,
    marks, live, x_now, x_parts, q_all, k_all, v_all, ctx_parts,
    n_one, r_one, slope, inner_parts, n_two, r_two,
    dl_parts, du_parts, do_all, dkv, dqkv, sums,
    grads, cores, slots_0, slots_1, slots_2, partial_0, partial_1, done, far, small, small_far, small_slots,
    local_sem, out_sem, send_sem, recv_sem,
):
    torus = Torus()
    core, half = torus.core, torus.half
    remote = Sender(send_sem, recv_sem)

    barrier = pltpu.get_barrier_semaphore()
    pl.semaphore_signal(barrier, inc=1, device_id=torus.sibling, device_id_type=MESH)
    for axis in "xyz":
        for _, device in torus.peers(axis):
            pl.semaphore_signal(barrier, inc=1, device_id=device, device_id_type=MESH)

    mine = 2 * core + half
    theirs = 2 * core + 1 - half
    weight_pairs = ((w_qkv_ref, w_qkv), (w_out_ref, w_out), (w_in_ref, w_in), (w_back_ref, w_back))
    len_own = pltpu.make_async_copy(len_ref, lengths, local_sem.at[0])
    x_own = pltpu.make_async_copy(act_ref.at[mine], x_in.at[0], local_sem.at[1])
    c_owns = [
        pltpu.make_async_copy(cot_ref.at[mine, :, pl.ds(part * 128, 128)], far.at[part], local_sem.at[9 + part])
        for part in range(2)
    ]
    w_owns = [
        pltpu.make_async_copy(src.at[0], dst.at[core], local_sem.at[3 + i])
        for i, (src, dst) in enumerate(weight_pairs)
    ]
    len_own.start()
    x_own.start()
    for copy in w_owns:
        copy.start()
    for copy in c_owns:
        copy.start()
    vecs[core] = jnp.concatenate([
        b_qv_ref[:, :WIDTH], b_qv_ref[:, WIDTH:], b_out_ref[...], gain_one_ref[...], shift_one_ref[...],
        b_in_ref[:, :WIDTH], b_in_ref[:, WIDTH:], b_back_ref[...], gain_two_ref[...], shift_two_ref[...],
        jnp.zeros((6, WIDTH), F32)], axis=0)

    pl.semaphore_wait(barrier, 10)

    x_send = remote(act_ref.at[theirs], x_in.at[1], torus.partner)
    c_sends = [
        remote(cot_ref.at[theirs, :, pl.ds(part * 128, 128)], far.at[2 + part], torus.partner) for part in range(2)
    ]
    w_sends = [remote(src.at[0], dst.at[core], torus.sibling) for src, dst in weight_pairs]
    w_sends.append(remote(vecs.at[core], vecs.at[core], torus.sibling))
    x_send.start()
    for copy in w_sends:
        copy.start()

    len_own.wait()
    lane = lax.broadcasted_iota(jnp.int32, (16, SLOT), 1)
    row = lax.broadcasted_iota(jnp.int32, (16, SLOT), 0)
    place = jnp.where(lane < HALF, half * HALF + lane, (1 - half) * HALF + lane - HALF)
    end_0 = lengths[0, 0, mine]
    end_1 = end_0 + lengths[1, 0, mine]
    end_2 = end_1 + lengths[2, 0, mine]
    one = jnp.ones_like(place)
    none = jnp.zeros_like(place)
    cell = (
        jnp.where(place >= end_0, one, none)
        + jnp.where(place >= end_1, one, none)
        + jnp.where(place >= end_2, one, none)
    )
    same = jnp.where(cell == row, 1.0, 0.0)
    marks[...] = same
    live[...] = jnp.where(cell < 3, 1.0, 0.0)[:8]
    key_marks = jnp.where(row < 4, (1.0 - same) * APART, jnp.where(row < 7, 1.0, 0.0)).astype(BF16)
    value_marks = jnp.where(row < 3, 1.0, 0.0).astype(BF16)
    query_marks = same.astype(BF16)
    for layer in range(2):
        for head in range(HEADS):
            q_all[layer, head, 192:208, :] = query_marks
            k_all[layer, head, 192:208, :] = key_marks
            v_all[layer, head, 192:208, :] = value_marks

    def col(index):
        return cols[:, index:index + 1]

    def load_cols(layer):
        cols[...] = jnp.concatenate([vecs[layer].T, jnp.zeros((WIDTH, 128 - SMALL_ROWS), F32)], axis=1)

    def project(layer, blocks):
        for block in blocks:
            at = slice(block * BLOCK, (block + 1) * BLOCK)
            x_high, x_low = split(x_now[:, at])
            x_parts[layer, 0, :, at] = x_high
            x_parts[layer, 1, :, at] = x_low
            queries, key_rows, value_rows = (
                dot3(parts_q[0, part], parts_q[1, part], x_high, x_low) for part in range(3))
            q_high, q_low = split((queries + col(V_Q)) * QUERY_SCALE)
            k_high, k_low = split(key_rows)
            v_high, v_low = split(value_rows + col(V_V))
            for head in range(HEADS):
                rows = slice(head * HEAD, (head + 1) * HEAD)
                q_all[layer, head, 0:64, at] = q_high[rows]
                q_all[layer, head, 64:128, at] = q_high[rows]
                q_all[layer, head, 128:192, at] = q_low[rows]
                k_all[layer, head, 0:64, at] = k_high[rows]
                k_all[layer, head, 64:128, at] = k_low[rows]
                k_all[layer, head, 128:192, at] = k_high[rows]
                v_all[layer, head, 0:64, at] = v_high[rows]
                v_all[layer, head, 64:128, at] = v_low[rows]
                v_all[layer, head, 128:192, at] = v_high[rows]

    def forward_weights(layer):
        load_cols(layer)
        for part in range(3):
            parts_q[0, part], parts_q[1, part] = split(w_qkv[layer, :, part * WIDTH:(part + 1) * WIDTH].T)
        half_o[0], half_o[1] = split(w_out[layer].T)
        half_a[0], half_a[1] = split(w_in[layer].T)
        half_b[0], half_b[1] = split(w_back[layer].T)

    def backward_weights(layer):
        load_cols(layer)
        for part in range(3):
            parts_q[0, part], parts_q[1, part] = split(w_qkv[layer, :, part * WIDTH:(part + 1) * WIDTH])
        half_o[0], half_o[1] = split(w_out[layer])
        half_a[0], half_a[1] = split(w_back[layer])
        half_b[0], half_b[1] = split(w_in[layer])

    def attend(layer):
        def one_head(head, inside):
            rows = span(head * HEAD, HEAD)
            for block in range(BLOCKS):
                at = slice(block * BLOCK, (block + 1) * BLOCK)
                scores = dot(k_all[layer, head], q_all[layer, head, :, at], left_t=True)
                top = jnp.max(scores, axis=0, keepdims=True)
                weights = jnp.exp2(scores - top)
                total = jnp.sum(weights, axis=0, keepdims=True)
                high, low = split(weights)
                both = dot(v_all[layer, head, 0:128, :], high)
                context = both[:64] + both[64:] + dot(v_all[layer, head, 0:64, :], low)
                context = context / total
                ctx_parts[layer, 0, rows, at], ctx_parts[layer, 1, rows, at] = split(context)
                log_total = top + jnp.log(total) * LOG2E
                q_all[layer, head, 192:208, at] = feature_tile(marks[:, at], -log_total, 4)
            return inside

        lax.fori_loop(0, HEADS, one_head, 0)

    def feed_forward(layer):
        for block in range(BLOCKS):
            at = slice(block * BLOCK, (block + 1) * BLOCK)
            upper = x_now[:, at] + dot3(
                half_o[0], half_o[1], ctx_parts[layer, 0, :, at], ctx_parts[layer, 1, :, at]) + col(V_OUT)
            normed, inverse = norm_rows(upper)
            n_one[layer, :, at] = normed
            r_one[layer, :, at] = inverse
            hidden = normed * col(V_GAIN1) + col(V_SHIFT1)
            hid_high, hid_low = split(hidden)
            in_bias = jnp.concatenate([col(V_IN), col(V_IN + 1)], axis=0)
            pre = dot3(half_a[0], half_a[1], hid_high, hid_low) + in_bias
            share = 0.5 + 0.5 * lax.erf(pre * math.sqrt(0.5))
            slope[layer, :, at] = share + pre * (jnp.exp(pre * pre * -0.5) * (1.0 / math.sqrt(2.0 * math.pi)))
            inner_high, inner_low = split(pre * share)
            inner_parts[layer, 0, :, at] = inner_high
            inner_parts[layer, 1, :, at] = inner_low
            lower = hidden + dot3(half_b[0], half_b[1], inner_high, inner_low) + col(V_BACK)
            normed, inverse = norm_rows(lower)
            n_two[layer, :, at] = normed
            r_two[layer, :, at] = inverse
            x_now[:, at] = live[0:1, at] * (normed * col(V_GAIN2) + col(V_SHIFT2))

    for copy in w_owns:
        copy.wait()
    for copy in w_sends:
        copy.wait()
    forward_weights(0)
    x_own.wait()
    x_now[:, :HALF] = x_in[0].T
    project(0, (0, 1))
    x_send.wait()
    for copy in c_sends:
        copy.start()
    x_now[:, HALF:] = x_in[1].T
    project(0, (2, 3))
    attend(0)
    feed_forward(0)
    forward_weights(1)
    project(1, (0, 1, 2, 3))
    attend(1)
    feed_forward(1)

    x_in[0] = x_now[:, :HALF].T
    x_in[1] = x_now[:, HALF:].T
    y_send = remote(x_in.at[1], final_ref.at[half], torus.partner)
    y_own = pltpu.make_async_copy(x_in.at[0], final_ref.at[half], local_sem.at[7])
    for copy in c_owns + c_sends:
        copy.wait()
    y_send.start()
    y_own.start()
    for part in range(2):
        x_now[part * 128:(part + 1) * 128, :HALF] = far[part].T
        x_now[part * 128:(part + 1) * 128, HALF:] = far[2 + part].T

    bufs = {
        "grads": grads, "cores": cores, "slots": (slots_0, slots_1, slots_2),
        "partial": (partial_0, partial_1), "done": done, "far": far,
    }

    def unit_sum(number, layer, first, count, order):
        return UnitSum(torus, remote, bufs, total_ref, out_sem.at[number], layer, first, count, order)

    dp_parts = dqkv.at[:, 0:INNER]
    hid_parts = dqkv.at[:, INNER:INNER + WIDTH]

    def add_sum(index, values):
        sums[index] += lane_fold(values)

    def finish_back(layer, after_block):
        sums[...] = jnp.zeros_like(sums)
        for block in range(BLOCKS):
            at = slice(block * BLOCK, (block + 1) * BLOCK)
            grad = live[0:1, at] * x_now[:, at]
            normed = n_two[layer, :, at]
            add_sum(V_GAIN2, grad * normed)
            add_sum(V_SHIFT2, grad)
            d_lower = norm_back(grad * col(V_GAIN2), normed, r_two[layer, :, at])
            add_sum(V_BACK, d_lower)
            high, low = split(d_lower)
            dl_parts[0, :, at] = high
            dl_parts[1, :, at] = low
            d_pre = dot3(half_a[0], half_a[1], high, low) * slope[layer, :, at]
            add_sum(V_IN, d_pre[:WIDTH])
            add_sum(V_IN + 1, d_pre[WIDTH:])
            high, low = split(d_pre)
            dp_parts[0, :, at] = high
            dp_parts[1, :, at] = low
            d_hidden = d_lower + dot3(half_b[0], half_b[1], high, low)
            normed = n_one[layer, :, at]
            hid_parts[0, :, at], hid_parts[1, :, at] = split(normed * col(V_GAIN1) + col(V_SHIFT1))
            add_sum(V_GAIN1, d_hidden * normed)
            add_sum(V_SHIFT1, d_hidden)
            d_upper = norm_back(d_hidden * col(V_GAIN1), normed, r_one[layer, :, at])
            add_sum(V_OUT, d_upper)
            x_now[:, at] = d_upper
            high, low = split(d_upper)
            du_parts[0, :, at] = high
            du_parts[1, :, at] = low
            d_context = dot3(half_o[0], half_o[1], high, low)
            high, low = split(d_context)
            context = ctx_parts[layer, 0, :, at].astype(F32) + ctx_parts[layer, 1, :, at].astype(F32)
            product = d_context * context
            for head in range(HEADS):
                rows = slice(head * HEAD, (head + 1) * HEAD)
                do_all[head, 0:64, at] = high[rows]
                do_all[head, 64:128, at] = high[rows]
                do_all[head, 128:192, at] = low[rows]
                row_dot = jnp.sum(product[rows], axis=0, keepdims=True)
                do_all[head, 192:208, at] = feature_tile(jnp.zeros((16, BLOCK), F32), -row_dot, 0)
            after_block(block)

    def put(layer, unit, first, values):
        rows = values.shape[0]
        for part in range(values.shape[1] // 128):
            begin = first + part * rows
            grads[layer, unit, begin:begin + rows, :] = values[:, part * 128:(part + 1) * 128]

    def finish_grads(layer):
        put(layer, 0, 0, dot3(
            inner_parts[layer, 0], inner_parts[layer, 1], dl_parts[0], dl_parts[1], right_t=True))
        put(layer, 1, 0, dot3(hid_parts[0], hid_parts[1], dp_parts[0], dp_parts[1], right_t=True))
        grad_out = dot3(ctx_parts[layer, 0], ctx_parts[layer, 1], du_parts[0], du_parts[1], right_t=True)
        put(layer, 2, 0, grad_out[:, :128])
        put(layer, 3, 0, grad_out[:, 128:])

    def attend_back(layer, after_head):
        def one_head(head, inside):
            rows = span(head * HEAD, HEAD)
            for block in range(BLOCKS):
                at = slice(block * BLOCK, (block + 1) * BLOCK)
                probs = jnp.exp2(dot(q_all[layer, head, :, at], k_all[layer, head], left_t=True))
                d_scores = probs * dot(do_all[head, :, at], v_all[layer, head], left_t=True)
                p_high, p_low = split(probs)
                s_high, s_low = split(d_scores)
                both = dot(k_all[layer, head, 0:128, :], s_high, right_t=True)
                d_query = (both[:64] + both[64:] + dot(k_all[layer, head, 0:64, :], s_low, right_t=True)) * KEY_SCALE
                sums[V_Q, rows, :] += lane_fold(d_query)
                dqkv[0, rows, at], dqkv[1, rows, at] = split(d_query)
                both = dot(q_all[layer, head, 64:192, at], s_high)
                d_key = both[:64] + both[64:] + dot(q_all[layer, head, 64:128, at], s_low)
                both = dot(do_all[head, 64:192, at], p_high)
                d_value = both[:64] + both[64:] + dot(do_all[head, 64:128, at], p_low)
                if block > 0:
                    d_key = dkv[0:64, :] + d_key
                    d_value = dkv[64:128, :] + d_value
                if block < BLOCKS - 1:
                    dkv[0:64, :] = d_key
                    dkv[64:128, :] = d_value
            k_rows = span(WIDTH + head * HEAD, HEAD)
            v_rows = span(2 * WIDTH + head * HEAD, HEAD)
            dqkv[0, k_rows, :], dqkv[1, k_rows, :] = split(d_key * LN2)
            dqkv[0, v_rows, :], dqkv[1, v_rows, :] = split(d_value)
            sums[V_V, rows, :] += lane_fold(d_value)
            for number, todo in enumerate(after_head):

                @pl.when(head == number)
                def _():
                    todo()

            return inside

        lax.fori_loop(0, HEADS, one_head, 0)

    def project_back(layer):
        for block in range(BLOCKS):
            at = slice(block * BLOCK, (block + 1) * BLOCK)
            total = x_now[:, at]
            for part in range(3):
                rows = slice(part * WIDTH, (part + 1) * WIDTH)
                total = total + dot3(parts_q[0, part], parts_q[1, part], dqkv[0, rows, at], dqkv[1, rows, at])
            x_now[:, at] = total

    def project_grads(layer):
        for part in range(3):
            rows = slice(part * WIDTH, (part + 1) * WIDTH)
            block = dot3(x_parts[layer, 0], x_parts[layer, 1], dqkv[0, rows], dqkv[1, rows], right_t=True)
            put(layer, 2, 256 + 256 * part, block[:, :128])
            put(layer, 3, 256 + 256 * part, block[:, 128:])
        lane_small = lax.broadcasted_iota(jnp.int32, (WIDTH, 128), 1)
        packed = jnp.zeros((WIDTH, 128), F32)
        for index in range(10):
            packed = jnp.where(lane_small == index, jnp.sum(sums[index], axis=1, keepdims=True), packed)
        small[layer] = packed.T[:SMALL_ROWS]

    def steps(*sums_of):
        def run():
            for one in sums_of:
                one.step()
        return run

    early_one = unit_sum(0, 1, 0, 2, "yzx")
    late_one = unit_sum(1, 1, 2, 2, "zyx")
    early_zero = unit_sum(2, 0, 0, 2, "yzx")
    late_zero = [unit_sum(3, 0, 2, 1, "yzx"), unit_sum(4, 0, 3, 1, "zyx")]

    def nothing():
        pass

    backward_weights(1)
    finish_back(1, lambda block: None)
    finish_grads(1)
    early_one.step()
    attend_back(1, [early_one.step, nothing, early_one.step, early_one.step])
    project_back(1)
    project_grads(1)
    early_one.step()
    late_one.step()

    backward_weights(0)
    between = {1: (late_one,), 3: (early_one,)}
    finish_back(0, lambda block: steps(*between.get(block, ()))())
    finish_grads(0)
    early_zero.step()
    early_one.step()
    late_one.step()
    attend_back(0, [
        steps(early_zero, late_one), steps(early_one, late_one),
        steps(early_one, early_zero, late_one), steps(early_zero, late_one),
    ])
    project_back(0)
    y_own.wait()
    y_send.wait()
    x_in[0] = x_now[:, :HALF].T
    x_in[1] = x_now[:, HALF:].T
    d_send = remote(x_in.at[1], grad_ref.at[half], torus.partner)
    d_own = pltpu.make_async_copy(x_in.at[0], grad_ref.at[half], local_sem.at[8])
    d_send.start()
    d_own.start()
    project_grads(0)
    for one in late_zero:
        one.step()
    small_copy = remote(small.at[1 - core], small_far, torus.sibling)
    small_copy.start()
    early_zero.step()
    late_one.step()
    small_copy.wait()
    small_now = small[core] + small_far[...]
    for number, axis in enumerate("xyz"):
        place = small_slots.at[number, torus.axes[axis][0]]
        place[...] = small_now
        copies = [remote(place, place, device) for _, device in torus.peers(axis)]
        for copy in copies:
            copy.start()
        for one in late_zero:
            one.step()
        if number < 2:
            early_zero.step()
        for copy in copies:
            copy.wait()
        small_now = (small_slots[number, 0] + small_slots[number, 1]) + (
            small_slots[number, 2] + small_slots[number, 3])
    small_ref[...] = small_now
    late_one.step()
    early_zero.step()
    early_zero.step()
    for _ in range(5):
        for one in late_zero:
            one.step()
    d_own.wait()
    d_send.wait()
    assert all(one.next == 9 for one in [early_one, late_one, early_zero] + late_zero)


def relay(*operands):
    anywhere = pl.BlockSpec(memory_space=pl.ANY)
    vmem = pl.BlockSpec(memory_space=pltpu.VMEM)
    shape = jax.ShapeDtypeStruct
    f32 = lambda *dims: pltpu.VMEM(dims, F32)
    bf16 = lambda *dims: pltpu.VMEM(dims, BF16)
    copies = 3 + 5 + 2 + 5 * (1 + 9 + 9 + 1) + 1 + 9
    return pl.pallas_call(
        relay_kernel,
        out_shape=(
            shape((2, HALF, WIDTH), F32),
            shape((2, HALF, WIDTH), F32),
            shape((UNITS, UNIT_ROWS, 128), F32),
            shape((SMALL_ROWS, WIDTH), F32),
        ),
        in_specs=[anywhere] * 7 + [vmem] * 8,
        out_specs=(anywhere, anywhere, anywhere, vmem),
        scratch_shapes=[
            f32(2, HALF, WIDTH), pltpu.SMEM((3, 1, 4), jnp.int32),
            f32(2, WIDTH, 3 * WIDTH), f32(2, WIDTH, WIDTH), f32(2, WIDTH, INNER), f32(2, INNER, WIDTH),
            f32(2, SMALL_ROWS, WIDTH),
            bf16(2, 3, WIDTH, WIDTH), bf16(2, WIDTH, WIDTH),
            bf16(2, INNER, WIDTH), bf16(2, WIDTH, INNER), f32(WIDTH, 128),
            f32(16, SLOT), f32(8, SLOT), f32(WIDTH, SLOT), bf16(2, 2, WIDTH, SLOT),
            bf16(2, HEADS, DEEP, SLOT), bf16(2, HEADS, DEEP, SLOT), bf16(2, HEADS, DEEP, SLOT),
            bf16(2, 2, WIDTH, SLOT),
            f32(2, WIDTH, SLOT), f32(2, 1, SLOT), f32(2, INNER, SLOT), bf16(2, 2, INNER, SLOT),
            f32(2, WIDTH, SLOT), f32(2, 1, SLOT),
            bf16(2, WIDTH, SLOT), bf16(2, WIDTH, SLOT),
            bf16(HEADS, DEEP, SLOT), f32(2 * HEAD, SLOT), bf16(2, 3 * WIDTH, SLOT), f32(10, WIDTH, 128),
            f32(2, UNITS, UNIT_ROWS, 128), f32(2, UNITS, UNIT_HALF, 128),
            f32(3, 2, UNITS, CHUNKS[0], 128), f32(3, 2, UNITS, CHUNKS[1], 128), f32(3, 2, UNITS, CHUNKS[2], 128),
            f32(2, UNITS, CHUNKS[0], 128), f32(2, UNITS, CHUNKS[1], 128),
            f32(2, UNITS, UNIT_HALF, 128), f32(UNITS, UNIT_HALF, 128),
            f32(2, SMALL_ROWS, WIDTH), f32(SMALL_ROWS, WIDTH), f32(3, 4, SMALL_ROWS, WIDTH),
            pltpu.SemaphoreType.DMA((11,)),
            pltpu.SemaphoreType.DMA((5, 2)),
            pltpu.SemaphoreType.DMA((copies,)),
            pltpu.SemaphoreType.DMA((copies,)),
        ],
        compiler_params=pltpu.CompilerParams(
            collective_id=0, has_side_effects=True, vmem_limit_bytes=VMEM_BYTES),
        name="relay",
    )(*operands)


def unpack_kernel(
    final_in, grad_in, total_in, small_in,
    final_out, grad_out, w_qkv, b_qv, w_out, b_out, gain_one, shift_one, w_in, b_in, w_back, b_back, gain_two, shift_two,
    final_now, grad_now, total_now, in_sem, sem,
):
    arrivals = [
        pltpu.make_async_copy(src, dst, in_sem.at[i])
        for i, (src, dst) in enumerate(((final_in, final_now), (grad_in, grad_now), (total_in, total_now)))
    ]
    for copy in arrivals:
        copy.start()

    def block(unit, first, rows):
        return total_now.at[unit, pl.ds(first, rows)]

    def lanes(ref, part):
        return ref.at[0, :, pl.ds(part * 128, 128)]

    pairs = [(block(0, 512 * part, 512), lanes(w_back, part)) for part in range(2)]
    pairs += [(block(1, 256 * part, 256), lanes(w_in, part)) for part in range(4)]
    pairs += [(block(2 + part, 0, 256), lanes(w_out, part)) for part in range(2)]
    pairs += [(block(2 + part % 2, 256 + 256 * (part // 2), 256), lanes(w_qkv, part)) for part in range(6)]
    copies = []

    def send(src, dst):
        copy = pltpu.make_async_copy(src, dst, sem.at[len(copies)])
        copy.start()
        copies.append(copy)

    for ref, first, count in (
        (b_qv, V_Q, 2), (b_out, V_OUT, 1), (gain_one, V_GAIN1, 1), (shift_one, V_SHIFT1, 1), (b_in, V_IN, 2),
        (b_back, V_BACK, 1), (gain_two, V_GAIN2, 1), (shift_two, V_SHIFT2, 1),
    ):
        for part in range(count):
            ref[:, part * WIDTH:(part + 1) * WIDTH] = small_in[first + part:first + part + 1, :]
    arrivals[0].wait()
    send(final_now, final_out)
    arrivals[1].wait()
    send(grad_now, grad_out)
    arrivals[2].wait()
    for src, dst in pairs:
        send(src, dst)
    for copy in copies:
        copy.wait()


def unpack(final_output, input_grad, total, small):
    anywhere = pl.BlockSpec(memory_space=pl.ANY)
    vmem = pl.BlockSpec(memory_space=pltpu.VMEM)
    shapes = [
        (2, HALF, WIDTH), (2, HALF, WIDTH), (1, WIDTH, 3 * WIDTH), (1, 2 * WIDTH), (1, WIDTH, WIDTH), (1, WIDTH),
        (1, WIDTH), (1, WIDTH), (1, WIDTH, INNER), (1, INNER), (1, INNER, WIDTH), (1, WIDTH), (1, WIDTH), (1, WIDTH),
    ]
    return pl.pallas_call(
        unpack_kernel,
        out_shape=tuple(jax.ShapeDtypeStruct(dims, F32) for dims in shapes),
        in_specs=[anywhere, anywhere, anywhere, vmem],
        out_specs=tuple(anywhere if len(dims) == 3 else vmem for dims in shapes),
        scratch_shapes=[
            pltpu.VMEM((2, HALF, WIDTH), F32), pltpu.VMEM((2, HALF, WIDTH), F32), pltpu.VMEM((UNITS, UNIT_ROWS, 128), F32),
            pltpu.SemaphoreType.DMA((3,)), pltpu.SemaphoreType.DMA((16,)),
        ],
        compiler_params=pltpu.CompilerParams(vmem_limit_bytes=VMEM_BYTES),
        name="unpack",
    )(final_output, input_grad, total, small)


def body(
    activations, cotangent, cell_lengths, w_qkv, b_qv, w_out, b_out, gain_one, shift_one,
    w_in, b_in, w_back, b_back, gain_two, shift_two,
):
    return unpack(*relay(
        activations, cotangent, jnp.transpose(cell_lengths, (2, 1, 0)), w_qkv, w_out, w_in, w_back,
        b_qv, b_out, gain_one, shift_one, b_in, b_back, gain_two, shift_two))


def solution(mesh):
    rows = P(None, ("dp", "seq"), None)
    matrix = P("pipe", None, None)
    vector = P("pipe", None)
    in_specs = (
        rows, rows, P(None, "dp", None), matrix, vector, matrix, vector, vector, vector,
        matrix, vector, matrix, vector, vector, vector,
    )
    out_rows = P("pipe", ("dp", "seq"), None)
    out_specs = (
        out_rows, out_rows, matrix, vector, matrix, vector, vector, vector,
        matrix, vector, matrix, vector, vector, vector,
    )
    return jax.shard_map(body, mesh=mesh, in_specs=in_specs, out_specs=out_specs, check_vma=False)
```

```python
import math

import jax
import jax.numpy as jnp
from jax import lax
from jax.experimental import pallas as pl
from jax.experimental.pallas import tpu as pltpu
from jax.sharding import PartitionSpec as P

MESH = pl.DeviceIdType.MESH
F32 = jnp.float32
BF16 = jnp.bfloat16

HEADS = 4
HEAD = 64
WIDTH = 256
INNER = 512
HALF = 512
SLOT = 1024
BLOCK = 256
BLOCKS = SLOT // BLOCK
DEEP = 3 * HEAD + 16
EPSILON = 1e-06
APART = -1e30
LOG2E = math.log2(math.e)
LN2 = math.log(2.0)
QUERY_SCALE = LOG2E / math.sqrt(HEAD)
KEY_SCALE = 1.0 / math.sqrt(HEAD)

UNITS, UNIT_ROWS, UNIT_HALF = 4, 1024, 512
CHUNKS = (128, 32, 8)
SMALL_ROWS = 16
VMEM_BYTES = 64 * 2 ** 20 - 2 ** 18
V_Q, V_V, V_OUT, V_GAIN1, V_SHIFT1, V_IN, V_BACK, V_GAIN2, V_SHIFT2 = 0, 1, 2, 3, 4, 5, 7, 8, 9


def dot(left, right, left_t=False, right_t=False):
    dims = (((0 if left_t else 1,), (1 if right_t else 0,)), ((), ()))
    return lax.dot_general(left, right, dims, preferred_element_type=F32)


def split(values):
    high = values.astype(BF16)
    return high, (values - high.astype(F32)).astype(BF16)


def dot3(left_high, left_low, right_high, right_low, left_t=False, right_t=False):
    return (
        dot(left_high, right_high, left_t, right_t)
        + dot(left_high, right_low, left_t, right_t)
        + dot(left_low, right_high, left_t, right_t)
    )


def skewed(tasks):
    waiting, running = list(tasks), []
    while waiting or running:
        if waiting:
            running.insert(0, waiting.pop(0))
        for task in list(running):
            if next(task, "end") == "end":
                running.remove(task)


def staged(count, first, second, third):
    first(0)
    for index in range(count + 1):
        if index + 1 < count:
            first(index + 1)
        if index > 0:
            third(index - 1)
        if index < count:
            second(index)


def col_mean(values):
    return jnp.mean(values, axis=0, keepdims=True)


def norm_rows(values):
    center = values - col_mean(values)
    spread = col_mean(center * center)
    inverse = lax.rsqrt(spread + EPSILON)
    return center * inverse, inverse


def norm_back(grad, normed, inverse):
    return (grad - col_mean(grad) - normed * col_mean(grad * normed)) * inverse


def feature_tile(base, values, first):
    high = values.astype(BF16).astype(F32)
    rest = values - high
    middle = rest.astype(BF16).astype(F32)
    low = rest - middle
    row = lax.broadcasted_iota(jnp.int32, base.shape, 0)
    tile = jnp.where(row == first, high, base)
    tile = jnp.where(row == first + 1, middle, tile)
    return jnp.where(row == first + 2, low, tile).astype(BF16)


def lane_fold(values):
    folded = values[:, :128]
    for first in range(128, values.shape[1], 128):
        folded = folded + values[:, first:first + 128]
    return folded


class Torus:
    def __init__(self):
        self.core = lax.axis_index("pipe")
        self.half = lax.axis_index("seq")
        dp = lax.axis_index("dp")
        x_high, z, y = dp // 16, (dp // 4) % 4, dp % 4
        self.sibling = {"pipe": 1 - self.core}
        self.partner = {"seq": 1 - self.half}
        self.axes = {
            "x": (x_high * 2 + self.half, lambda i: {"dp": (i // 2) * 16 + dp % 16, "seq": i % 2}),
            "y": (y, lambda i: {"dp": dp - y + i}),
            "z": (z, lambda i: {"dp": x_high * 16 + i * 4 + y}),
        }

        self.far_x = [{"dp": (1 - x_high) * 16 + dp % 16, "seq": i} for i in range(2)]
        self.near = {
            axis: [((index + step) % 4, where((index + step) % 4)) for step in (1, 2, 3)]
            for axis, (index, where) in self.axes.items()
        }

    def peer(self, axis, step):
        return self.near[axis][step - 1]

    def peers(self, axis):
        return self.near[axis]


class Sender:
    def __init__(self, send_sem, recv_sem):
        self.send_sem, self.recv_sem, self.used = send_sem, recv_sem, 0

    def take(self):
        self.used += 1
        return self.used - 1

    def __call__(self, src, dst, device):
        return self.build(self.take(), src, dst, device)

    def build(self, index, src, dst, device):
        return pltpu.make_async_remote_copy(
            src_ref=src, dst_ref=dst, send_sem=self.send_sem.at[index], recv_sem=self.recv_sem.at[index],
            device_id=device, device_id_type=MESH,
        )


def span(first, size):
    return pl.ds(pl.multiple_of(first, size), size)


class UnitSum:
    def __init__(self, torus, remote, bufs, total_ref, local_sems, layer, first, count, order):
        self.torus, self.remote, self.bufs = torus, remote, bufs
        self.total_ref, self.local_sems = total_ref, local_sems
        self.layer, self.units, self.order = layer, slice(first, first + count), order
        self.pending = []
        self.next = 0

    def send(self, makers):
        self.pending = [(self.remote.take(), maker) for maker in makers]
        for index, maker in self.pending:
            self.remote.build(index, *maker()).start()

    def settle(self):
        for index, maker in self.pending:
            self.remote.build(index, *maker()).wait()
        self.pending = []

    def offset(self, depth):
        first = 0
        for level in range(depth):
            first = first + self.torus.axes[self.order[level]][0] * CHUNKS[level]
        return first

    def step(self):
        getattr(self, "step_%d" % self.next)()
        self.next += 1

    def step_0(self):
        self.send([lambda: (
            self.bufs["grads"].at[self.layer, self.units, span((1 - self.torus.core) * UNIT_HALF, UNIT_HALF)],
            self.bufs["cores"].at[self.layer, self.units], self.torus.sibling)])

    def base(self, level):
        return self.torus.core * UNIT_HALF if level == 0 else 0

    def scatter(self, level, source):
        size = CHUNKS[level]
        slots = self.bufs["slots"][level]

        def maker(step):
            def make():
                peer, device = self.torus.peer(self.order[level], step)
                return (source.at[self.layer, self.units, span(self.base(level) + peer * size, size)],
                        slots.at[step - 1, self.layer, self.units], device)
            return make

        self.send([maker(step) for step in (1, 2, 3)])

    def gathered(self, level, source):
        size = CHUNKS[level]
        slots = self.bufs["slots"][level]
        first = self.base(level) + self.torus.axes[self.order[level]][0] * size
        own = source[self.layer, self.units, span(first, size), :]
        return (own + slots[0, self.layer, self.units]) + (
            slots[1, self.layer, self.units] + slots[2, self.layer, self.units])

    def step_1(self):
        self.settle()
        grads, cores = self.bufs["grads"], self.bufs["cores"]
        home = span(self.torus.core * UNIT_HALF, UNIT_HALF)
        grads[self.layer, self.units, home, :] += cores[self.layer, self.units]
        self.scatter(0, grads)

    def step_2(self):
        self.settle()
        partial = self.bufs["partial"][0]
        partial[self.layer, self.units] = self.gathered(0, self.bufs["grads"])
        self.scatter(1, partial)

    def step_3(self):
        self.settle()
        partial = self.bufs["partial"][1]
        partial[self.layer, self.units] = self.gathered(1, self.bufs["partial"][0])
        self.scatter(2, partial)

    def spread(self, level):
        size = CHUNKS[level]

        def maker(step):
            def make():
                chunk = self.bufs["done"].at[self.layer, self.units, span(self.offset(level + 1), size)]
                return chunk, chunk, self.torus.peer(self.order[level], step)[1]
            return make

        self.send([maker(step) for step in (1, 2, 3)])

    def step_4(self):
        self.settle()
        rows = span(self.offset(3), CHUNKS[2])
        self.bufs["done"][self.layer, self.units, rows, :] = self.gathered(2, self.bufs["partial"][1])
        self.spread(2)

    def step_5(self):
        self.settle()
        self.spread(1)

    def step_6(self):
        self.settle()
        self.spread(0)

    def away_copy(self):
        return self.remote.build(
            self.away, self.bufs["done"].at[self.layer, self.units], self.bufs["far"].at[self.units], self.torus.sibling)

    def near_copy(self):
        return pltpu.make_async_copy(
            self.bufs["done"].at[self.layer, self.units],
            self.total_ref.at[self.units, span(self.torus.core * UNIT_HALF, UNIT_HALF)], self.local_sems.at[0])

    def far_copy(self):
        return pltpu.make_async_copy(
            self.bufs["far"].at[self.units],
            self.total_ref.at[self.units, span((1 - self.torus.core) * UNIT_HALF, UNIT_HALF)], self.local_sems.at[1])

    def step_7(self):
        self.settle()
        self.away = self.remote.take()

        @pl.when(self.torus.core == self.layer)
        def _():
            self.near_copy().start()

        @pl.when(self.torus.core != self.layer)
        def _():
            self.away_copy().start()

    def step_8(self):
        @pl.when(self.torus.core == self.layer)
        def _():
            self.away_copy().wait_recv()
            self.far_copy().start()
            self.near_copy().wait()
            self.far_copy().wait()

        @pl.when(self.torus.core != self.layer)
        def _():
            self.away_copy().wait_send()


def relay_kernel(
    act_ref, cot_ref, len_ref, w_qkv_ref, w_out_ref, w_in_ref, w_back_ref,
    b_qv_ref, b_out_ref, gain_one_ref, shift_one_ref, b_in_ref, b_back_ref, gain_two_ref, shift_two_ref,
    final_ref, grad_ref, total_ref, small_ref,
    x_in, lengths, vecs, p_qkv, p_out, p_in, p_back, cols,
    marks, live, x_now, x_parts, q_all, k_all, v_all, ctx_parts,
    n_one, r_one, slope, inner_parts, n_two, r_two,
    dl_parts, du_parts, do_all, dkv, dqkv, sums,
    grads, cores, slots_0, slots_1, slots_2, partial_0, partial_1, done, far, small, small_far, small_slots,
    local_sem, out_sem, send_sem, recv_sem,
):
    torus = Torus()
    core, half = torus.core, torus.half
    remote = Sender(send_sem, recv_sem)

    barrier = pltpu.get_barrier_semaphore()
    pl.semaphore_signal(barrier, inc=1, device_id=torus.partner, device_id_type=MESH)
    pl.semaphore_signal(barrier, inc=1, device_id=torus.sibling, device_id_type=MESH)
    for axis in "yz":
        for _, device in torus.peers(axis):
            pl.semaphore_signal(barrier, inc=1, device_id=device, device_id_type=MESH)
    pl.semaphore_signal(barrier, inc=1, device_id=torus.far_x[0], device_id_type=MESH)
    pl.semaphore_signal(barrier, inc=1, device_id=torus.far_x[1], device_id_type=MESH)

    mine = 2 * core + half
    theirs = 2 * core + 1 - half

    def weight_pairs(layer):
        return (
            (w_qkv_ref.at[0], slope.at[layer, 0:WIDTH, 0:768]),
            (w_out_ref.at[0], slope.at[layer, WIDTH:INNER, 0:WIDTH]),
            (w_in_ref.at[0], slope.at[layer, WIDTH:INNER, WIDTH:768]),
            (w_back_ref.at[0], slope.at[layer, 0:INNER, 768:SLOT]),
        )

    len_own = pltpu.make_async_copy(len_ref, lengths, local_sem.at[0])
    x_own = pltpu.make_async_copy(act_ref.at[mine], x_in.at[0], local_sem.at[1])
    c_owns = [
        pltpu.make_async_copy(cot_ref.at[mine, :, pl.ds(part * 128, 128)], far.at[part], local_sem.at[9 + part])
        for part in range(2)
    ]
    w_owns = [
        pltpu.make_async_copy(src, dst, local_sem.at[3 + i])
        for i, (src, dst) in enumerate(weight_pairs(core))
    ]
    len_own.start()
    x_own.start()
    for copy in w_owns:
        copy.start()
    vecs[core] = jnp.concatenate([
        b_qv_ref[:, :WIDTH], b_qv_ref[:, WIDTH:], b_out_ref[...], gain_one_ref[...], shift_one_ref[...],
        b_in_ref[:, :WIDTH], b_in_ref[:, WIDTH:], b_back_ref[...], gain_two_ref[...], shift_two_ref[...],
        jnp.zeros((6, WIDTH), F32)], axis=0)

    pl.semaphore_wait(barrier, 10)

    x_sends = [
        remote(act_ref.at[theirs, pl.ds(part * BLOCK, BLOCK)], x_in.at[1, pl.ds(part * BLOCK, BLOCK)], torus.partner)
        for part in range(2)
    ]
    c_sends = [
        remote(cot_ref.at[theirs, :, pl.ds(part * 128, 128)], far.at[2 + part], torus.partner) for part in range(2)
    ]
    w_sends = [remote(src, dst, torus.sibling) for src, dst in weight_pairs(core)]
    w_sends.append(remote(vecs.at[core], vecs.at[core], torus.sibling))
    for copy in x_sends + w_sends:
        copy.start()
    for copy in c_owns:
        copy.start()

    len_own.wait()
    lane = lax.broadcasted_iota(jnp.int32, (16, SLOT), 1)
    row = lax.broadcasted_iota(jnp.int32, (16, SLOT), 0)
    place = jnp.where(lane < HALF, half * HALF + lane, (1 - half) * HALF + lane - HALF)
    end_0 = lengths[0, 0, mine]
    end_1 = end_0 + lengths[1, 0, mine]
    end_2 = end_1 + lengths[2, 0, mine]
    one = jnp.ones_like(place)
    none = jnp.zeros_like(place)
    cell = (
        jnp.where(place >= end_0, one, none)
        + jnp.where(place >= end_1, one, none)
        + jnp.where(place >= end_2, one, none)
    )
    same = jnp.where(cell == row, 1.0, 0.0)
    marks[...] = same
    live[...] = jnp.where(cell < 3, 1.0, 0.0)[:8]
    key_marks = jnp.where(row < 4, (1.0 - same) * APART, jnp.where(row < 7, 1.0, 0.0)).astype(BF16)
    value_marks = jnp.where(row < 3, 1.0, 0.0).astype(BF16)
    query_marks = same.astype(BF16)
    for layer in range(2):
        for head in range(HEADS):
            q_all[layer, head, 192:208, :] = query_marks
            k_all[layer, head, 192:208, :] = key_marks
            v_all[layer, head, 192:208, :] = value_marks

    def load_weights(layer):
        cols[layer] = jnp.concatenate([vecs[layer].T, jnp.zeros((WIDTH, 128 - SMALL_ROWS), F32)], axis=1)
        p_qkv[layer, 0], p_qkv[layer, 1] = split(slope[layer, 0:WIDTH, 0:768])
        p_out[layer, 0], p_out[layer, 1] = split(slope[layer, WIDTH:INNER, 0:WIDTH])
        p_in[layer, 0], p_in[layer, 1] = split(slope[layer, WIDTH:INNER, WIDTH:768])
        p_back[layer, 0], p_back[layer, 1] = split(slope[layer, 0:INNER, 768:SLOT])

    def col(layer, index):
        return cols[layer, :, index:index + 1]

    def block_at(block):
        return slice(block * BLOCK, (block + 1) * BLOCK)

    def project_block(layer, block):
        at = block_at(block)
        x_high, x_low = split(x_now[:, at])
        x_parts[layer, 0, :, at] = x_high
        x_parts[layer, 1, :, at] = x_low
        queries, key_rows, value_rows = (
            dot3(p_qkv[layer, 0, :, part * WIDTH:(part + 1) * WIDTH], p_qkv[layer, 1, :, part * WIDTH:(part + 1) * WIDTH],
                 x_high, x_low, left_t=True)
            for part in range(3))
        yield
        q_high, q_low = split((queries + col(layer, V_Q)) * QUERY_SCALE)
        k_high, k_low = split(key_rows)
        v_high, v_low = split(value_rows + col(layer, V_V))
        for head in range(HEADS):
            rows = slice(head * HEAD, (head + 1) * HEAD)
            q_all[layer, head, 0:64, at] = q_high[rows]
            q_all[layer, head, 64:128, at] = q_high[rows]
            q_all[layer, head, 128:192, at] = q_low[rows]
            k_all[layer, head, 0:64, at] = k_high[rows]
            k_all[layer, head, 64:128, at] = k_low[rows]
            k_all[layer, head, 128:192, at] = k_high[rows]
            v_all[layer, head, 0:64, at] = v_high[rows]
            v_all[layer, head, 64:128, at] = v_low[rows]
            v_all[layer, head, 128:192, at] = v_high[rows]

    def project(layer, blocks):
        skewed(project_block(layer, block) for block in blocks)

    def attend(layer):
        def two_heads(pair, inside):
            def one_block(index):
                head = pair * 2 + index // BLOCKS
                rows = span(head * HEAD, HEAD)
                at = block_at(index % BLOCKS)
                scores = dot(k_all[layer, head], q_all[layer, head, :, at], left_t=True)
                yield
                top = jnp.max(scores, axis=0, keepdims=True)
                weights = jnp.exp2(scores - top)
                total = jnp.sum(weights, axis=0, keepdims=True)
                high, low = split(weights)
                both = dot(v_all[layer, head, 0:128, :], high)
                context = both[:64] + both[64:] + dot(v_all[layer, head, 0:64, :], low)
                context = context / total
                ctx_parts[layer, 0, rows, at], ctx_parts[layer, 1, rows, at] = split(context)
                log_total = top + jnp.log(total) * LOG2E
                q_all[layer, head, 192:208, at] = feature_tile(marks[:, at], -log_total, 4)

            skewed(one_block(index) for index in range(2 * BLOCKS))
            return inside

        lax.fori_loop(0, HEADS // 2, two_heads, 0)

    def feed_block(layer, block):
        at = block_at(block)
        upper = x_now[:, at] + dot3(
            p_out[layer, 0], p_out[layer, 1], ctx_parts[layer, 0, :, at], ctx_parts[layer, 1, :, at], left_t=True
        ) + col(layer, V_OUT)
        normed, inverse = norm_rows(upper)
        n_one[layer, :, at] = normed
        r_one[layer, :, at] = inverse
        hidden = normed * col(layer, V_GAIN1) + col(layer, V_SHIFT1)
        hid_high, hid_low = split(hidden)
        yield
        in_bias = jnp.concatenate([col(layer, V_IN), col(layer, V_IN + 1)], axis=0)
        pre = dot3(p_in[layer, 0], p_in[layer, 1], hid_high, hid_low, left_t=True) + in_bias
        share = 0.5 + 0.5 * lax.erf(pre * math.sqrt(0.5))
        slope[layer, :, at] = share + pre * (jnp.exp(pre * pre * -0.5) * (1.0 / math.sqrt(2.0 * math.pi)))
        inner_high, inner_low = split(pre * share)
        inner_parts[layer, 0, :, at] = inner_high
        inner_parts[layer, 1, :, at] = inner_low
        yield
        lower = hidden + dot3(p_back[layer, 0], p_back[layer, 1], inner_high, inner_low, left_t=True) + col(layer, V_BACK)
        normed, inverse = norm_rows(lower)
        n_two[layer, :, at] = normed
        r_two[layer, :, at] = inverse
        x_now[:, at] = live[0:1, at] * (normed * col(layer, V_GAIN2) + col(layer, V_SHIFT2))

    def feed_forward(layer):
        skewed(feed_block(layer, block) for block in range(BLOCKS))

    for copy in w_owns:
        copy.wait()
    for copy in w_sends:
        copy.wait()
    load_weights(0)
    x_own.wait()
    x_now[:, :HALF] = x_in[0].T
    project(0, (0, 1))
    load_weights(1)
    for part in range(2):
        x_sends[part].wait()
        if part == 1:
            for copy in c_sends:
                copy.start()
        x_now[:, block_at(2 + part)] = x_in[1, part * BLOCK:(part + 1) * BLOCK].T
        project(0, (2 + part,))
    attend(0)
    feed_forward(0)
    project(1, (0, 1, 2, 3))
    attend(1)
    feed_forward(1)

    x_in[0] = x_now[:, :HALF].T
    x_in[1] = x_now[:, HALF:].T
    y_send = remote(x_in.at[1], final_ref.at[half], torus.partner)
    y_own = pltpu.make_async_copy(x_in.at[0], final_ref.at[half], local_sem.at[7])
    for copy in c_owns + c_sends:
        copy.wait()
    y_send.start()
    y_own.start()
    for part in range(2):
        x_now[part * 128:(part + 1) * 128, :HALF] = far[part].T
        x_now[part * 128:(part + 1) * 128, HALF:] = far[2 + part].T

    bufs = {
        "grads": grads, "cores": cores, "slots": (slots_0, slots_1, slots_2),
        "partial": (partial_0, partial_1), "done": done, "far": far,
    }

    def unit_sum(number, layer, first, count, order):
        return UnitSum(torus, remote, bufs, total_ref, out_sem.at[number], layer, first, count, order)

    dp_parts = dqkv.at[:, 0:INNER]
    hid_parts = dqkv.at[:, INNER:INNER + WIDTH]

    def add_sum(index, values):
        sums[index] += lane_fold(values)

    def back_block(layer, block):
        at = block_at(block)
        grad = live[0:1, at] * x_now[:, at]
        normed = n_two[layer, :, at]
        add_sum(V_GAIN2, grad * normed)
        add_sum(V_SHIFT2, grad)
        d_lower = norm_back(grad * col(layer, V_GAIN2), normed, r_two[layer, :, at])
        add_sum(V_BACK, d_lower)
        high, low = split(d_lower)
        dl_parts[0, :, at] = high
        dl_parts[1, :, at] = low
        yield
        d_pre = dot3(p_back[layer, 0], p_back[layer, 1], high, low) * slope[layer, :, at]
        add_sum(V_IN, d_pre[:WIDTH])
        add_sum(V_IN + 1, d_pre[WIDTH:])
        high, low = split(d_pre)
        dp_parts[0, :, at] = high
        dp_parts[1, :, at] = low
        yield
        d_hidden = d_lower + dot3(p_in[layer, 0], p_in[layer, 1], high, low)
        normed = n_one[layer, :, at]
        hid_parts[0, :, at], hid_parts[1, :, at] = split(normed * col(layer, V_GAIN1) + col(layer, V_SHIFT1))
        add_sum(V_GAIN1, d_hidden * normed)
        add_sum(V_SHIFT1, d_hidden)
        d_upper = norm_back(d_hidden * col(layer, V_GAIN1), normed, r_one[layer, :, at])
        add_sum(V_OUT, d_upper)
        x_now[:, at] = d_upper
        high, low = split(d_upper)
        du_parts[0, :, at] = high
        du_parts[1, :, at] = low
        yield
        d_context = dot3(p_out[layer, 0], p_out[layer, 1], high, low)
        high, low = split(d_context)
        context = ctx_parts[layer, 0, :, at].astype(F32) + ctx_parts[layer, 1, :, at].astype(F32)
        product = d_context * context
        for head in range(HEADS):
            rows = slice(head * HEAD, (head + 1) * HEAD)
            do_all[head, 0:64, at] = high[rows]
            do_all[head, 64:128, at] = high[rows]
            do_all[head, 128:192, at] = low[rows]
            row_dot = jnp.sum(product[rows], axis=0, keepdims=True)
            do_all[head, 192:208, at] = feature_tile(jnp.zeros((16, BLOCK), F32), -row_dot, 0)

    def finish_back(layer, blocks):
        skewed(back_block(layer, block) for block in blocks)

    def put(layer, unit, first, values):
        rows = values.shape[0]
        for part in range(values.shape[1] // 128):
            begin = first + part * rows
            grads[layer, unit, begin:begin + rows, :] = values[:, part * 128:(part + 1) * 128]

    def finish_grads(layer):
        put(layer, 0, 0, dot3(
            inner_parts[layer, 0], inner_parts[layer, 1], dl_parts[0], dl_parts[1], right_t=True))
        put(layer, 1, 0, dot3(hid_parts[0], hid_parts[1], dp_parts[0], dp_parts[1], right_t=True))
        grad_out = dot3(ctx_parts[layer, 0], ctx_parts[layer, 1], du_parts[0], du_parts[1], right_t=True)
        put(layer, 2, 0, grad_out[:, :128])
        put(layer, 3, 0, grad_out[:, 128:])

    def attend_back(layer, after_head):
        def one_head(head, inside):
            rows = span(head * HEAD, HEAD)
            products, parts = {}, {}

            def scores(block):
                at = block_at(block)
                products[block] = (
                    dot(q_all[layer, head, :, at], k_all[layer, head], left_t=True),
                    dot(do_all[head, :, at], v_all[layer, head], left_t=True),
                )

            def weigh(block):
                exponent, d_probs = products.pop(block)
                probs = jnp.exp2(exponent)
                parts[block] = split(probs) + split(probs * d_probs)

            def multiply(block):
                at = block_at(block)
                p_high, p_low, s_high, s_low = parts.pop(block)
                both = dot(k_all[layer, head, 0:128, :], s_high, right_t=True)
                d_query = (both[:64] + both[64:] + dot(k_all[layer, head, 0:64, :], s_low, right_t=True)) * KEY_SCALE
                sums[V_Q, rows, :] += lane_fold(d_query)
                dqkv[0, rows, at], dqkv[1, rows, at] = split(d_query)
                both = dot(q_all[layer, head, 64:192, at], s_high)
                d_key = both[:64] + both[64:] + dot(q_all[layer, head, 64:128, at], s_low)
                both = dot(do_all[head, 64:192, at], p_high)
                d_value = both[:64] + both[64:] + dot(do_all[head, 64:128, at], p_low)
                if block > 0:
                    d_key = dkv[0:64, :] + d_key
                    d_value = dkv[64:128, :] + d_value
                if block < BLOCKS - 1:
                    dkv[0:64, :] = d_key
                    dkv[64:128, :] = d_value
                    return
                k_rows = span(WIDTH + head * HEAD, HEAD)
                v_rows = span(2 * WIDTH + head * HEAD, HEAD)
                dqkv[0, k_rows, :], dqkv[1, k_rows, :] = split(d_key * LN2)
                dqkv[0, v_rows, :], dqkv[1, v_rows, :] = split(d_value)
                sums[V_V, rows, :] += lane_fold(d_value)

            staged(BLOCKS, scores, weigh, multiply)
            for number, todo in enumerate(after_head):

                @pl.when(head == number)
                def _():
                    todo()

            return inside

        lax.fori_loop(0, HEADS, one_head, 0)

    def project_back(layer):
        for block in range(BLOCKS):
            at = block_at(block)
            total = x_now[:, at]
            for part in range(3):
                rows = slice(part * WIDTH, (part + 1) * WIDTH)
                total = total + dot3(
                    p_qkv[layer, 0, :, rows], p_qkv[layer, 1, :, rows], dqkv[0, rows, at], dqkv[1, rows, at])
            x_now[:, at] = total

    def project_grads(layer, pair):
        for part in range(3):
            rows = slice(part * WIDTH + pair * 128, part * WIDTH + (pair + 1) * 128)
            begin = WIDTH + part * WIDTH
            grads[layer, 2 + pair, begin:begin + WIDTH, :] = dot3(
                x_parts[layer, 0], x_parts[layer, 1], dqkv[0, rows], dqkv[1, rows], right_t=True)

    def sum_lanes(layer):
        lane_small = lax.broadcasted_iota(jnp.int32, (WIDTH, 128), 1)
        packed = jnp.zeros((WIDTH, 128), F32)
        for index in range(10):
            packed = jnp.where(lane_small == index, jnp.sum(sums[index], axis=1, keepdims=True), packed)
        small[layer] = packed.T[:SMALL_ROWS]

    def steps(*sums_of):
        def run():
            for one in sums_of:
                one.step()
        return run

    one_a = unit_sum(0, 1, 0, 2, "yzx")
    one_b = unit_sum(1, 1, 2, 2, "zyx")
    zero_a = unit_sum(2, 0, 0, 2, "zyx")
    zero_b = unit_sum(3, 0, 2, 1, "xyz")
    zero_c = unit_sum(4, 0, 3, 1, "yzx")

    def nothing():
        pass

    sums[...] = jnp.zeros_like(sums)
    finish_back(1, range(BLOCKS))
    finish_grads(1)
    one_a.step()
    attend_back(1, [one_a.step, nothing, one_a.step])
    project_grads(1, 0)
    project_grads(1, 1)
    one_b.step()
    one_a.step()
    project_back(1)
    sum_lanes(1)

    sums[...] = jnp.zeros_like(sums)
    one_b.step()
    one_a.step()
    finish_back(0, range(BLOCKS))
    one_a.step()
    finish_grads(0)
    zero_a.step()
    one_b.step()
    one_a.step()

    def after_second():
        one_b.step()
        project_grads(0, 0)
        zero_b.step()

    attend_back(0, [
        zero_a.step, after_second, steps(one_a, zero_a, one_b, zero_b), steps(one_a, zero_a, one_b),
    ])
    project_grads(0, 1)
    zero_c.step()
    sum_lanes(0)
    small_copy = remote(small.at[1 - core], small_far, torus.sibling)
    small_copy.start()
    project_back(0)
    y_own.wait()
    y_send.wait()
    x_in[1] = x_now[:, HALF:].T
    d_send = remote(x_in.at[1], grad_ref.at[half], torus.partner)
    d_send.start()
    zero_c.step()
    x_in[0] = x_now[:, :HALF].T
    d_own = pltpu.make_async_copy(x_in.at[0], grad_ref.at[half], local_sem.at[8])
    d_own.start()
    small_copy.wait()
    small_now = small[core] + small_far[...]
    rounds = ((zero_b, one_b), (zero_b, zero_a), (zero_b, zero_a, one_b), (zero_b, zero_a), (zero_b, zero_a))
    for number, others in enumerate(rounds):
        copies = []
        if number < 3:
            axis = "yzx"[number]
            place = small_slots.at[number, torus.axes[axis][0]]
            place[...] = small_now
            copies = [remote(place, place, device) for _, device in torus.peers(axis)]
            for copy in copies:
                copy.start()
        zero_c.step()
        for one in others:
            one.step()
        for copy in copies:
            copy.wait()
        if number < 3:
            small_now = (small_slots[number, 0] + small_slots[number, 1]) + (
                small_slots[number, 2] + small_slots[number, 3])
    small_ref[...] = small_now
    for one in (one_b, zero_a, zero_b, zero_b, zero_c, zero_c):
        one.step()
    d_own.wait()
    d_send.wait()
    assert all(one.next == 9 for one in (one_a, one_b, zero_a, zero_b, zero_c))


def relay(*operands):
    anywhere = pl.BlockSpec(memory_space=pl.ANY)
    vmem = pl.BlockSpec(memory_space=pltpu.VMEM)
    shape = jax.ShapeDtypeStruct
    f32 = lambda *dims: pltpu.VMEM(dims, F32)
    bf16 = lambda *dims: pltpu.VMEM(dims, BF16)
    copies = 4 + 5 + 2 + 5 * (1 + 9 + 9 + 1) + 1 + 9
    return pl.pallas_call(
        relay_kernel,
        out_shape=(
            shape((2, HALF, WIDTH), F32),
            shape((2, HALF, WIDTH), F32),
            shape((UNITS, UNIT_ROWS, 128), F32),
            shape((SMALL_ROWS, WIDTH), F32),
        ),
        in_specs=[anywhere] * 7 + [vmem] * 8,
        out_specs=(anywhere, anywhere, anywhere, vmem),
        scratch_shapes=[
            f32(2, HALF, WIDTH), pltpu.SMEM((3, 1, 4), jnp.int32),
            f32(2, SMALL_ROWS, WIDTH),
            bf16(2, 2, WIDTH, 3 * WIDTH), bf16(2, 2, WIDTH, WIDTH), bf16(2, 2, WIDTH, INNER), bf16(2, 2, INNER, WIDTH),
            f32(2, WIDTH, 128),
            f32(16, SLOT), f32(8, SLOT), f32(WIDTH, SLOT), bf16(2, 2, WIDTH, SLOT),
            bf16(2, HEADS, DEEP, SLOT), bf16(2, HEADS, DEEP, SLOT), bf16(2, HEADS, DEEP, SLOT),
            bf16(2, 2, WIDTH, SLOT),
            f32(2, WIDTH, SLOT), f32(2, 1, SLOT), f32(2, INNER, SLOT), bf16(2, 2, INNER, SLOT),
            f32(2, WIDTH, SLOT), f32(2, 1, SLOT),
            bf16(2, WIDTH, SLOT), bf16(2, WIDTH, SLOT),
            bf16(HEADS, DEEP, SLOT), f32(2 * HEAD, SLOT), bf16(2, 3 * WIDTH, SLOT), f32(10, WIDTH, 128),
            f32(2, UNITS, UNIT_ROWS, 128), f32(2, UNITS, UNIT_HALF, 128),
            f32(3, 2, UNITS, CHUNKS[0], 128), f32(3, 2, UNITS, CHUNKS[1], 128), f32(3, 2, UNITS, CHUNKS[2], 128),
            f32(2, UNITS, CHUNKS[0], 128), f32(2, UNITS, CHUNKS[1], 128),
            f32(2, UNITS, UNIT_HALF, 128), f32(UNITS, UNIT_HALF, 128),
            f32(2, SMALL_ROWS, WIDTH), f32(SMALL_ROWS, WIDTH), f32(3, 4, SMALL_ROWS, WIDTH),
            pltpu.SemaphoreType.DMA((11,)),
            pltpu.SemaphoreType.DMA((5, 2)),
            pltpu.SemaphoreType.DMA((copies,)),
            pltpu.SemaphoreType.DMA((copies,)),
        ],
        compiler_params=pltpu.CompilerParams(
            collective_id=0, has_side_effects=True, vmem_limit_bytes=VMEM_BYTES),
        name="relay",
    )(*operands)


def unpack_kernel(
    final_in, grad_in, total_in, small_in,
    final_out, grad_out, w_qkv, b_qv, w_out, b_out, gain_one, shift_one, w_in, b_in, w_back, b_back, gain_two, shift_two,
    final_now, grad_now, total_now, in_sem, sem,
):
    arrivals = [
        pltpu.make_async_copy(src, dst, in_sem.at[i])
        for i, (src, dst) in enumerate(((final_in, final_now), (grad_in, grad_now), (total_in, total_now)))
    ]
    for copy in arrivals:
        copy.start()

    def block(unit, first, rows):
        return total_now.at[unit, pl.ds(first, rows)]

    def lanes(ref, part):
        return ref.at[0, :, pl.ds(part * 128, 128)]

    pairs = [(block(0, 512 * part, 512), lanes(w_back, part)) for part in range(2)]
    pairs += [(block(1, 256 * part, 256), lanes(w_in, part)) for part in range(4)]
    pairs += [(block(2 + part, 0, 256), lanes(w_out, part)) for part in range(2)]
    pairs += [(block(2 + part % 2, 256 + 256 * (part // 2), 256), lanes(w_qkv, part)) for part in range(6)]
    copies = []

    def send(src, dst):
        copy = pltpu.make_async_copy(src, dst, sem.at[len(copies)])
        copy.start()
        copies.append(copy)

    for ref, first, count in (
        (b_qv, V_Q, 2), (b_out, V_OUT, 1), (gain_one, V_GAIN1, 1), (shift_one, V_SHIFT1, 1), (b_in, V_IN, 2),
        (b_back, V_BACK, 1), (gain_two, V_GAIN2, 1), (shift_two, V_SHIFT2, 1),
    ):
        for part in range(count):
            ref[:, part * WIDTH:(part + 1) * WIDTH] = small_in[first + part:first + part + 1, :]
    arrivals[0].wait()
    send(final_now, final_out)
    arrivals[1].wait()
    send(grad_now, grad_out)
    arrivals[2].wait()
    for src, dst in pairs:
        send(src, dst)
    for copy in copies:
        copy.wait()


def unpack(final_output, input_grad, total, small):
    anywhere = pl.BlockSpec(memory_space=pl.ANY)
    vmem = pl.BlockSpec(memory_space=pltpu.VMEM)
    shapes = [
        (2, HALF, WIDTH), (2, HALF, WIDTH), (1, WIDTH, 3 * WIDTH), (1, 2 * WIDTH), (1, WIDTH, WIDTH), (1, WIDTH),
        (1, WIDTH), (1, WIDTH), (1, WIDTH, INNER), (1, INNER), (1, INNER, WIDTH), (1, WIDTH), (1, WIDTH), (1, WIDTH),
    ]
    return pl.pallas_call(
        unpack_kernel,
        out_shape=tuple(jax.ShapeDtypeStruct(dims, F32) for dims in shapes),
        in_specs=[anywhere, anywhere, anywhere, vmem],
        out_specs=tuple(anywhere if len(dims) == 3 else vmem for dims in shapes),
        scratch_shapes=[
            pltpu.VMEM((2, HALF, WIDTH), F32), pltpu.VMEM((2, HALF, WIDTH), F32), pltpu.VMEM((UNITS, UNIT_ROWS, 128), F32),
            pltpu.SemaphoreType.DMA((3,)), pltpu.SemaphoreType.DMA((16,)),
        ],
        compiler_params=pltpu.CompilerParams(vmem_limit_bytes=VMEM_BYTES),
        name="unpack",
    )(final_output, input_grad, total, small)


def body(
    activations, cotangent, cell_lengths, w_qkv, b_qv, w_out, b_out, gain_one, shift_one,
    w_in, b_in, w_back, b_back, gain_two, shift_two,
):
    return unpack(*relay(
        activations, cotangent, jnp.transpose(cell_lengths, (2, 1, 0)), w_qkv, w_out, w_in, w_back,
        b_qv, b_out, gain_one, shift_one, b_in, b_back, gain_two, shift_two))


def solution(mesh):
    rows = P(None, ("dp", "seq"), None)
    matrix = P("pipe", None, None)
    vector = P("pipe", None)
    in_specs = (
        rows, rows, P(None, "dp", None), matrix, vector, matrix, vector, vector, vector,
        matrix, vector, matrix, vector, vector, vector,
    )
    out_rows = P("pipe", ("dp", "seq"), None)
    out_specs = (
        out_rows, out_rows, matrix, vector, matrix, vector, vector, vector,
        matrix, vector, matrix, vector, vector, vector,
    )
    return jax.shard_map(body, mesh=mesh, in_specs=in_specs, out_specs=out_specs, check_vma=False)
```

```python
import math

import jax
import jax.numpy as jnp
from jax import lax
from jax.experimental import pallas as pl
from jax.experimental.pallas import tpu as pltpu
from jax.sharding import PartitionSpec as P

MESH = pl.DeviceIdType.MESH
F32 = jnp.float32
BF16 = jnp.bfloat16

HEADS = 4
HEAD = 64
WIDTH = 256
INNER = 512
HALF = 512
SLOT = 1024
BLOCK = 256
BLOCKS = SLOT // BLOCK
DEEP = 3 * HEAD + 16
EPSILON = 1e-06
APART = -1e30
LOG2E = math.log2(math.e)
LN2 = math.log(2.0)
QUERY_SCALE = LOG2E / math.sqrt(HEAD)
KEY_SCALE = 1.0 / math.sqrt(HEAD)

UNITS, UNIT_ROWS, UNIT_HALF = 4, 1024, 512
CHUNKS = (128, 32)
SMALL_ROWS = 16
VMEM_BYTES = 64 * 2 ** 20 - 2 ** 18
V_Q, V_V, V_OUT, V_GAIN1, V_SHIFT1, V_IN, V_BACK, V_GAIN2, V_SHIFT2 = 0, 1, 2, 3, 4, 5, 7, 8, 9


def dot(left, right, left_t=False, right_t=False):
    dims = (((0 if left_t else 1,), (1 if right_t else 0,)), ((), ()))
    return lax.dot_general(left, right, dims, preferred_element_type=F32)


def split(values):
    high = values.astype(BF16)
    return high, (values - high.astype(F32)).astype(BF16)


def dot3(left_high, left_low, right_high, right_low, left_t=False, right_t=False):
    return (
        dot(left_high, right_high, left_t, right_t)
        + dot(left_high, right_low, left_t, right_t)
        + dot(left_low, right_high, left_t, right_t)
    )


def skewed(tasks):
    waiting, running = list(tasks), []
    while waiting or running:
        if waiting:
            running.insert(0, waiting.pop(0))
        for task in list(running):
            if next(task, "end") == "end":
                running.remove(task)


def staged(count, first, second, third):
    first(0)
    for index in range(count + 1):
        if index + 1 < count:
            first(index + 1)
        if index > 0:
            third(index - 1)
        if index < count:
            second(index)


def col_mean(values):
    return jnp.mean(values, axis=0, keepdims=True)


def norm_rows(values):
    center = values - col_mean(values)
    spread = col_mean(center * center)
    inverse = lax.rsqrt(spread + EPSILON)
    return center * inverse, inverse


def norm_back(grad, normed, inverse):
    return (grad - col_mean(grad) - normed * col_mean(grad * normed)) * inverse


def feature_tile(base, values, first):
    high = values.astype(BF16).astype(F32)
    rest = values - high
    middle = rest.astype(BF16).astype(F32)
    low = rest - middle
    row = lax.broadcasted_iota(jnp.int32, base.shape, 0)
    tile = jnp.where(row == first, high, base)
    tile = jnp.where(row == first + 1, middle, tile)
    return jnp.where(row == first + 2, low, tile).astype(BF16)


def lane_fold(values):
    folded = values[:, :128]
    for first in range(128, values.shape[1], 128):
        folded = folded + values[:, first:first + 128]
    return folded


class Torus:
    def __init__(self):
        self.core = lax.axis_index("pipe")
        self.half = lax.axis_index("seq")
        dp = lax.axis_index("dp")
        x_high, z, y = dp // 16, (dp // 4) % 4, dp % 4
        self.sibling = {"pipe": 1 - self.core}
        self.partner = {"seq": 1 - self.half}
        self.axes = {
            "x": (x_high * 2 + self.half, lambda i: {"dp": (i // 2) * 16 + dp % 16, "seq": i % 2}),
            "y": (y, lambda i: {"dp": dp - y + i}),
            "z": (z, lambda i: {"dp": x_high * 16 + i * 4 + y}),
        }

        self.near = {
            axis: [((index + step) % 4, where((index + step) % 4)) for step in (1, 2, 3)]
            for axis, (index, where) in self.axes.items()
        }

    def peer(self, axis, step):
        return self.near[axis][step - 1]

    def peers(self, axis):
        return self.near[axis]


class Sender:
    def __init__(self, send_sem, recv_sem):
        self.send_sem, self.recv_sem, self.used = send_sem, recv_sem, 0

    def take(self, count=1):
        self.used += count
        return self.used - count

    def __call__(self, src, dst, device):
        return self.build(self.take(), src, dst, device)

    def build(self, index, src, dst, device):
        return pltpu.make_async_remote_copy(
            src_ref=src, dst_ref=dst, send_sem=self.send_sem.at[index], recv_sem=self.recv_sem.at[index],
            device_id=device, device_id_type=MESH,
        )


def span(first, size):
    return pl.ds(pl.multiple_of(first, size), size)


class UnitSum:
    def __init__(self, torus, remote, bufs, total_ref, done_sem, layer, first, count, order):
        self.torus, self.remote, self.bufs = torus, remote, bufs
        self.total_ref, self.done_sem = total_ref, done_sem
        self.layer, self.units, self.order = layer, slice(first, first + count), order
        self.pending = []
        self.next = 0

    def send(self, makers):
        self.pending = [(self.remote.take(), maker) for maker in makers]
        for index, maker in self.pending:
            self.remote.build(index, *maker()).start()

    def settle(self):
        for index, maker in self.pending:
            self.remote.build(index, *maker()).wait()
        self.pending = []

    def place(self, level):
        return self.torus.axes[self.order[level]][0]

    def step(self):
        getattr(self, "step_%d" % self.next)()
        self.next += 1

    def step_0(self):
        self.send([lambda: (
            self.bufs["grads"].at[self.layer, self.units, span((1 - self.torus.core) * UNIT_HALF, UNIT_HALF)],
            self.bufs["cores"].at[self.layer, self.units], self.torus.sibling)])

    def base(self, level):
        return self.torus.core * UNIT_HALF if level == 0 else 0

    def scatter(self, level, source):
        size = CHUNKS[level]
        slots = self.bufs["slots"][level]

        def maker(step):
            def make():
                peer, device = self.torus.peer(self.order[level], step)
                return (source.at[self.layer, self.units, span(self.base(level) + peer * size, size)],
                        slots.at[step - 1, self.layer, self.units], device)
            return make

        self.send([maker(step) for step in (1, 2, 3)])

    def gathered(self, level, source):
        size = CHUNKS[level]
        slots = self.bufs["slots"][level]
        own = source[self.layer, self.units, span(self.base(level) + self.place(level) * size, size), :]
        return (own + slots[0, self.layer, self.units]) + (
            slots[1, self.layer, self.units] + slots[2, self.layer, self.units])

    def step_1(self):
        self.settle()
        grads, cores = self.bufs["grads"], self.bufs["cores"]
        home = span(self.torus.core * UNIT_HALF, UNIT_HALF)
        grads[self.layer, self.units, home, :] += cores[self.layer, self.units]
        self.scatter(0, grads)

    def step_2(self):
        self.settle()
        partial = self.bufs["partial"]
        partial[self.layer, self.units] = self.gathered(0, self.bufs["grads"])
        self.scatter(1, partial)

    def spread(self, level, chunk):
        def maker(step):
            def make():
                return chunk(), chunk(), self.torus.peer(self.order[level], step)[1]
            return make

        self.send([maker(step) for step in (1, 2, 3)])

    def step_3(self):
        self.settle()
        cross = self.bufs["cross"]
        cross[self.place(2), self.layer, self.units] = self.gathered(1, self.bufs["partial"])
        self.spread(2, lambda: cross.at[self.place(2), self.layer, self.units])

    def step_4(self):
        self.settle()
        cross, ring = self.bufs["cross"], self.bufs["ring"]
        ring[self.layer, self.units, span(self.place(1) * CHUNKS[1], CHUNKS[1]), :] = (
            cross[0, self.layer, self.units] + cross[1, self.layer, self.units]) + (
            cross[2, self.layer, self.units] + cross[3, self.layer, self.units])
        self.spread(1, lambda: ring.at[self.layer, self.units, span(self.place(1) * CHUNKS[1], CHUNKS[1])])

    def rows(self):
        return span(self.torus.core * UNIT_HALF + self.place(0) * CHUNKS[0], CHUNKS[0])

    def last(self, step, across):
        device = dict(self.torus.peer(self.order[0], step)[1]) if step else {}
        if across:
            device.update(self.torus.sibling)
        return self.remote.build(
            self.first_index + step + 4 * across, self.bufs["ring"].at[self.layer, self.units],
            self.bufs["done"].at[self.units, self.rows()], device)

    def step_5(self):
        self.settle()
        self.first_index = self.remote.take(8)

        @pl.when(self.torus.core == self.layer)
        def _():
            for step in (1, 2, 3):
                self.last(step, 0).start()
            self.bufs["done"][self.units, self.rows(), :] = self.bufs["ring"][self.layer, self.units]

        @pl.when(self.torus.core != self.layer)
        def _():
            for step in (1, 2, 3, 0):
                self.last(step, 1).start()

    def copy_out(self):
        return pltpu.make_async_copy(
            self.bufs["done"].at[self.units], self.total_ref.at[self.units], self.done_sem)

    def step_6(self):
        @pl.when(self.torus.core == self.layer)
        def _():
            for step in (1, 2, 3):
                self.last(step, 0).wait()
            for step in (0, 1, 2, 3):
                self.last(step, 1).wait_recv()
            self.copy_out().start()

        @pl.when(self.torus.core != self.layer)
        def _():
            for step in (1, 2, 3, 0):
                self.last(step, 1).wait_send()

    def finish(self):
        @pl.when(self.torus.core == self.layer)
        def _():
            self.copy_out().wait()


def relay_kernel(
    act_ref, cot_ref, len_ref, w_qkv_ref, w_out_ref, w_in_ref, w_back_ref,
    b_qv_ref, b_out_ref, gain_one_ref, shift_one_ref, b_in_ref, b_back_ref, gain_two_ref, shift_two_ref,
    final_ref, grad_ref, total_ref, small_ref,
    x_in, lengths, vecs, p_qkv, p_out, p_in, p_back, cols,
    marks, live, x_now, x_parts, q_all, k_all, v_all, ctx_parts,
    n_one, r_one, slope, inner_parts, n_two, r_two,
    dl_parts, du_parts, do_all, dkv, dqkv, sums,
    grads, cores, slots_0, slots_1, partial, cross, ring, done, small, small_far, small_slots,
    local_sem, out_sem, send_sem, recv_sem,
):
    torus = Torus()
    core, half = torus.core, torus.half
    remote = Sender(send_sem, recv_sem)

    barrier = pltpu.get_barrier_semaphore()
    pl.semaphore_signal(barrier, inc=1, device_id=torus.sibling, device_id_type=MESH)
    for axis in "xyz":
        for _, device in torus.peers(axis):
            pl.semaphore_signal(barrier, inc=1, device_id=device, device_id_type=MESH)
            if axis != "x":
                pl.semaphore_signal(barrier, inc=1, device_id={**device, **torus.sibling}, device_id_type=MESH)

    mine = 2 * core + half
    theirs = 2 * core + 1 - half

    def weight_pairs(layer):
        return (
            (w_qkv_ref.at[0], slope.at[layer, 0:WIDTH, 0:768]),
            (w_out_ref.at[0], slope.at[layer, WIDTH:INNER, 0:WIDTH]),
            (w_in_ref.at[0], slope.at[layer, WIDTH:INNER, WIDTH:768]),
            (w_back_ref.at[0], slope.at[layer, 0:INNER, 768:SLOT]),
        )

    len_own = pltpu.make_async_copy(len_ref, lengths, local_sem.at[0])
    x_own = pltpu.make_async_copy(act_ref.at[mine], x_in.at[0], local_sem.at[1])
    c_owns = [
        pltpu.make_async_copy(cot_ref.at[mine, :, pl.ds(part * 128, 128)], done.at[part, 0:HALF], local_sem.at[9 + part])
        for part in range(2)
    ]
    w_owns = [
        pltpu.make_async_copy(src, dst, local_sem.at[3 + i])
        for i, (src, dst) in enumerate(weight_pairs(core))
    ]
    len_own.start()
    x_own.start()
    for copy in w_owns:
        copy.start()
    vecs[core] = jnp.concatenate([
        b_qv_ref[:, :WIDTH], b_qv_ref[:, WIDTH:], b_out_ref[...], gain_one_ref[...], shift_one_ref[...],
        b_in_ref[:, :WIDTH], b_in_ref[:, WIDTH:], b_back_ref[...], gain_two_ref[...], shift_two_ref[...],
        jnp.zeros((6, WIDTH), F32)], axis=0)

    pl.semaphore_wait(barrier, 16)

    x_sends = [
        remote(act_ref.at[theirs, pl.ds(part * BLOCK, BLOCK)], x_in.at[1, pl.ds(part * BLOCK, BLOCK)], torus.partner)
        for part in range(2)
    ]
    c_sends = [
        remote(cot_ref.at[theirs, :, pl.ds(part * 128, 128)], done.at[2 + part, 0:HALF], torus.partner) for part in range(2)
    ]
    w_sends = [remote(src, dst, torus.sibling) for src, dst in weight_pairs(core)]
    w_sends.append(remote(vecs.at[core], vecs.at[core], torus.sibling))
    for copy in x_sends + w_sends:
        copy.start()
    for copy in c_owns:
        copy.start()

    len_own.wait()
    lane = lax.broadcasted_iota(jnp.int32, (16, SLOT), 1)
    row = lax.broadcasted_iota(jnp.int32, (16, SLOT), 0)
    place = jnp.where(lane < HALF, half * HALF + lane, (1 - half) * HALF + lane - HALF)
    end_0 = lengths[0, 0, mine]
    end_1 = end_0 + lengths[1, 0, mine]
    end_2 = end_1 + lengths[2, 0, mine]
    one = jnp.ones_like(place)
    none = jnp.zeros_like(place)
    cell = (
        jnp.where(place >= end_0, one, none)
        + jnp.where(place >= end_1, one, none)
        + jnp.where(place >= end_2, one, none)
    )
    same = jnp.where(cell == row, 1.0, 0.0)
    marks[...] = same
    live[...] = jnp.where(cell < 3, 1.0, 0.0)[:8]
    key_marks = jnp.where(row < 4, (1.0 - same) * APART, jnp.where(row < 7, 1.0, 0.0)).astype(BF16)
    value_marks = jnp.where(row < 3, 1.0, 0.0).astype(BF16)
    query_marks = same.astype(BF16)
    for layer in range(2):
        for head in range(HEADS):
            q_all[layer, head, 192:208, :] = query_marks
            k_all[layer, head, 192:208, :] = key_marks
            v_all[layer, head, 192:208, :] = value_marks

    def load_weights(layer):
        cols[layer] = jnp.concatenate([vecs[layer].T, jnp.zeros((WIDTH, 128 - SMALL_ROWS), F32)], axis=1)
        p_qkv[layer, 0], p_qkv[layer, 1] = split(slope[layer, 0:WIDTH, 0:768])
        p_out[layer, 0], p_out[layer, 1] = split(slope[layer, WIDTH:INNER, 0:WIDTH])
        p_in[layer, 0], p_in[layer, 1] = split(slope[layer, WIDTH:INNER, WIDTH:768])
        p_back[layer, 0], p_back[layer, 1] = split(slope[layer, 0:INNER, 768:SLOT])

    def col(layer, index):
        return cols[layer, :, index:index + 1]

    def block_at(block):
        return slice(block * BLOCK, (block + 1) * BLOCK)

    def project_block(layer, block):
        at = block_at(block)
        x_high, x_low = split(x_now[:, at])
        x_parts[layer, 0, :, at] = x_high
        x_parts[layer, 1, :, at] = x_low
        queries, key_rows, value_rows = (
            dot3(p_qkv[layer, 0, :, part * WIDTH:(part + 1) * WIDTH], p_qkv[layer, 1, :, part * WIDTH:(part + 1) * WIDTH],
                 x_high, x_low, left_t=True)
            for part in range(3))
        yield
        q_high, q_low = split((queries + col(layer, V_Q)) * QUERY_SCALE)
        k_high, k_low = split(key_rows)
        v_high, v_low = split(value_rows + col(layer, V_V))
        for head in range(HEADS):
            rows = slice(head * HEAD, (head + 1) * HEAD)
            q_all[layer, head, 0:64, at] = q_high[rows]
            q_all[layer, head, 64:128, at] = q_high[rows]
            q_all[layer, head, 128:192, at] = q_low[rows]
            k_all[layer, head, 0:64, at] = k_high[rows]
            k_all[layer, head, 64:128, at] = k_low[rows]
            k_all[layer, head, 128:192, at] = k_high[rows]
            v_all[layer, head, 0:64, at] = v_high[rows]
            v_all[layer, head, 64:128, at] = v_low[rows]
            v_all[layer, head, 128:192, at] = v_high[rows]

    def project(layer, blocks):
        skewed(project_block(layer, block) for block in blocks)

    def attend(layer):
        def two_heads(pair, inside):
            def one_block(index):
                head = pair * 2 + index // BLOCKS
                rows = span(head * HEAD, HEAD)
                at = block_at(index % BLOCKS)
                scores = dot(k_all[layer, head], q_all[layer, head, :, at], left_t=True)
                yield
                top = jnp.max(scores, axis=0, keepdims=True)
                weights = jnp.exp2(scores - top)
                total = jnp.sum(weights, axis=0, keepdims=True)
                high, low = split(weights)
                both = dot(v_all[layer, head, 0:128, :], high)
                context = both[:64] + both[64:] + dot(v_all[layer, head, 0:64, :], low)
                context = context / total
                ctx_parts[layer, 0, rows, at], ctx_parts[layer, 1, rows, at] = split(context)
                log_total = top + jnp.log(total) * LOG2E
                q_all[layer, head, 192:208, at] = feature_tile(marks[:, at], -log_total, 4)

            skewed(one_block(index) for index in range(2 * BLOCKS))
            return inside

        lax.fori_loop(0, HEADS // 2, two_heads, 0)

    def feed_block(layer, block):
        at = block_at(block)
        upper = x_now[:, at] + dot3(
            p_out[layer, 0], p_out[layer, 1], ctx_parts[layer, 0, :, at], ctx_parts[layer, 1, :, at], left_t=True
        ) + col(layer, V_OUT)
        normed, inverse = norm_rows(upper)
        n_one[layer, :, at] = normed
        r_one[layer, :, at] = inverse
        hidden = normed * col(layer, V_GAIN1) + col(layer, V_SHIFT1)
        hid_high, hid_low = split(hidden)
        yield
        in_bias = jnp.concatenate([col(layer, V_IN), col(layer, V_IN + 1)], axis=0)
        pre = dot3(p_in[layer, 0], p_in[layer, 1], hid_high, hid_low, left_t=True) + in_bias
        share = 0.5 + 0.5 * lax.erf(pre * math.sqrt(0.5))
        slope[layer, :, at] = share + pre * (jnp.exp(pre * pre * -0.5) * (1.0 / math.sqrt(2.0 * math.pi)))
        inner_high, inner_low = split(pre * share)
        inner_parts[layer, 0, :, at] = inner_high
        inner_parts[layer, 1, :, at] = inner_low
        yield
        lower = hidden + dot3(p_back[layer, 0], p_back[layer, 1], inner_high, inner_low, left_t=True) + col(layer, V_BACK)
        normed, inverse = norm_rows(lower)
        n_two[layer, :, at] = normed
        r_two[layer, :, at] = inverse
        x_now[:, at] = live[0:1, at] * (normed * col(layer, V_GAIN2) + col(layer, V_SHIFT2))

    def feed_forward(layer):
        skewed(feed_block(layer, block) for block in range(BLOCKS))

    for copy in w_owns:
        copy.wait()
    for copy in w_sends:
        copy.wait()
    load_weights(0)
    x_own.wait()
    x_now[:, :HALF] = x_in[0].T
    project(0, (0, 1))
    load_weights(1)
    for part in range(2):
        x_sends[part].wait()
        if part == 1:
            for copy in c_sends:
                copy.start()
        x_now[:, block_at(2 + part)] = x_in[1, part * BLOCK:(part + 1) * BLOCK].T
        project(0, (2 + part,))
    attend(0)
    feed_forward(0)
    project(1, (0, 1, 2, 3))
    attend(1)
    feed_forward(1)

    x_in[0] = x_now[:, :HALF].T
    x_in[1] = x_now[:, HALF:].T
    y_send = remote(x_in.at[1], final_ref.at[half], torus.partner)
    y_own = pltpu.make_async_copy(x_in.at[0], final_ref.at[half], local_sem.at[7])
    for copy in c_owns + c_sends:
        copy.wait()
    y_send.start()
    y_own.start()
    for part in range(2):
        x_now[part * 128:(part + 1) * 128, :HALF] = done[part, 0:HALF].T
        x_now[part * 128:(part + 1) * 128, HALF:] = done[2 + part, 0:HALF].T

    bufs = {
        "grads": grads, "cores": cores, "slots": (slots_0, slots_1),
        "partial": partial, "cross": cross, "ring": ring, "done": done,
    }

    def unit_sum(number, layer, first, count, order):
        return UnitSum(torus, remote, bufs, total_ref, out_sem.at[number], layer, first, count, order)

    dp_parts = dqkv.at[:, 0:INNER]
    hid_parts = dqkv.at[:, INNER:INNER + WIDTH]

    def add_sum(index, values):
        sums[index] += lane_fold(values)

    def back_block(layer, block):
        at = block_at(block)
        grad = live[0:1, at] * x_now[:, at]
        normed = n_two[layer, :, at]
        add_sum(V_GAIN2, grad * normed)
        add_sum(V_SHIFT2, grad)
        d_lower = norm_back(grad * col(layer, V_GAIN2), normed, r_two[layer, :, at])
        add_sum(V_BACK, d_lower)
        high, low = split(d_lower)
        dl_parts[0, :, at] = high
        dl_parts[1, :, at] = low
        yield
        d_pre = dot3(p_back[layer, 0], p_back[layer, 1], high, low) * slope[layer, :, at]
        add_sum(V_IN, d_pre[:WIDTH])
        add_sum(V_IN + 1, d_pre[WIDTH:])
        high, low = split(d_pre)
        dp_parts[0, :, at] = high
        dp_parts[1, :, at] = low
        yield
        d_hidden = d_lower + dot3(p_in[layer, 0], p_in[layer, 1], high, low)
        normed = n_one[layer, :, at]
        hid_parts[0, :, at], hid_parts[1, :, at] = split(normed * col(layer, V_GAIN1) + col(layer, V_SHIFT1))
        add_sum(V_GAIN1, d_hidden * normed)
        add_sum(V_SHIFT1, d_hidden)
        d_upper = norm_back(d_hidden * col(layer, V_GAIN1), normed, r_one[layer, :, at])
        add_sum(V_OUT, d_upper)
        x_now[:, at] = d_upper
        high, low = split(d_upper)
        du_parts[0, :, at] = high
        du_parts[1, :, at] = low
        yield
        d_context = dot3(p_out[layer, 0], p_out[layer, 1], high, low)
        high, low = split(d_context)
        context = ctx_parts[layer, 0, :, at].astype(F32) + ctx_parts[layer, 1, :, at].astype(F32)
        product = d_context * context
        for head in range(HEADS):
            rows = slice(head * HEAD, (head + 1) * HEAD)
            do_all[head, 0:64, at] = high[rows]
            do_all[head, 64:128, at] = high[rows]
            do_all[head, 128:192, at] = low[rows]
            row_dot = jnp.sum(product[rows], axis=0, keepdims=True)
            do_all[head, 192:208, at] = feature_tile(jnp.zeros((16, BLOCK), F32), -row_dot, 0)

    def finish_back(layer, blocks):
        skewed(back_block(layer, block) for block in blocks)

    def put(layer, unit, first, values):
        rows = values.shape[0]
        for part in range(values.shape[1] // 128):
            begin = first + part * rows
            grads[layer, unit, begin:begin + rows, :] = values[:, part * 128:(part + 1) * 128]

    def finish_grads(layer):
        put(layer, 0, 0, dot3(
            inner_parts[layer, 0], inner_parts[layer, 1], dl_parts[0], dl_parts[1], right_t=True))
        put(layer, 1, 0, dot3(hid_parts[0], hid_parts[1], dp_parts[0], dp_parts[1], right_t=True))
        grad_out = dot3(ctx_parts[layer, 0], ctx_parts[layer, 1], du_parts[0], du_parts[1], right_t=True)
        put(layer, 2, 0, grad_out[:, :128])
        put(layer, 3, 0, grad_out[:, 128:])

    def attend_back(layer, after_head):
        def one_head(head, inside):
            rows = span(head * HEAD, HEAD)
            products, parts = {}, {}

            def scores(block):
                at = block_at(block)
                products[block] = (
                    dot(q_all[layer, head, :, at], k_all[layer, head], left_t=True),
                    dot(do_all[head, :, at], v_all[layer, head], left_t=True),
                )

            def weigh(block):
                exponent, d_probs = products.pop(block)
                probs = jnp.exp2(exponent)
                parts[block] = split(probs) + split(probs * d_probs)

            def multiply(block):
                at = block_at(block)
                p_high, p_low, s_high, s_low = parts.pop(block)
                both = dot(k_all[layer, head, 0:128, :], s_high, right_t=True)
                d_query = (both[:64] + both[64:] + dot(k_all[layer, head, 0:64, :], s_low, right_t=True)) * KEY_SCALE
                sums[V_Q, rows, :] += lane_fold(d_query)
                dqkv[0, rows, at], dqkv[1, rows, at] = split(d_query)
                both = dot(q_all[layer, head, 64:192, at], s_high)
                d_key = both[:64] + both[64:] + dot(q_all[layer, head, 64:128, at], s_low)
                both = dot(do_all[head, 64:192, at], p_high)
                d_value = both[:64] + both[64:] + dot(do_all[head, 64:128, at], p_low)
                if block > 0:
                    d_key = dkv[0:64, :] + d_key
                    d_value = dkv[64:128, :] + d_value
                if block < BLOCKS - 1:
                    dkv[0:64, :] = d_key
                    dkv[64:128, :] = d_value
                    return
                k_rows = span(WIDTH + head * HEAD, HEAD)
                v_rows = span(2 * WIDTH + head * HEAD, HEAD)
                dqkv[0, k_rows, :], dqkv[1, k_rows, :] = split(d_key * LN2)
                dqkv[0, v_rows, :], dqkv[1, v_rows, :] = split(d_value)
                sums[V_V, rows, :] += lane_fold(d_value)

            staged(BLOCKS, scores, weigh, multiply)
            for number, todo in enumerate(after_head):

                @pl.when(head == number)
                def _():
                    todo()

            return inside

        lax.fori_loop(0, HEADS, one_head, 0)

    def project_back(layer):
        for block in range(BLOCKS):
            at = block_at(block)
            total = x_now[:, at]
            for part in range(3):
                rows = slice(part * WIDTH, (part + 1) * WIDTH)
                total = total + dot3(
                    p_qkv[layer, 0, :, rows], p_qkv[layer, 1, :, rows], dqkv[0, rows, at], dqkv[1, rows, at])
            x_now[:, at] = total

    def project_grads(layer, pair):
        for part in range(3):
            rows = slice(part * WIDTH + pair * 128, part * WIDTH + (pair + 1) * 128)
            begin = WIDTH + part * WIDTH
            grads[layer, 2 + pair, begin:begin + WIDTH, :] = dot3(
                x_parts[layer, 0], x_parts[layer, 1], dqkv[0, rows], dqkv[1, rows], right_t=True)

    def sum_lanes(layer):
        lane_small = lax.broadcasted_iota(jnp.int32, (WIDTH, 128), 1)
        packed = jnp.zeros((WIDTH, 128), F32)
        for index in range(10):
            packed = jnp.where(lane_small == index, jnp.sum(sums[index], axis=1, keepdims=True), packed)
        small[layer] = packed.T[:SMALL_ROWS]

    def steps(*sums_of):
        def run():
            for one in sums_of:
                one.step()
        return run

    one_a = unit_sum(0, 1, 0, 2, "zyx")
    one_b = unit_sum(1, 1, 2, 2, "zyx")
    zero_a = unit_sum(2, 0, 0, 2, "yzx")
    zero_b = unit_sum(3, 0, 2, 1, "zyx")
    zero_c = unit_sum(4, 0, 3, 1, "yzx")

    def nothing():
        pass

    sums[...] = jnp.zeros_like(sums)
    finish_back(1, range(BLOCKS))
    finish_grads(1)
    one_a.step()
    attend_back(1, [one_a.step, nothing, one_a.step])
    project_grads(1, 0)
    project_grads(1, 1)
    one_b.step()
    one_a.step()
    project_back(1)
    sum_lanes(1)

    sums[...] = jnp.zeros_like(sums)
    one_b.step()
    finish_back(0, range(BLOCKS))
    one_a.step()
    finish_grads(0)
    zero_a.step()

    def after_second():
        project_grads(0, 0)
        zero_b.step()

    attend_back(0, [
        steps(zero_a, one_b, one_a), after_second, steps(zero_b, zero_a, one_b, one_a), one_b.step,
    ])
    project_grads(0, 1)
    zero_c.step()
    zero_b.step()
    zero_a.step()
    sum_lanes(0)
    small_copy = remote(small.at[1 - core], small_far, torus.sibling)
    small_copy.start()
    project_back(0)
    y_own.wait()
    y_send.wait()
    x_in[1] = x_now[:, HALF:].T
    d_send = remote(x_in.at[1], grad_ref.at[half], torus.partner)
    d_send.start()
    zero_c.step()
    one_b.step()
    x_in[0] = x_now[:, :HALF].T
    d_own = pltpu.make_async_copy(x_in.at[0], grad_ref.at[half], local_sem.at[8])
    d_own.start()
    small_copy.wait()
    small_now = small[core] + small_far[...]
    rounds = ((zero_a, zero_b), (zero_a, zero_b, one_b), (), (zero_b, zero_a), (zero_b,))
    for number, others in enumerate(rounds):
        copies = []
        if number < 3:
            axis = "yzx"[number]
            place = small_slots.at[number, torus.axes[axis][0]]
            place[...] = small_now
            copies = [remote(place, place, device) for _, device in torus.peers(axis)]
            for copy in copies:
                copy.start()
        zero_c.step()
        for one in others:
            one.step()
        for copy in copies:
            copy.wait()
        if number < 3:
            small_now = (small_slots[number, 0] + small_slots[number, 1]) + (
                small_slots[number, 2] + small_slots[number, 3])
    small_ref[...] = small_now
    for one in (one_a, one_b, zero_a, zero_b, zero_c):
        one.finish()
    d_own.wait()
    d_send.wait()
    assert all(one.next == 7 for one in (one_a, one_b, zero_a, zero_b, zero_c))


def relay(*operands):
    anywhere = pl.BlockSpec(memory_space=pl.ANY)
    vmem = pl.BlockSpec(memory_space=pltpu.VMEM)
    shape = jax.ShapeDtypeStruct
    f32 = lambda *dims: pltpu.VMEM(dims, F32)
    bf16 = lambda *dims: pltpu.VMEM(dims, BF16)
    copies = 4 + 5 + 2 + 5 * (1 + 12 + 8) + 1 + 9
    return pl.pallas_call(
        relay_kernel,
        out_shape=(
            shape((2, HALF, WIDTH), F32),
            shape((2, HALF, WIDTH), F32),
            shape((UNITS, UNIT_ROWS, 128), F32),
            shape((SMALL_ROWS, WIDTH), F32),
        ),
        in_specs=[anywhere] * 7 + [vmem] * 8,
        out_specs=(anywhere, anywhere, anywhere, vmem),
        scratch_shapes=[
            f32(2, HALF, WIDTH), pltpu.SMEM((3, 1, 4), jnp.int32),
            f32(2, SMALL_ROWS, WIDTH),
            bf16(2, 2, WIDTH, 3 * WIDTH), bf16(2, 2, WIDTH, WIDTH), bf16(2, 2, WIDTH, INNER), bf16(2, 2, INNER, WIDTH),
            f32(2, WIDTH, 128),
            f32(16, SLOT), f32(8, SLOT), f32(WIDTH, SLOT), bf16(2, 2, WIDTH, SLOT),
            bf16(2, HEADS, DEEP, SLOT), bf16(2, HEADS, DEEP, SLOT), bf16(2, HEADS, DEEP, SLOT),
            bf16(2, 2, WIDTH, SLOT),
            f32(2, WIDTH, SLOT), f32(2, 1, SLOT), f32(2, INNER, SLOT), bf16(2, 2, INNER, SLOT),
            f32(2, WIDTH, SLOT), f32(2, 1, SLOT),
            bf16(2, WIDTH, SLOT), bf16(2, WIDTH, SLOT),
            bf16(HEADS, DEEP, SLOT), f32(2 * HEAD, SLOT), bf16(2, 3 * WIDTH, SLOT), f32(10, WIDTH, 128),
            f32(2, UNITS, UNIT_ROWS, 128), f32(2, UNITS, UNIT_HALF, 128),
            f32(3, 2, UNITS, CHUNKS[0], 128), f32(3, 2, UNITS, CHUNKS[1], 128),
            f32(2, UNITS, CHUNKS[0], 128), f32(4, 2, UNITS, CHUNKS[1], 128),
            f32(2, UNITS, CHUNKS[0], 128), f32(UNITS, UNIT_ROWS, 128),
            f32(2, SMALL_ROWS, WIDTH), f32(SMALL_ROWS, WIDTH), f32(3, 4, SMALL_ROWS, WIDTH),
            pltpu.SemaphoreType.DMA((11,)),
            pltpu.SemaphoreType.DMA((5,)),
            pltpu.SemaphoreType.DMA((copies,)),
            pltpu.SemaphoreType.DMA((copies,)),
        ],
        compiler_params=pltpu.CompilerParams(
            collective_id=0, has_side_effects=True, vmem_limit_bytes=VMEM_BYTES),
        name="relay",
    )(*operands)


def unpack_kernel(
    final_in, grad_in, total_in, small_in,
    final_out, grad_out, w_qkv, b_qv, w_out, b_out, gain_one, shift_one, w_in, b_in, w_back, b_back, gain_two, shift_two,
    final_now, grad_now, total_now, small_now, wide, narrow, in_sem, sem,
):
    pairs = [(small_in, small_now)]
    pairs += [(total_in.at[unit], total_now.at[unit]) for unit in range(UNITS)]
    pairs += [(final_in.at[part], final_now.at[part]) for part in range(2)]
    pairs += [(grad_in.at[part], grad_now.at[part]) for part in range(2)]
    arrivals = [pltpu.make_async_copy(src, dst, in_sem.at[i]) for i, (src, dst) in enumerate(pairs)]
    for copy in arrivals:
        copy.start()
    copies = []

    def send(src, dst):
        copy = pltpu.make_async_copy(src, dst, sem.at[len(copies)])
        copy.start()
        copies.append(copy)

    def block(unit, first, rows):
        return total_now.at[unit, pl.ds(first, rows)]

    def lanes(ref, part):
        return ref.at[0, :, pl.ds(part * 128, 128)]

    arrivals[0].wait()
    for number, (ref, first) in enumerate(((b_qv, V_Q), (b_in, V_IN))):
        wide[number, :, :WIDTH] = small_now[first:first + 1, :]
        wide[number, :, WIDTH:] = small_now[first + 1:first + 2, :]
        send(wide.at[number], ref)
    for number, (ref, first) in enumerate((
        (b_out, V_OUT), (gain_one, V_GAIN1), (shift_one, V_SHIFT1), (b_back, V_BACK), (gain_two, V_GAIN2),
        (shift_two, V_SHIFT2),
    )):
        narrow[number] = small_now[first:first + 1, :]
        send(narrow.at[number], ref)
    arrivals[1].wait()
    for part in range(2):
        send(block(0, 512 * part, 512), lanes(w_back, part))
    arrivals[2].wait()
    for part in range(4):
        send(block(1, 256 * part, 256), lanes(w_in, part))
    for pair in range(2):
        arrivals[3 + pair].wait()
        send(block(2 + pair, 0, 256), lanes(w_out, pair))
        for part in range(3):
            send(block(2 + pair, 256 + 256 * part, 256), lanes(w_qkv, 2 * part + pair))
    for part in range(2):
        arrivals[5 + part].wait()
        send(final_now.at[part], final_out.at[part])
    for part in range(2):
        arrivals[7 + part].wait()
        send(grad_now.at[part], grad_out.at[part])
    for copy in copies:
        copy.wait()


def unpack(final_output, input_grad, total, small):
    anywhere = pl.BlockSpec(memory_space=pl.ANY)
    shapes = [
        (2, HALF, WIDTH), (2, HALF, WIDTH), (1, WIDTH, 3 * WIDTH), (1, 2 * WIDTH), (1, WIDTH, WIDTH), (1, WIDTH),
        (1, WIDTH), (1, WIDTH), (1, WIDTH, INNER), (1, INNER), (1, INNER, WIDTH), (1, WIDTH), (1, WIDTH), (1, WIDTH),
    ]
    return pl.pallas_call(
        unpack_kernel,
        out_shape=tuple(jax.ShapeDtypeStruct(dims, F32) for dims in shapes),
        in_specs=[anywhere] * 4,
        out_specs=tuple(anywhere for dims in shapes),
        scratch_shapes=[
            pltpu.VMEM((2, HALF, WIDTH), F32), pltpu.VMEM((2, HALF, WIDTH), F32), pltpu.VMEM((UNITS, UNIT_ROWS, 128), F32),
            pltpu.VMEM((SMALL_ROWS, WIDTH), F32), pltpu.VMEM((2, 1, INNER), F32), pltpu.VMEM((6, 1, WIDTH), F32),
            pltpu.SemaphoreType.DMA((9,)), pltpu.SemaphoreType.DMA((26,)),
        ],
        compiler_params=pltpu.CompilerParams(vmem_limit_bytes=VMEM_BYTES),
        name="unpack",
    )(final_output, input_grad, total, small)


def body(
    activations, cotangent, cell_lengths, w_qkv, b_qv, w_out, b_out, gain_one, shift_one,
    w_in, b_in, w_back, b_back, gain_two, shift_two,
):
    return unpack(*relay(
        activations, cotangent, jnp.transpose(cell_lengths, (2, 1, 0)), w_qkv, w_out, w_in, w_back,
        b_qv, b_out, gain_one, shift_one, b_in, b_back, gain_two, shift_two))


def solution(mesh):
    rows = P(None, ("dp", "seq"), None)
    matrix = P("pipe", None, None)
    vector = P("pipe", None)
    in_specs = (
        rows, rows, P(None, "dp", None), matrix, vector, matrix, vector, vector, vector,
        matrix, vector, matrix, vector, vector, vector,
    )
    out_rows = P("pipe", ("dp", "seq"), None)
    out_specs = (
        out_rows, out_rows, matrix, vector, matrix, vector, vector, vector,
        matrix, vector, matrix, vector, vector, vector,
    )
    return jax.shard_map(body, mesh=mesh, in_specs=in_specs, out_specs=out_specs, check_vma=False)
```

```python
import math

import jax
import jax.numpy as jnp
from jax import lax
from jax.experimental import pallas as pl
from jax.experimental.pallas import tpu as pltpu
from jax.sharding import PartitionSpec as P

MESH = pl.DeviceIdType.MESH
F32 = jnp.float32
BF16 = jnp.bfloat16

HEADS = 4
HEAD = 64
WIDTH = 256
INNER = 512
HALF = 512
SLOT = 1024
BLOCK = 256
BLOCKS = SLOT // BLOCK
DEEP = 3 * HEAD + 16
EPSILON = 1e-06
APART = -1e30
LOG2E = math.log2(math.e)
LN2 = math.log(2.0)
QUERY_SCALE = LOG2E / math.sqrt(HEAD)
KEY_SCALE = 1.0 / math.sqrt(HEAD)

AT_BACK, AT_IN, AT_OUT, AT_PAIR, PAIR_ROWS, PACKED_ROWS = 0, 1024, 2048, 2560, 768, 4096
SMALL_ROWS = 16
VMEM_BYTES = 64 * 2 ** 20 - 2 ** 18
V_Q, V_V, V_OUT, V_GAIN1, V_SHIFT1, V_IN, V_BACK, V_GAIN2, V_SHIFT2 = 0, 1, 2, 3, 4, 5, 7, 8, 9


def dot(left, right, left_t=False, right_t=False):
    dims = (((0 if left_t else 1,), (1 if right_t else 0,)), ((), ()))
    return lax.dot_general(left, right, dims, preferred_element_type=F32)


def split(values):
    high = values.astype(BF16)
    return high, (values - high.astype(F32)).astype(BF16)


def dot3(left_high, left_low, right_high, right_low, left_t=False, right_t=False):
    return (
        dot(left_high, right_high, left_t, right_t)
        + dot(left_high, right_low, left_t, right_t)
        + dot(left_low, right_high, left_t, right_t)
    )


def skewed(tasks):
    waiting, running = list(tasks), []
    while waiting or running:
        if waiting:
            running.insert(0, waiting.pop(0))
        for task in list(running):
            if next(task, "end") == "end":
                running.remove(task)


def staged(count, first, second, third):
    first(0)
    for index in range(count + 1):
        if index + 1 < count:
            first(index + 1)
        if index > 0:
            third(index - 1)
        if index < count:
            second(index)


def col_mean(values):
    return jnp.mean(values, axis=0, keepdims=True)


def norm_rows(values):
    center = values - col_mean(values)
    spread = col_mean(center * center)
    inverse = lax.rsqrt(spread + EPSILON)
    return center * inverse, inverse


def norm_back(grad, normed, inverse):
    return (grad - col_mean(grad) - normed * col_mean(grad * normed)) * inverse


def feature_tile(base, values, first):
    high = values.astype(BF16).astype(F32)
    rest = values - high
    middle = rest.astype(BF16).astype(F32)
    low = rest - middle
    row = lax.broadcasted_iota(jnp.int32, base.shape, 0)
    tile = jnp.where(row == first, high, base)
    tile = jnp.where(row == first + 1, middle, tile)
    return jnp.where(row == first + 2, low, tile).astype(BF16)


def lane_fold(values):
    folded = values[:, :128]
    for first in range(128, values.shape[1], 128):
        folded = folded + values[:, first:first + 128]
    return folded


class Torus:
    def __init__(self):
        self.core = lax.axis_index("pipe")
        self.half = lax.axis_index("seq")
        dp = lax.axis_index("dp")
        x_high, z, y = dp // 16, (dp // 4) % 4, dp % 4
        self.sibling = {"pipe": 1 - self.core}
        self.partner = {"seq": 1 - self.half}
        self.axes = {
            "x": (x_high * 2 + self.half, lambda i: {"dp": (i // 2) * 16 + dp % 16, "seq": i % 2}),
            "y": (y, lambda i: {"dp": dp - y + i}),
            "z": (z, lambda i: {"dp": x_high * 16 + i * 4 + y}),
        }

        self.near = {
            axis: [((index + step) % 4, where((index + step) % 4)) for step in (1, 2, 3)]
            for axis, (index, where) in self.axes.items()
        }

    def peer(self, axis, step):
        return self.near[axis][step - 1]

    def peers(self, axis):
        return self.near[axis]


class Sender:
    def __init__(self, send_sem, recv_sem):
        self.send_sem, self.recv_sem, self.used = send_sem, recv_sem, 0

    def take(self, count=1):
        self.used += count
        return self.used - count

    def __call__(self, src, dst, device):
        return self.build(self.take(), src, dst, device)

    def build(self, index, src, dst, device):
        return pltpu.make_async_remote_copy(
            src_ref=src, dst_ref=dst, send_sem=self.send_sem.at[index], recv_sem=self.recv_sem.at[index],
            device_id=device, device_id_type=MESH,
        )


def span(first, size):
    return pl.ds(pl.multiple_of(first, size), size)


def rows_at(first, size):
    return pl.ds(pl.multiple_of(first, 8), size)


class RowSum:
    def __init__(self, torus, remote, bufs, total_ref, own_sem, layer, first, count, order):
        self.torus, self.remote, self.bufs = torus, remote, bufs
        self.total_ref, self.own_sem = total_ref, own_sem
        self.layer, self.first, self.order = layer, first, order
        self.half, self.quarter, self.part = count // 2, count // 8, count // 32
        self.pending = []
        self.next = 0

    def send(self, makers):
        self.pending = [(self.remote.take(), maker) for maker in makers]
        for index, maker in self.pending:
            self.remote.build(index, *maker()).start()

    def settle(self):
        for index, maker in self.pending:
            self.remote.build(index, *maker()).wait()
        self.pending = []

    def place(self, level):
        return self.torus.axes[self.order[level]][0]

    def step(self):
        getattr(self, "step_%d" % self.next)()
        self.next += 1

    def half_rows(self, core):
        return rows_at(self.first + core * self.half, self.half)

    def quarter_rows(self, index):
        return rows_at(self.first + self.torus.core * self.half + index * self.quarter, self.quarter)

    def part_rows(self, index):
        return rows_at(self.first // 8 + index * self.part, self.part)

    def quarters(self):
        return pl.ds(self.first // 8, self.quarter)

    def parts(self):
        return pl.ds(self.first // 32, self.part)

    def step_0(self):
        self.send([lambda: (
            self.bufs["grads"].at[self.layer, self.half_rows(1 - self.torus.core)],
            self.bufs["cores"].at[self.layer, pl.ds(self.first // 2, self.half)], self.torus.sibling)])

    def to_peers(self, level, make):
        def maker(step):
            def made():
                peer, device = self.torus.peer(self.order[level], step)
                return (*make(step, peer), device)
            return made

        self.send([maker(step) for step in (1, 2, 3)])

    def step_1(self):
        self.settle()
        grads, cores, slots = self.bufs["grads"], self.bufs["cores"], self.bufs["slots"][0]
        grads[self.layer, self.half_rows(self.torus.core), :] += cores[self.layer, pl.ds(self.first // 2, self.half), :]
        self.to_peers(0, lambda step, peer: (
            grads.at[self.layer, self.quarter_rows(peer)], slots.at[step - 1, self.layer, self.quarters()]))

    def gathered(self, slots, own, rows):
        return (own + slots[0, self.layer, rows, :]) + (slots[1, self.layer, rows, :] + slots[2, self.layer, rows, :])

    def step_2(self):
        self.settle()
        partial, slots = self.bufs["partial"], self.bufs["slots"][1]
        own = self.bufs["grads"][self.layer, self.quarter_rows(self.place(0)), :]
        partial[self.layer, self.quarters(), :] = self.gathered(self.bufs["slots"][0], own, self.quarters())
        self.to_peers(1, lambda step, peer: (
            partial.at[self.layer, self.part_rows(peer)], slots.at[step - 1, self.layer, self.parts()]))

    def step_3(self):
        self.settle()
        cross = self.bufs["cross"]
        own = self.bufs["partial"][self.layer, self.part_rows(self.place(1)), :]
        cross[self.place(2), self.layer, self.parts(), :] = self.gathered(self.bufs["slots"][1], own, self.parts())

        def chunk():
            return cross.at[self.place(2), self.layer, self.parts()]

        self.to_peers(2, lambda step, peer: (chunk(), chunk()))

    def step_4(self):
        self.settle()
        cross, ring = self.bufs["cross"], self.bufs["ring"]
        one, two, three, four = (cross[index, self.layer, self.parts(), :] for index in range(4))
        ring[self.layer, self.part_rows(self.place(1)), :] = (one + two) + (three + four)

        def chunk():
            return ring.at[self.layer, self.part_rows(self.place(1))]

        self.to_peers(1, lambda step, peer: (chunk(), chunk()))

    def last(self, step, across):
        device = dict(self.torus.peer(self.order[0], step)[1]) if step else {}
        if across:
            device.update(self.torus.sibling)
        return self.remote.build(
            self.first_index + step + 4 * across, self.bufs["ring"].at[self.layer, self.quarters()],
            self.total_ref.at[self.quarter_rows(self.place(0))], device)

    def own_copy(self):
        return pltpu.make_async_copy(
            self.bufs["ring"].at[self.layer, self.quarters()], self.total_ref.at[self.quarter_rows(self.place(0))],
            self.own_sem)

    def step_5(self):
        self.settle()
        self.first_index = self.remote.take(8)

        @pl.when(self.torus.core == self.layer)
        def _():
            for step in (1, 2, 3):
                self.last(step, 0).start()
            self.own_copy().start()

        @pl.when(self.torus.core != self.layer)
        def _():
            for step in (1, 2, 3, 0):
                self.last(step, 1).start()

    def step_6(self):
        @pl.when(self.torus.core == self.layer)
        def _():
            for step in (1, 2, 3):
                self.last(step, 0).wait()
            for step in (0, 1, 2, 3):
                self.last(step, 1).wait_recv()
            self.own_copy().wait()

        @pl.when(self.torus.core != self.layer)
        def _():
            for step in (1, 2, 3, 0):
                self.last(step, 1).wait_send()


def relay_kernel(
    act_ref, cot_ref, len_ref, w_qkv_ref, w_out_ref, w_in_ref, w_back_ref,
    b_qv_ref, b_out_ref, gain_one_ref, shift_one_ref, b_in_ref, b_back_ref, gain_two_ref, shift_two_ref,
    final_ref, grad_ref, total_ref, small_ref,
    x_in, lengths, vecs, p_qkv, p_out, p_in, p_back, cols,
    marks, live, x_now, x_parts, q_all, k_all, v_all, ctx_parts,
    n_one, r_one, slope, inner_parts, n_two, r_two,
    dl_parts, du_parts, do_all, dkv, dqkv, sums,
    grads, cores, slots_0, slots_1, partial, cross, ring, small, small_far, small_slots,
    local_sem, out_sem, send_sem, recv_sem,
):
    torus = Torus()
    core, half = torus.core, torus.half
    remote = Sender(send_sem, recv_sem)

    barrier = pltpu.get_barrier_semaphore()
    pl.semaphore_signal(barrier, inc=1, device_id=torus.sibling, device_id_type=MESH)
    for axis in "xyz":
        for _, device in torus.peers(axis):
            pl.semaphore_signal(barrier, inc=1, device_id=device, device_id_type=MESH)
            if axis != "x":
                pl.semaphore_signal(barrier, inc=1, device_id={**device, **torus.sibling}, device_id_type=MESH)

    mine = 2 * core + half
    theirs = 2 * core + 1 - half

    def weight_pairs(layer):
        return (
            (w_qkv_ref.at[0], slope.at[layer, 0:WIDTH, 0:768]),
            (w_out_ref.at[0], slope.at[layer, WIDTH:INNER, 0:WIDTH]),
            (w_in_ref.at[0], slope.at[layer, WIDTH:INNER, WIDTH:768]),
            (w_back_ref.at[0], slope.at[layer, 0:INNER, 768:SLOT]),
        )

    len_own = pltpu.make_async_copy(len_ref, lengths, local_sem.at[0])
    x_own = pltpu.make_async_copy(act_ref.at[mine], x_in.at[0], local_sem.at[1])
    c_owns = [
        pltpu.make_async_copy(cot_ref.at[mine, :, pl.ds(part * 128, 128)], cores.at[0, pl.ds(part * HALF, HALF)], local_sem.at[9 + part])
        for part in range(2)
    ]
    w_owns = [
        pltpu.make_async_copy(src, dst, local_sem.at[3 + i])
        for i, (src, dst) in enumerate(weight_pairs(core))
    ]
    len_own.start()
    x_own.start()
    for copy in w_owns:
        copy.start()
    vecs[core] = jnp.concatenate([
        b_qv_ref[:, :WIDTH], b_qv_ref[:, WIDTH:], b_out_ref[...], gain_one_ref[...], shift_one_ref[...],
        b_in_ref[:, :WIDTH], b_in_ref[:, WIDTH:], b_back_ref[...], gain_two_ref[...], shift_two_ref[...],
        jnp.zeros((6, WIDTH), F32)], axis=0)

    pl.semaphore_wait(barrier, 16)

    x_sends = [
        remote(act_ref.at[theirs, pl.ds(part * BLOCK, BLOCK)], x_in.at[1, pl.ds(part * BLOCK, BLOCK)], torus.partner)
        for part in range(2)
    ]
    c_sends = [
        remote(cot_ref.at[theirs, :, pl.ds(part * 128, 128)], cores.at[0, pl.ds((2 + part) * HALF, HALF)], torus.partner) for part in range(2)
    ]
    w_sends = [remote(src, dst, torus.sibling) for src, dst in weight_pairs(core)]
    w_sends.append(remote(vecs.at[core], vecs.at[core], torus.sibling))
    for copy in x_sends + w_sends:
        copy.start()
    for copy in c_owns:
        copy.start()

    len_own.wait()
    lane = lax.broadcasted_iota(jnp.int32, (16, SLOT), 1)
    row = lax.broadcasted_iota(jnp.int32, (16, SLOT), 0)
    place = jnp.where(lane < HALF, half * HALF + lane, (1 - half) * HALF + lane - HALF)
    end_0 = lengths[0, 0, mine]
    end_1 = end_0 + lengths[1, 0, mine]
    end_2 = end_1 + lengths[2, 0, mine]
    one = jnp.ones_like(place)
    none = jnp.zeros_like(place)
    cell = (
        jnp.where(place >= end_0, one, none)
        + jnp.where(place >= end_1, one, none)
        + jnp.where(place >= end_2, one, none)
    )
    same = jnp.where(cell == row, 1.0, 0.0)
    marks[...] = same
    live[...] = jnp.where(cell < 3, 1.0, 0.0)[:8]
    key_marks = jnp.where(row < 4, (1.0 - same) * APART, jnp.where(row < 7, 1.0, 0.0)).astype(BF16)
    value_marks = jnp.where(row < 3, 1.0, 0.0).astype(BF16)
    query_marks = same.astype(BF16)
    for layer in range(2):
        for head in range(HEADS):
            q_all[layer, head, 192:208, :] = query_marks
            k_all[layer, head, 192:208, :] = key_marks
            v_all[layer, head, 192:208, :] = value_marks

    def load_weights(layer):
        cols[layer] = jnp.concatenate([vecs[layer].T, jnp.zeros((WIDTH, 128 - SMALL_ROWS), F32)], axis=1)
        p_qkv[layer, 0], p_qkv[layer, 1] = split(slope[layer, 0:WIDTH, 0:768])
        p_out[layer, 0], p_out[layer, 1] = split(slope[layer, WIDTH:INNER, 0:WIDTH])
        p_in[layer, 0], p_in[layer, 1] = split(slope[layer, WIDTH:INNER, WIDTH:768])
        p_back[layer, 0], p_back[layer, 1] = split(slope[layer, 0:INNER, 768:SLOT])

    def col(layer, index):
        return cols[layer, :, index:index + 1]

    def block_at(block):
        return slice(block * BLOCK, (block + 1) * BLOCK)

    def project_block(layer, block):
        at = block_at(block)
        x_high, x_low = split(x_now[:, at])
        x_parts[layer, 0, :, at] = x_high
        x_parts[layer, 1, :, at] = x_low
        queries, key_rows, value_rows = (
            dot3(p_qkv[layer, 0, :, part * WIDTH:(part + 1) * WIDTH], p_qkv[layer, 1, :, part * WIDTH:(part + 1) * WIDTH],
                 x_high, x_low, left_t=True)
            for part in range(3))
        yield
        q_high, q_low = split((queries + col(layer, V_Q)) * QUERY_SCALE)
        k_high, k_low = split(key_rows)
        v_high, v_low = split(value_rows + col(layer, V_V))
        for head in range(HEADS):
            rows = slice(head * HEAD, (head + 1) * HEAD)
            q_all[layer, head, 0:64, at] = q_high[rows]
            q_all[layer, head, 64:128, at] = q_high[rows]
            q_all[layer, head, 128:192, at] = q_low[rows]
            k_all[layer, head, 0:64, at] = k_high[rows]
            k_all[layer, head, 64:128, at] = k_low[rows]
            k_all[layer, head, 128:192, at] = k_high[rows]
            v_all[layer, head, 0:64, at] = v_high[rows]
            v_all[layer, head, 64:128, at] = v_low[rows]
            v_all[layer, head, 128:192, at] = v_high[rows]

    def project(layer, blocks):
        skewed(project_block(layer, block) for block in blocks)

    def attend(layer):
        def two_heads(pair, inside):
            def one_block(index):
                head = pair * 2 + index // BLOCKS
                rows = span(head * HEAD, HEAD)
                at = block_at(index % BLOCKS)
                scores = dot(k_all[layer, head], q_all[layer, head, :, at], left_t=True)
                yield
                top = jnp.max(scores, axis=0, keepdims=True)
                weights = jnp.exp2(scores - top)
                total = jnp.sum(weights, axis=0, keepdims=True)
                high, low = split(weights)
                both = dot(v_all[layer, head, 0:128, :], high)
                context = both[:64] + both[64:] + dot(v_all[layer, head, 0:64, :], low)
                context = context / total
                ctx_parts[layer, 0, rows, at], ctx_parts[layer, 1, rows, at] = split(context)
                log_total = top + jnp.log(total) * LOG2E
                q_all[layer, head, 192:208, at] = feature_tile(marks[:, at], -log_total, 4)

            skewed(one_block(index) for index in range(2 * BLOCKS))
            return inside

        lax.fori_loop(0, HEADS // 2, two_heads, 0)

    def feed_block(layer, block):
        at = block_at(block)
        upper = x_now[:, at] + dot3(
            p_out[layer, 0], p_out[layer, 1], ctx_parts[layer, 0, :, at], ctx_parts[layer, 1, :, at], left_t=True
        ) + col(layer, V_OUT)
        normed, inverse = norm_rows(upper)
        n_one[layer, :, at] = normed
        r_one[layer, :, at] = inverse
        hidden = normed * col(layer, V_GAIN1) + col(layer, V_SHIFT1)
        hid_high, hid_low = split(hidden)
        yield
        in_bias = jnp.concatenate([col(layer, V_IN), col(layer, V_IN + 1)], axis=0)
        pre = dot3(p_in[layer, 0], p_in[layer, 1], hid_high, hid_low, left_t=True) + in_bias
        share = 0.5 + 0.5 * lax.erf(pre * math.sqrt(0.5))
        slope[layer, :, at] = share + pre * (jnp.exp(pre * pre * -0.5) * (1.0 / math.sqrt(2.0 * math.pi)))
        inner_high, inner_low = split(pre * share)
        inner_parts[layer, 0, :, at] = inner_high
        inner_parts[layer, 1, :, at] = inner_low
        yield
        lower = hidden + dot3(p_back[layer, 0], p_back[layer, 1], inner_high, inner_low, left_t=True) + col(layer, V_BACK)
        normed, inverse = norm_rows(lower)
        n_two[layer, :, at] = normed
        r_two[layer, :, at] = inverse
        x_now[:, at] = live[0:1, at] * (normed * col(layer, V_GAIN2) + col(layer, V_SHIFT2))

    def feed_forward(layer):
        skewed(feed_block(layer, block) for block in range(BLOCKS))

    for copy in w_owns:
        copy.wait()
    for copy in w_sends:
        copy.wait()
    load_weights(0)
    x_own.wait()
    x_now[:, :HALF] = x_in[0].T
    project(0, (0, 1))
    load_weights(1)
    for part in range(2):
        x_sends[part].wait()
        if part == 1:
            for copy in c_sends:
                copy.start()
        x_now[:, block_at(2 + part)] = x_in[1, part * BLOCK:(part + 1) * BLOCK].T
        project(0, (2 + part,))
    attend(0)
    feed_forward(0)
    project(1, (0, 1, 2, 3))
    attend(1)
    feed_forward(1)

    x_in[0] = x_now[:, :HALF].T
    x_in[1] = x_now[:, HALF:].T
    y_send = remote(x_in.at[1], final_ref.at[half], torus.partner)
    y_own = pltpu.make_async_copy(x_in.at[0], final_ref.at[half], local_sem.at[7])
    for copy in c_owns + c_sends:
        copy.wait()
    y_send.start()
    y_own.start()
    for part in range(2):
        x_now[part * 128:(part + 1) * 128, :HALF] = cores[0, part * HALF:(part + 1) * HALF].T
        x_now[part * 128:(part + 1) * 128, HALF:] = cores[0, (2 + part) * HALF:(3 + part) * HALF].T

    bufs = {
        "grads": grads, "cores": cores, "slots": (slots_0, slots_1),
        "partial": partial, "cross": cross, "ring": ring,
    }

    def row_sum(number, layer, first, count, order):
        return RowSum(torus, remote, bufs, total_ref, out_sem.at[number], layer, first, count, order)

    dp_parts = dqkv.at[:, 0:INNER]
    hid_parts = dqkv.at[:, INNER:INNER + WIDTH]

    def add_sum(index, values):
        sums[index] += lane_fold(values)

    def back_block(layer, block):
        at = block_at(block)
        grad = live[0:1, at] * x_now[:, at]
        normed = n_two[layer, :, at]
        add_sum(V_GAIN2, grad * normed)
        add_sum(V_SHIFT2, grad)
        d_lower = norm_back(grad * col(layer, V_GAIN2), normed, r_two[layer, :, at])
        add_sum(V_BACK, d_lower)
        high, low = split(d_lower)
        dl_parts[0, :, at] = high
        dl_parts[1, :, at] = low
        yield
        d_pre = dot3(p_back[layer, 0], p_back[layer, 1], high, low) * slope[layer, :, at]
        add_sum(V_IN, d_pre[:WIDTH])
        add_sum(V_IN + 1, d_pre[WIDTH:])
        high, low = split(d_pre)
        dp_parts[0, :, at] = high
        dp_parts[1, :, at] = low
        yield
        d_hidden = d_lower + dot3(p_in[layer, 0], p_in[layer, 1], high, low)
        normed = n_one[layer, :, at]
        hid_parts[0, :, at], hid_parts[1, :, at] = split(normed * col(layer, V_GAIN1) + col(layer, V_SHIFT1))
        add_sum(V_GAIN1, d_hidden * normed)
        add_sum(V_SHIFT1, d_hidden)
        d_upper = norm_back(d_hidden * col(layer, V_GAIN1), normed, r_one[layer, :, at])
        add_sum(V_OUT, d_upper)
        x_now[:, at] = d_upper
        high, low = split(d_upper)
        du_parts[0, :, at] = high
        du_parts[1, :, at] = low
        yield
        d_context = dot3(p_out[layer, 0], p_out[layer, 1], high, low)
        high, low = split(d_context)
        context = ctx_parts[layer, 0, :, at].astype(F32) + ctx_parts[layer, 1, :, at].astype(F32)
        product = d_context * context
        for head in range(HEADS):
            rows = slice(head * HEAD, (head + 1) * HEAD)
            do_all[head, 0:64, at] = high[rows]
            do_all[head, 64:128, at] = high[rows]
            do_all[head, 128:192, at] = low[rows]
            row_dot = jnp.sum(product[rows], axis=0, keepdims=True)
            do_all[head, 192:208, at] = feature_tile(jnp.zeros((16, BLOCK), F32), -row_dot, 0)

    def finish_back(layer, blocks):
        skewed(back_block(layer, block) for block in blocks)

    def put(layer, first, values):
        rows = values.shape[0]
        for part in range(values.shape[1] // 128):
            grads[layer, first + part * rows:first + (part + 1) * rows, :] = values[:, part * 128:(part + 1) * 128]

    def finish_grads(layer):
        put(layer, AT_BACK, dot3(
            inner_parts[layer, 0], inner_parts[layer, 1], dl_parts[0], dl_parts[1], right_t=True))
        put(layer, AT_IN, dot3(hid_parts[0], hid_parts[1], dp_parts[0], dp_parts[1], right_t=True))
        put(layer, AT_OUT, dot3(ctx_parts[layer, 0], ctx_parts[layer, 1], du_parts[0], du_parts[1], right_t=True))

    def attend_back(layer, after_head):
        def one_head(head, inside):
            rows = span(head * HEAD, HEAD)
            products, parts = {}, {}

            def scores(block):
                at = block_at(block)
                products[block] = (
                    dot(q_all[layer, head, :, at], k_all[layer, head], left_t=True),
                    dot(do_all[head, :, at], v_all[layer, head], left_t=True),
                )

            def weigh(block):
                exponent, d_probs = products.pop(block)
                probs = jnp.exp2(exponent)
                parts[block] = split(probs) + split(probs * d_probs)

            def multiply(block):
                at = block_at(block)
                p_high, p_low, s_high, s_low = parts.pop(block)
                both = dot(k_all[layer, head, 0:128, :], s_high, right_t=True)
                d_query = (both[:64] + both[64:] + dot(k_all[layer, head, 0:64, :], s_low, right_t=True)) * KEY_SCALE
                sums[V_Q, rows, :] += lane_fold(d_query)
                dqkv[0, rows, at], dqkv[1, rows, at] = split(d_query)
                both = dot(q_all[layer, head, 64:192, at], s_high)
                d_key = both[:64] + both[64:] + dot(q_all[layer, head, 64:128, at], s_low)
                both = dot(do_all[head, 64:192, at], p_high)
                d_value = both[:64] + both[64:] + dot(do_all[head, 64:128, at], p_low)
                if block > 0:
                    d_key = dkv[0:64, :] + d_key
                    d_value = dkv[64:128, :] + d_value
                if block < BLOCKS - 1:
                    dkv[0:64, :] = d_key
                    dkv[64:128, :] = d_value
                    return
                k_rows = span(WIDTH + head * HEAD, HEAD)
                v_rows = span(2 * WIDTH + head * HEAD, HEAD)
                dqkv[0, k_rows, :], dqkv[1, k_rows, :] = split(d_key * LN2)
                dqkv[0, v_rows, :], dqkv[1, v_rows, :] = split(d_value)
                sums[V_V, rows, :] += lane_fold(d_value)

            staged(BLOCKS, scores, weigh, multiply)
            for number, todo in enumerate(after_head):

                @pl.when(head == number)
                def _():
                    todo()

            return inside

        lax.fori_loop(0, HEADS, one_head, 0)

    def project_back(layer):
        for block in range(BLOCKS):
            at = block_at(block)
            total = x_now[:, at]
            for part in range(3):
                rows = slice(part * WIDTH, (part + 1) * WIDTH)
                total = total + dot3(
                    p_qkv[layer, 0, :, rows], p_qkv[layer, 1, :, rows], dqkv[0, rows, at], dqkv[1, rows, at])
            x_now[:, at] = total

    def project_grads(layer, pairs):
        spans = [(part, pair) for part in range(3) for pair in pairs]
        for first in range(0, len(spans), 2 if len(pairs) == 2 else 3):
            group = spans[first:first + (2 if len(pairs) == 2 else 3)]
            rows = [slice(part * WIDTH + pair * 128, part * WIDTH + (pair + 1) * 128) for part, pair in group]
            high, low = (jnp.concatenate([dqkv[i, one] for one in rows], axis=0) for i in range(2))
            block = dot3(x_parts[layer, 0], x_parts[layer, 1], high, low, right_t=True)
            for number, (part, pair) in enumerate(group):
                put(layer, AT_PAIR + pair * PAIR_ROWS + part * WIDTH, block[:, number * 128:(number + 1) * 128])

    def sum_lanes(layer):
        lane_small = lax.broadcasted_iota(jnp.int32, (WIDTH, 128), 1)
        packed = jnp.zeros((WIDTH, 128), F32)
        for index in range(10):
            packed = jnp.where(lane_small == index, jnp.sum(sums[index], axis=1, keepdims=True), packed)
        small[layer] = packed.T[:SMALL_ROWS]

    def steps(*sums_of):
        def run():
            for one in sums_of:
                one.step()
        return run

    one_a = row_sum(0, 1, AT_BACK, 2048, "yzx")
    one_b = row_sum(1, 1, AT_OUT, 2048, "zyx")
    zero_a = row_sum(2, 0, AT_BACK, AT_OUT, "zyx")
    zero_b = row_sum(3, 0, AT_OUT, AT_PAIR - AT_OUT + PAIR_ROWS, "zxy")
    zero_c = row_sum(4, 0, AT_PAIR + PAIR_ROWS, PAIR_ROWS, "xyz")

    def nothing():
        pass

    sums[...] = jnp.zeros_like(sums)
    finish_back(1, range(BLOCKS))
    finish_grads(1)
    one_a.step()
    attend_back(1, [one_a.step, nothing, one_a.step])
    project_grads(1, (0, 1))
    one_b.step()
    one_a.step()
    project_back(1)
    sum_lanes(1)

    sums[...] = jnp.zeros_like(sums)
    one_b.step()
    finish_back(0, range(BLOCKS))
    one_a.step()
    finish_grads(0)
    zero_a.step()

    def after_second():
        project_grads(0, (0,))
        zero_b.step()

    attend_back(0, [
        steps(zero_a, one_b, one_a), after_second, steps(zero_b, zero_a, one_b, one_a), one_b.step,
    ])
    project_grads(0, (1,))
    zero_c.step()
    zero_a.step()
    zero_b.step()
    project_back(0)
    zero_c.step()
    one_b.step()
    sum_lanes(0)
    small_copy = remote(small.at[1 - core], small_far, torus.sibling)
    small_copy.start()
    y_own.wait()
    y_send.wait()
    x_in[1] = x_now[:, HALF:].T
    d_send = remote(x_in.at[1], grad_ref.at[half], torus.partner)
    d_send.start()
    x_in[0] = x_now[:, :HALF].T
    d_own = pltpu.make_async_copy(x_in.at[0], grad_ref.at[half], local_sem.at[8])
    d_own.start()
    rounds = ((zero_a, zero_b), (one_b, zero_a, zero_b), (), (zero_b,), (zero_a, zero_b))
    copies = [small_copy]
    for number, others in enumerate(rounds):
        zero_c.step()
        if number < 4:
            for copy in copies:
                copy.wait()
            if number == 0:
                small_now = small[core] + small_far[...]
            else:
                small_now = (small_slots[number - 1, 0] + small_slots[number - 1, 1]) + (
                    small_slots[number - 1, 2] + small_slots[number - 1, 3])
        if number < 3:
            axis = "yzx"[number]
            place = small_slots.at[number, torus.axes[axis][0]]
            place[...] = small_now
            copies = [remote(place, place, device) for _, device in torus.peers(axis)]
            for copy in copies:
                copy.start()
        for one in others:
            one.step()
    small_ref[...] = small_now
    d_own.wait()
    d_send.wait()
    assert [one.next for one in (one_a, one_b, zero_a, zero_b, zero_c)] == [7, 7, 7, 7, 7]


def relay(*operands):
    anywhere = pl.BlockSpec(memory_space=pl.ANY)
    vmem = pl.BlockSpec(memory_space=pltpu.VMEM)
    shape = jax.ShapeDtypeStruct
    f32 = lambda *dims: pltpu.VMEM(dims, F32)
    bf16 = lambda *dims: pltpu.VMEM(dims, BF16)
    copies = 4 + 5 + 2 + 5 * (1 + 12 + 8) + 1 + 9
    return pl.pallas_call(
        relay_kernel,
        out_shape=(
            shape((2, HALF, WIDTH), F32),
            shape((2, HALF, WIDTH), F32),
            shape((PACKED_ROWS, 128), F32),
            shape((SMALL_ROWS, WIDTH), F32),
        ),
        in_specs=[anywhere] * 7 + [vmem] * 8,
        out_specs=(anywhere, anywhere, anywhere, vmem),
        scratch_shapes=[
            f32(2, HALF, WIDTH), pltpu.SMEM((3, 1, 4), jnp.int32),
            f32(2, SMALL_ROWS, WIDTH),
            bf16(2, 2, WIDTH, 3 * WIDTH), bf16(2, 2, WIDTH, WIDTH), bf16(2, 2, WIDTH, INNER), bf16(2, 2, INNER, WIDTH),
            f32(2, WIDTH, 128),
            f32(16, SLOT), f32(8, SLOT), f32(WIDTH, SLOT), bf16(2, 2, WIDTH, SLOT),
            bf16(2, HEADS, DEEP, SLOT), bf16(2, HEADS, DEEP, SLOT), bf16(2, HEADS, DEEP, SLOT),
            bf16(2, 2, WIDTH, SLOT),
            f32(2, WIDTH, SLOT), f32(2, 1, SLOT), f32(2, INNER, SLOT), bf16(2, 2, INNER, SLOT),
            f32(2, WIDTH, SLOT), f32(2, 1, SLOT),
            bf16(2, WIDTH, SLOT), bf16(2, WIDTH, SLOT),
            bf16(HEADS, DEEP, SLOT), f32(2 * HEAD, SLOT), bf16(2, 3 * WIDTH, SLOT), f32(10, WIDTH, 128),
            f32(2, PACKED_ROWS, 128), f32(2, PACKED_ROWS // 2, 128),
            f32(3, 2, PACKED_ROWS // 8, 128), f32(3, 2, PACKED_ROWS // 32, 128),
            f32(2, PACKED_ROWS // 8, 128), f32(4, 2, PACKED_ROWS // 32, 128), f32(2, PACKED_ROWS // 8, 128),
            f32(2, SMALL_ROWS, WIDTH), f32(SMALL_ROWS, WIDTH), f32(3, 4, SMALL_ROWS, WIDTH),
            pltpu.SemaphoreType.DMA((11,)),
            pltpu.SemaphoreType.DMA((5,)),
            pltpu.SemaphoreType.DMA((copies,)),
            pltpu.SemaphoreType.DMA((copies,)),
        ],
        compiler_params=pltpu.CompilerParams(
            collective_id=0, has_side_effects=True, vmem_limit_bytes=VMEM_BYTES),
        name="relay",
    )(*operands)


def unpack_kernel(
    final_in, grad_in, total_in, small_in,
    final_out, grad_out, w_qkv, b_qv, w_out, b_out, gain_one, shift_one, w_in, b_in, w_back, b_back, gain_two, shift_two,
    final_now, grad_now, total_now, small_now, wide, narrow, in_sem, sem,
):
    pairs = [(small_in, small_now)]
    groups = ((AT_BACK, 1024), (AT_IN, 1024), (AT_OUT, 512), (AT_PAIR, PAIR_ROWS), (AT_PAIR + PAIR_ROWS, PAIR_ROWS))
    pairs += [(total_in.at[pl.ds(*group)], total_now.at[pl.ds(*group)]) for group in groups]
    pairs += [(final_in.at[part], final_now.at[part]) for part in range(2)]
    pairs += [(grad_in.at[part], grad_now.at[part]) for part in range(2)]
    arrivals = [pltpu.make_async_copy(src, dst, in_sem.at[i]) for i, (src, dst) in enumerate(pairs)]
    for copy in arrivals:
        copy.start()
    copies = []

    def send(src, dst):
        copy = pltpu.make_async_copy(src, dst, sem.at[len(copies)])
        copy.start()
        copies.append(copy)

    def block(first, rows):
        return total_now.at[pl.ds(first, rows)]

    def lanes(ref, part):
        return ref.at[0, :, pl.ds(part * 128, 128)]

    arrivals[0].wait()
    for number, (ref, first) in enumerate(((b_qv, V_Q), (b_in, V_IN))):
        wide[number, :, :WIDTH] = small_now[first:first + 1, :]
        wide[number, :, WIDTH:] = small_now[first + 1:first + 2, :]
        send(wide.at[number], ref)
    for number, (ref, first) in enumerate((
        (b_out, V_OUT), (gain_one, V_GAIN1), (shift_one, V_SHIFT1), (b_back, V_BACK), (gain_two, V_GAIN2),
        (shift_two, V_SHIFT2),
    )):
        narrow[number] = small_now[first:first + 1, :]
        send(narrow.at[number], ref)
    arrivals[1].wait()
    for part in range(2):
        send(block(AT_BACK + 512 * part, 512), lanes(w_back, part))
    arrivals[2].wait()
    for part in range(4):
        send(block(AT_IN + 256 * part, 256), lanes(w_in, part))
    arrivals[3].wait()
    for part in range(2):
        send(block(AT_OUT + 256 * part, 256), lanes(w_out, part))
    for pair in range(2):
        arrivals[4 + pair].wait()
        for part in range(3):
            send(block(AT_PAIR + PAIR_ROWS * pair + 256 * part, 256), lanes(w_qkv, 2 * part + pair))
    for part in range(2):
        arrivals[6 + part].wait()
        send(final_now.at[part], final_out.at[part])
    for part in range(2):
        arrivals[8 + part].wait()
        send(grad_now.at[part], grad_out.at[part])
    for copy in copies:
        copy.wait()


def unpack(final_output, input_grad, total, small):
    anywhere = pl.BlockSpec(memory_space=pl.ANY)
    shapes = [
        (2, HALF, WIDTH), (2, HALF, WIDTH), (1, WIDTH, 3 * WIDTH), (1, 2 * WIDTH), (1, WIDTH, WIDTH), (1, WIDTH),
        (1, WIDTH), (1, WIDTH), (1, WIDTH, INNER), (1, INNER), (1, INNER, WIDTH), (1, WIDTH), (1, WIDTH), (1, WIDTH),
    ]
    return pl.pallas_call(
        unpack_kernel,
        out_shape=tuple(jax.ShapeDtypeStruct(dims, F32) for dims in shapes),
        in_specs=[anywhere] * 4,
        out_specs=tuple(anywhere for dims in shapes),
        scratch_shapes=[
            pltpu.VMEM((2, HALF, WIDTH), F32), pltpu.VMEM((2, HALF, WIDTH), F32), pltpu.VMEM((PACKED_ROWS, 128), F32),
            pltpu.VMEM((SMALL_ROWS, WIDTH), F32), pltpu.VMEM((2, 1, INNER), F32), pltpu.VMEM((6, 1, WIDTH), F32),
            pltpu.SemaphoreType.DMA((10,)), pltpu.SemaphoreType.DMA((26,)),
        ],
        compiler_params=pltpu.CompilerParams(vmem_limit_bytes=VMEM_BYTES),
        name="unpack",
    )(final_output, input_grad, total, small)


def body(
    activations, cotangent, cell_lengths, w_qkv, b_qv, w_out, b_out, gain_one, shift_one,
    w_in, b_in, w_back, b_back, gain_two, shift_two,
):
    return unpack(*relay(
        activations, cotangent, jnp.transpose(cell_lengths, (2, 1, 0)), w_qkv, w_out, w_in, w_back,
        b_qv, b_out, gain_one, shift_one, b_in, b_back, gain_two, shift_two))


def solution(mesh):
    rows = P(None, ("dp", "seq"), None)
    matrix = P("pipe", None, None)
    vector = P("pipe", None)
    in_specs = (
        rows, rows, P(None, "dp", None), matrix, vector, matrix, vector, vector, vector,
        matrix, vector, matrix, vector, vector, vector,
    )
    out_rows = P("pipe", ("dp", "seq"), None)
    out_specs = (
        out_rows, out_rows, matrix, vector, matrix, vector, vector, vector,
        matrix, vector, matrix, vector, vector, vector,
    )
    return jax.shard_map(body, mesh=mesh, in_specs=in_specs, out_specs=out_specs, check_vma=False)
```

```python
import math

import jax
import jax.numpy as jnp
from jax import lax
from jax.experimental import pallas as pl
from jax.experimental.pallas import tpu as pltpu
from jax.sharding import PartitionSpec as P

MESH = pl.DeviceIdType.MESH
F32 = jnp.float32
BF16 = jnp.bfloat16

HEADS = 4
HEAD = 64
WIDTH = 256
INNER = 512
HALF = 512
SLOT = 1024
BLOCK = 256
BLOCKS = SLOT // BLOCK
DEEP = 3 * HEAD + 16
EPSILON = 1e-06
APART = -1e30
LOG2E = math.log2(math.e)
LN2 = math.log(2.0)
QUERY_SCALE = LOG2E / math.sqrt(HEAD)
KEY_SCALE = 1.0 / math.sqrt(HEAD)

AT_BACK, AT_IN, AT_OUT, AT_PAIR, PAIR_ROWS, PACKED_ROWS = 0, 1024, 2048, 2560, 768, 4096
SMALL_ROWS = 16
VMEM_BYTES = 64 * 2 ** 20 - 2 ** 18
V_Q, V_V, V_OUT, V_GAIN1, V_SHIFT1, V_IN, V_BACK, V_GAIN2, V_SHIFT2 = 0, 1, 2, 3, 4, 5, 7, 8, 9


def dot(left, right, left_t=False, right_t=False):
    dims = (((0 if left_t else 1,), (1 if right_t else 0,)), ((), ()))
    return lax.dot_general(left, right, dims, preferred_element_type=F32)


def split(values):
    high = values.astype(BF16)
    return high, (values - high.astype(F32)).astype(BF16)


def dot3(left_high, left_low, right_high, right_low, left_t=False, right_t=False):
    return (
        dot(left_high, right_high, left_t, right_t)
        + dot(left_high, right_low, left_t, right_t)
        + dot(left_low, right_high, left_t, right_t)
    )


def skewed(tasks):
    waiting, running = list(tasks), []
    while waiting or running:
        if waiting:
            running.insert(0, waiting.pop(0))
        for task in list(running):
            if next(task, "end") == "end":
                running.remove(task)


def staged(count, first, second, third):
    first(0)
    for index in range(count + 1):
        if index + 1 < count:
            first(index + 1)
        if index > 0:
            third(index - 1)
        if index < count:
            second(index)


def col_mean(values):
    return jnp.mean(values, axis=0, keepdims=True)


def norm_rows(values):
    center = values - col_mean(values)
    spread = col_mean(center * center)
    inverse = lax.rsqrt(spread + EPSILON)
    return center * inverse, inverse


def norm_back(grad, normed, inverse):
    return (grad - col_mean(grad) - normed * col_mean(grad * normed)) * inverse


def feature_tile(base, values, first):
    high = values.astype(BF16).astype(F32)
    rest = values - high
    middle = rest.astype(BF16).astype(F32)
    low = rest - middle
    row = lax.broadcasted_iota(jnp.int32, base.shape, 0)
    tile = jnp.where(row == first, high, base)
    tile = jnp.where(row == first + 1, middle, tile)
    return jnp.where(row == first + 2, low, tile).astype(BF16)


def lane_fold(values):
    folded = values[:, :128]
    for first in range(128, values.shape[1], 128):
        folded = folded + values[:, first:first + 128]
    return folded


class Torus:
    def __init__(self):
        self.core = lax.axis_index("pipe")
        self.half = lax.axis_index("seq")
        dp = lax.axis_index("dp")
        x_high, z, y = dp // 16, (dp // 4) % 4, dp % 4
        self.sibling = {"pipe": 1 - self.core}
        self.partner = {"seq": 1 - self.half}
        self.axes = {
            "x": (x_high * 2 + self.half, lambda i: {"dp": (i // 2) * 16 + dp % 16, "seq": i % 2}),
            "y": (y, lambda i: {"dp": dp - y + i}),
            "z": (z, lambda i: {"dp": x_high * 16 + i * 4 + y}),
        }

        self.near = {
            axis: [((index + step) % 4, where((index + step) % 4)) for step in (1, 2, 3)]
            for axis, (index, where) in self.axes.items()
        }

    def peer(self, axis, step):
        return self.near[axis][step - 1]

    def peers(self, axis):
        return self.near[axis]


class Sender:
    def __init__(self, send_sem, recv_sem):
        self.send_sem, self.recv_sem, self.used = send_sem, recv_sem, 0

    def take(self, count=1):
        self.used += count
        return self.used - count

    def __call__(self, src, dst, device):
        return self.build(self.take(), src, dst, device)

    def build(self, index, src, dst, device):
        return pltpu.make_async_remote_copy(
            src_ref=src, dst_ref=dst, send_sem=self.send_sem.at[index], recv_sem=self.recv_sem.at[index],
            device_id=device, device_id_type=MESH,
        )


def span(first, size):
    return pl.ds(pl.multiple_of(first, size), size)


def rows_at(first, size):
    return pl.ds(pl.multiple_of(first, 8), size)


class RowSum:
    def __init__(self, torus, remote, bufs, total_ref, own_sem, layer, first, count, order):
        self.torus, self.remote, self.bufs = torus, remote, bufs
        self.total_ref, self.own_sem = total_ref, own_sem
        self.layer, self.first, self.order = layer, first, order
        self.half, self.quarter, self.part = count // 2, count // 8, count // 32
        self.pending = []
        self.next = 0

    def send(self, makers):
        self.pending = [(self.remote.take(), maker) for maker in makers]
        for index, maker in self.pending:
            self.remote.build(index, *maker()).start()

    def settle(self):
        for index, maker in self.pending:
            self.remote.build(index, *maker()).wait()
        self.pending = []

    def place(self, level):
        return self.torus.axes[self.order[level]][0]

    def step(self):
        getattr(self, "step_%d" % self.next)()
        self.next += 1

    def half_rows(self, core):
        return rows_at(self.first + core * self.half, self.half)

    def quarter_rows(self, index):
        return rows_at(self.first + self.torus.core * self.half + index * self.quarter, self.quarter)

    def part_rows(self, index):
        return rows_at(self.first // 8 + index * self.part, self.part)

    def quarters(self):
        return pl.ds(self.first // 8, self.quarter)

    def parts(self):
        return pl.ds(self.first // 32, self.part)

    def step_0(self):
        self.send([lambda: (
            self.bufs["grads"].at[self.layer, self.half_rows(1 - self.torus.core)],
            self.bufs["cores"].at[self.layer, pl.ds(self.first // 2, self.half)], self.torus.sibling)])

    def to_peers(self, level, make):
        def maker(step):
            def made():
                peer, device = self.torus.peer(self.order[level], step)
                return (*make(step, peer), device)
            return made

        self.send([maker(step) for step in (1, 2, 3)])

    def step_1(self):
        self.settle()
        grads, cores, slots = self.bufs["grads"], self.bufs["cores"], self.bufs["slots"][0]
        grads[self.layer, self.half_rows(self.torus.core), :] += cores[self.layer, pl.ds(self.first // 2, self.half), :]
        self.to_peers(0, lambda step, peer: (
            grads.at[self.layer, self.quarter_rows(peer)], slots.at[step - 1, self.layer, self.quarters()]))

    def gathered(self, slots, own, rows):
        return (own + slots[0, self.layer, rows, :]) + (slots[1, self.layer, rows, :] + slots[2, self.layer, rows, :])

    def step_2(self):
        self.settle()
        partial, slots = self.bufs["partial"], self.bufs["slots"][1]
        own = self.bufs["grads"][self.layer, self.quarter_rows(self.place(0)), :]
        partial[self.layer, self.quarters(), :] = self.gathered(self.bufs["slots"][0], own, self.quarters())
        self.to_peers(1, lambda step, peer: (
            partial.at[self.layer, self.part_rows(peer)], slots.at[step - 1, self.layer, self.parts()]))

    def step_3(self):
        self.settle()
        cross = self.bufs["cross"]
        own = self.bufs["partial"][self.layer, self.part_rows(self.place(1)), :]
        cross[self.place(2), self.layer, self.parts(), :] = self.gathered(self.bufs["slots"][1], own, self.parts())

        def chunk():
            return cross.at[self.place(2), self.layer, self.parts()]

        self.to_peers(2, lambda step, peer: (chunk(), chunk()))

    def step_4(self):
        self.settle()
        cross, ring = self.bufs["cross"], self.bufs["ring"]
        one, two, three, four = (cross[index, self.layer, self.parts(), :] for index in range(4))
        ring[self.layer, self.part_rows(self.place(1)), :] = (one + two) + (three + four)

        def chunk():
            return ring.at[self.layer, self.part_rows(self.place(1))]

        self.to_peers(1, lambda step, peer: (chunk(), chunk()))

    def last(self, step, across):
        device = dict(self.torus.peer(self.order[0], step)[1]) if step else {}
        if across:
            device.update(self.torus.sibling)
        return self.remote.build(
            self.first_index + step + 4 * across, self.bufs["ring"].at[self.layer, self.quarters()],
            self.total_ref.at[self.quarter_rows(self.place(0))], device)

    def own_copy(self):
        return pltpu.make_async_copy(
            self.bufs["ring"].at[self.layer, self.quarters()], self.total_ref.at[self.quarter_rows(self.place(0))],
            self.own_sem)

    def step_5(self):
        self.settle()
        self.first_index = self.remote.take(8)

        @pl.when(self.torus.core == self.layer)
        def _():
            for step in (1, 2, 3):
                self.last(step, 0).start()
            self.own_copy().start()

        @pl.when(self.torus.core != self.layer)
        def _():
            for step in (1, 2, 3, 0):
                self.last(step, 1).start()

    def step_6(self):
        @pl.when(self.torus.core == self.layer)
        def _():
            for step in (1, 2, 3):
                self.last(step, 0).wait()
            for step in (0, 1, 2, 3):
                self.last(step, 1).wait_recv()
            self.own_copy().wait()

        @pl.when(self.torus.core != self.layer)
        def _():
            for step in (1, 2, 3, 0):
                self.last(step, 1).wait_send()


def relay_kernel(
    act_ref, cot_ref, len_ref, w_qkv_ref, w_out_ref, w_in_ref, w_back_ref,
    b_qv_ref, b_out_ref, gain_one_ref, shift_one_ref, b_in_ref, b_back_ref, gain_two_ref, shift_two_ref,
    final_ref, grad_ref, total_ref, small_ref,
    x_in, lengths, wide, narrow, vecs, p_qkv, p_out, p_in, p_back, cols,
    marks, live, tops, x_now, x_parts, q_all, k_all, v_all, ctx_parts,
    n_one, r_one, slope, inner_parts, n_two, r_two,
    dl_parts, du_parts, do_all, dkv, dqkv, sums,
    grads, cores, slots_0, slots_1, partial, cross, ring, small, small_far, small_slots,
    local_sem, out_sem, send_sem, recv_sem,
):
    torus = Torus()
    core, half = torus.core, torus.half
    remote = Sender(send_sem, recv_sem)

    barrier = pltpu.get_barrier_semaphore()
    pl.semaphore_signal(barrier, inc=1, device_id=torus.sibling, device_id_type=MESH)
    for axis in "xyz":
        for _, device in torus.peers(axis):
            pl.semaphore_signal(barrier, inc=1, device_id=device, device_id_type=MESH)
            if axis != "x":
                pl.semaphore_signal(barrier, inc=1, device_id={**device, **torus.sibling}, device_id_type=MESH)

    mine = 2 * core + half
    theirs = 2 * core + 1 - half

    def weight_pairs(layer):
        return (
            (w_qkv_ref.at[0], slope.at[layer, 0:WIDTH, 0:768]),
            (w_out_ref.at[0], slope.at[layer, WIDTH:INNER, 0:WIDTH]),
            (w_in_ref.at[0], slope.at[layer, WIDTH:INNER, WIDTH:768]),
            (w_back_ref.at[0], slope.at[layer, 0:INNER, 768:SLOT]),
        )

    len_own = pltpu.make_async_copy(len_ref, lengths, local_sem.at[0])
    x_own = pltpu.make_async_copy(act_ref.at[mine], x_in.at[0], local_sem.at[1])
    c_owns = [
        pltpu.make_async_copy(cot_ref.at[mine, :, pl.ds(part * 128, 128)], cores.at[0, pl.ds(part * HALF, HALF)], local_sem.at[9 + part])
        for part in range(2)
    ]
    w_owns = [
        pltpu.make_async_copy(src, dst, local_sem.at[3 + i])
        for i, (src, dst) in enumerate(weight_pairs(core))
    ]
    len_own.start()
    x_own.start()
    for copy in w_owns:
        copy.start()
    v_owns = [
        pltpu.make_async_copy(src, dst, local_sem.at[11 + i])
        for i, (src, dst) in enumerate((
            (b_qv_ref, wide.at[0]), (b_in_ref, wide.at[1]), (b_out_ref, narrow.at[0]), (gain_one_ref, narrow.at[1]),
            (shift_one_ref, narrow.at[2]), (b_back_ref, narrow.at[3]), (gain_two_ref, narrow.at[4]),
            (shift_two_ref, narrow.at[5]),
        ))
    ]
    for copy in v_owns:
        copy.start()
    pl.semaphore_wait(barrier, 16)

    x_sends = [
        remote(act_ref.at[theirs, pl.ds(part * BLOCK, BLOCK)], x_in.at[1, pl.ds(part * BLOCK, BLOCK)], torus.partner)
        for part in range(2)
    ]
    c_sends = [
        remote(cot_ref.at[theirs, :, pl.ds(part * 128, 128)], cores.at[0, pl.ds((2 + part) * HALF, HALF)], torus.partner) for part in range(2)
    ]
    w_sends = [remote(src, dst, torus.sibling) for src, dst in weight_pairs(core)]
    w_sends.append(remote(vecs.at[core], vecs.at[core], torus.sibling))
    for copy in x_sends + w_sends[:-1]:
        copy.start()
    for copy in v_owns:
        copy.wait()
    vecs[core] = jnp.concatenate([
        wide[0, :, :WIDTH], wide[0, :, WIDTH:], narrow[0], narrow[1], narrow[2], wide[1, :, :WIDTH], wide[1, :, WIDTH:],
        narrow[3], narrow[4], narrow[5], jnp.zeros((6, WIDTH), F32)], axis=0)
    w_sends[-1].start()
    for copy in c_owns:
        copy.start()

    len_own.wait()
    lane = lax.broadcasted_iota(jnp.int32, (16, SLOT), 1)
    row = lax.broadcasted_iota(jnp.int32, (16, SLOT), 0)
    place = jnp.where(lane < HALF, half * HALF + lane, (1 - half) * HALF + lane - HALF)
    end_0 = lengths[0, 0, mine]
    end_1 = end_0 + lengths[1, 0, mine]
    end_2 = end_1 + lengths[2, 0, mine]
    one = jnp.ones_like(place)
    none = jnp.zeros_like(place)
    cell = (
        jnp.where(place >= end_0, one, none)
        + jnp.where(place >= end_1, one, none)
        + jnp.where(place >= end_2, one, none)
    )
    same = jnp.where(cell == row, 1.0, 0.0)
    marks[...] = same
    live[...] = jnp.where(cell < 3, 1.0, 0.0)[:8]
    key_marks = jnp.where(row < 4, (1.0 - same) * APART, jnp.where(row < 7, 1.0, 0.0)).astype(BF16)
    value_marks = jnp.where(row < 3, 1.0, 0.0).astype(BF16)
    query_marks = same.astype(BF16)
    for layer in range(2):
        for head in range(HEADS):
            q_all[layer, head, 192:208, :] = query_marks
            k_all[layer, head, 192:208, :] = key_marks
            v_all[layer, head, 192:208, :] = value_marks

    def load_weights(layer):
        cols[layer] = jnp.concatenate([vecs[layer].T, jnp.zeros((WIDTH, 128 - SMALL_ROWS), F32)], axis=1)
        p_qkv[layer, 0], p_qkv[layer, 1] = split(slope[layer, 0:WIDTH, 0:768])
        p_out[layer, 0], p_out[layer, 1] = split(slope[layer, WIDTH:INNER, 0:WIDTH])
        p_in[layer, 0], p_in[layer, 1] = split(slope[layer, WIDTH:INNER, WIDTH:768])
        p_back[layer, 0], p_back[layer, 1] = split(slope[layer, 0:INNER, 768:SLOT])

    def col(layer, index):
        return cols[layer, :, index:index + 1]

    def block_at(block):
        return slice(block * BLOCK, (block + 1) * BLOCK)

    def project_block(layer, block):
        at = block_at(block)
        x_high, x_low = split(x_now[:, at])
        x_parts[layer, 0, :, at] = x_high
        x_parts[layer, 1, :, at] = x_low
        queries, key_rows, value_rows = (
            dot3(p_qkv[layer, 0, :, part * WIDTH:(part + 1) * WIDTH], p_qkv[layer, 1, :, part * WIDTH:(part + 1) * WIDTH],
                 x_high, x_low, left_t=True)
            for part in range(3))
        yield
        q_high, q_low = split((queries + col(layer, V_Q)) * QUERY_SCALE)
        k_high, k_low = split(key_rows)
        v_high, v_low = split(value_rows + col(layer, V_V))
        for head in range(HEADS):
            rows = slice(head * HEAD, (head + 1) * HEAD)
            q_all[layer, head, 0:64, at] = q_high[rows]
            q_all[layer, head, 64:128, at] = q_high[rows]
            q_all[layer, head, 128:192, at] = q_low[rows]
            k_all[layer, head, 0:64, at] = k_high[rows]
            k_all[layer, head, 64:128, at] = k_low[rows]
            k_all[layer, head, 128:192, at] = k_high[rows]
            v_all[layer, head, 0:64, at] = v_high[rows]
            v_all[layer, head, 64:128, at] = v_low[rows]
            v_all[layer, head, 128:192, at] = v_high[rows]

    def project(layer, blocks):
        skewed(project_block(layer, block) for block in blocks)

    def weigh_values(layer, head, at, keys, top_before):
        scores = dot(k_all[layer, head, :, keys], q_all[layer, head, :, at], left_t=True)
        yield
        top = jnp.max(scores, axis=0, keepdims=True)
        if top_before is not None:
            top = jnp.maximum(top, top_before())
        weights = jnp.exp2(scores - top)
        total = jnp.sum(weights, axis=0, keepdims=True)
        high, low = split(weights)
        both = dot(v_all[layer, head, 0:128, keys], high)
        return top, total, both[:64] + both[64:] + dot(v_all[layer, head, 0:64, keys], low)

    own, other, every = slice(0, HALF), slice(HALF, SLOT), slice(0, SLOT)

    def attend_own():
        def one_block(head, block):
            at = block_at(block)
            top, total, mixed = yield from weigh_values(0, head, at, own, None)
            tops[head, 0, :, at] = top
            tops[head, 1, :, at] = total
            n_two[0, head * HEAD:(head + 1) * HEAD, at] = mixed

        skewed(one_block(head, block) for head in range(HEADS) for block in range(2))

    def attend(layer):
        def two_heads(pair, inside):
            def one_block(index):
                head, block = pair * 2 + index // BLOCKS, index % BLOCKS
                rows = span(head * HEAD, HEAD)
                at = block_at(block)
                begun = layer == 0 and block < 2
                top, total, context = yield from weigh_values(
                    layer, head, at, other if begun else every, (lambda: tops[head, 0, :, at]) if begun else None)
                if begun:
                    scale = jnp.exp2(tops[head, 0, :, at] - top)
                    total = total + tops[head, 1, :, at] * scale
                    context = context + n_two[0, rows, at] * scale
                context = context / total
                ctx_parts[layer, 0, rows, at], ctx_parts[layer, 1, rows, at] = split(context)
                log_total = top + jnp.log(total) * LOG2E
                q_all[layer, head, 192:208, at] = feature_tile(marks[:, at], -log_total, 4)

            skewed(one_block(index) for index in range(2 * BLOCKS))
            return inside

        lax.fori_loop(0, HEADS // 2, two_heads, 0)

    def feed_block(layer, block):
        at = block_at(block)
        upper = x_now[:, at] + dot3(
            p_out[layer, 0], p_out[layer, 1], ctx_parts[layer, 0, :, at], ctx_parts[layer, 1, :, at], left_t=True
        ) + col(layer, V_OUT)
        normed, inverse = norm_rows(upper)
        n_one[layer, :, at] = normed
        r_one[layer, :, at] = inverse
        hidden = normed * col(layer, V_GAIN1) + col(layer, V_SHIFT1)
        hid_high, hid_low = split(hidden)
        yield
        in_bias = jnp.concatenate([col(layer, V_IN), col(layer, V_IN + 1)], axis=0)
        pre = dot3(p_in[layer, 0], p_in[layer, 1], hid_high, hid_low, left_t=True) + in_bias
        share = 0.5 + 0.5 * lax.erf(pre * math.sqrt(0.5))
        slope[layer, :, at] = share + pre * (jnp.exp(pre * pre * -0.5) * (1.0 / math.sqrt(2.0 * math.pi)))
        inner_high, inner_low = split(pre * share)
        inner_parts[layer, 0, :, at] = inner_high
        inner_parts[layer, 1, :, at] = inner_low
        yield
        lower = hidden + dot3(p_back[layer, 0], p_back[layer, 1], inner_high, inner_low, left_t=True) + col(layer, V_BACK)
        normed, inverse = norm_rows(lower)
        n_two[layer, :, at] = normed
        r_two[layer, :, at] = inverse
        x_now[:, at] = live[0:1, at] * (normed * col(layer, V_GAIN2) + col(layer, V_SHIFT2))

    def feed_forward(layer):
        skewed(feed_block(layer, block) for block in range(BLOCKS))

    for copy in w_owns:
        copy.wait()
    for copy in w_sends:
        copy.wait()
    load_weights(0)
    x_own.wait()
    x_now[:, :HALF] = x_in[0].T
    project(0, (0, 1))
    attend_own()
    load_weights(1)
    for part in range(2):
        x_sends[part].wait()
        if part == 1:
            for copy in c_sends:
                copy.start()
        x_now[:, block_at(2 + part)] = x_in[1, part * BLOCK:(part + 1) * BLOCK].T
        project(0, (2 + part,))
    attend(0)
    feed_forward(0)
    project(1, (0, 1, 2, 3))
    attend(1)
    feed_forward(1)

    x_in[0] = x_now[:, :HALF].T
    x_in[1] = x_now[:, HALF:].T
    y_send = remote(x_in.at[1], final_ref.at[half], torus.partner)
    y_own = pltpu.make_async_copy(x_in.at[0], final_ref.at[half], local_sem.at[7])
    for copy in c_owns + c_sends:
        copy.wait()
    y_send.start()
    y_own.start()
    for part in range(2):
        x_now[part * 128:(part + 1) * 128, :HALF] = cores[0, part * HALF:(part + 1) * HALF].T
        x_now[part * 128:(part + 1) * 128, HALF:] = cores[0, (2 + part) * HALF:(3 + part) * HALF].T

    bufs = {
        "grads": grads, "cores": cores, "slots": (slots_0, slots_1),
        "partial": partial, "cross": cross, "ring": ring,
    }

    def row_sum(number, layer, first, count, order):
        return RowSum(torus, remote, bufs, total_ref, out_sem.at[number], layer, first, count, order)

    dp_parts = dqkv.at[:, 0:INNER]
    hid_parts = dqkv.at[:, INNER:INNER + WIDTH]

    def add_sum(index, values):
        sums[index] += lane_fold(values)

    def back_block(layer, block):
        at = block_at(block)
        grad = live[0:1, at] * x_now[:, at]
        normed = n_two[layer, :, at]
        add_sum(V_GAIN2, grad * normed)
        add_sum(V_SHIFT2, grad)
        d_lower = norm_back(grad * col(layer, V_GAIN2), normed, r_two[layer, :, at])
        add_sum(V_BACK, d_lower)
        high, low = split(d_lower)
        dl_parts[0, :, at] = high
        dl_parts[1, :, at] = low
        yield
        d_pre = dot3(p_back[layer, 0], p_back[layer, 1], high, low) * slope[layer, :, at]
        add_sum(V_IN, d_pre[:WIDTH])
        add_sum(V_IN + 1, d_pre[WIDTH:])
        high, low = split(d_pre)
        dp_parts[0, :, at] = high
        dp_parts[1, :, at] = low
        yield
        d_hidden = d_lower + dot3(p_in[layer, 0], p_in[layer, 1], high, low)
        normed = n_one[layer, :, at]
        hid_parts[0, :, at], hid_parts[1, :, at] = split(normed * col(layer, V_GAIN1) + col(layer, V_SHIFT1))
        add_sum(V_GAIN1, d_hidden * normed)
        add_sum(V_SHIFT1, d_hidden)
        d_upper = norm_back(d_hidden * col(layer, V_GAIN1), normed, r_one[layer, :, at])
        add_sum(V_OUT, d_upper)
        x_now[:, at] = d_upper
        high, low = split(d_upper)
        du_parts[0, :, at] = high
        du_parts[1, :, at] = low
        yield
        d_context = dot3(p_out[layer, 0], p_out[layer, 1], high, low)
        high, low = split(d_context)
        context = ctx_parts[layer, 0, :, at].astype(F32) + ctx_parts[layer, 1, :, at].astype(F32)
        product = d_context * context
        for head in range(HEADS):
            rows = slice(head * HEAD, (head + 1) * HEAD)
            do_all[head, 0:64, at] = high[rows]
            do_all[head, 64:128, at] = high[rows]
            do_all[head, 128:192, at] = low[rows]
            row_dot = jnp.sum(product[rows], axis=0, keepdims=True)
            do_all[head, 192:208, at] = feature_tile(jnp.zeros((16, BLOCK), F32), -row_dot, 0)

    def finish_back(layer, blocks):
        skewed(back_block(layer, block) for block in blocks)

    def put(layer, first, values):
        rows = values.shape[0]
        for part in range(values.shape[1] // 128):
            grads[layer, first + part * rows:first + (part + 1) * rows, :] = values[:, part * 128:(part + 1) * 128]

    def finish_grads(layer):
        put(layer, AT_BACK, dot3(
            inner_parts[layer, 0], inner_parts[layer, 1], dl_parts[0], dl_parts[1], right_t=True))
        put(layer, AT_IN, dot3(hid_parts[0], hid_parts[1], dp_parts[0], dp_parts[1], right_t=True))
        put(layer, AT_OUT, dot3(ctx_parts[layer, 0], ctx_parts[layer, 1], du_parts[0], du_parts[1], right_t=True))

    def attend_back(layer, after_head):
        def one_head(head, inside):
            rows = span(head * HEAD, HEAD)
            products, parts = {}, {}

            def scores(block):
                at = block_at(block)
                products[block] = (
                    dot(q_all[layer, head, :, at], k_all[layer, head], left_t=True),
                    dot(do_all[head, :, at], v_all[layer, head], left_t=True),
                )

            def weigh(block):
                exponent, d_probs = products.pop(block)
                probs = jnp.exp2(exponent)
                parts[block] = split(probs) + split(probs * d_probs)

            def multiply(block):
                at = block_at(block)
                p_high, p_low, s_high, s_low = parts.pop(block)
                both = dot(k_all[layer, head, 0:128, :], s_high, right_t=True)
                d_query = (both[:64] + both[64:] + dot(k_all[layer, head, 0:64, :], s_low, right_t=True)) * KEY_SCALE
                sums[V_Q, rows, :] += lane_fold(d_query)
                dqkv[0, rows, at], dqkv[1, rows, at] = split(d_query)
                both = dot(q_all[layer, head, 64:192, at], s_high)
                d_key = both[:64] + both[64:] + dot(q_all[layer, head, 64:128, at], s_low)
                both = dot(do_all[head, 64:192, at], p_high)
                d_value = both[:64] + both[64:] + dot(do_all[head, 64:128, at], p_low)
                if block > 0:
                    d_key = dkv[0:64, :] + d_key
                    d_value = dkv[64:128, :] + d_value
                if block < BLOCKS - 1:
                    dkv[0:64, :] = d_key
                    dkv[64:128, :] = d_value
                    return
                k_rows = span(WIDTH + head * HEAD, HEAD)
                v_rows = span(2 * WIDTH + head * HEAD, HEAD)
                dqkv[0, k_rows, :], dqkv[1, k_rows, :] = split(d_key * LN2)
                dqkv[0, v_rows, :], dqkv[1, v_rows, :] = split(d_value)
                sums[V_V, rows, :] += lane_fold(d_value)

            staged(BLOCKS, scores, weigh, multiply)
            for number, todo in enumerate(after_head):

                @pl.when(head == number)
                def _():
                    todo()

            return inside

        lax.fori_loop(0, HEADS, one_head, 0)

    def project_back(layer):
        for block in range(BLOCKS):
            at = block_at(block)
            total = x_now[:, at]
            for part in range(3):
                rows = slice(part * WIDTH, (part + 1) * WIDTH)
                total = total + dot3(
                    p_qkv[layer, 0, :, rows], p_qkv[layer, 1, :, rows], dqkv[0, rows, at], dqkv[1, rows, at])
            x_now[:, at] = total

    def project_grads(layer, pairs):
        spans = [(part, pair) for part in range(3) for pair in pairs]
        for first in range(0, len(spans), 2 if len(pairs) == 2 else 3):
            group = spans[first:first + (2 if len(pairs) == 2 else 3)]
            rows = [slice(part * WIDTH + pair * 128, part * WIDTH + (pair + 1) * 128) for part, pair in group]
            high, low = (jnp.concatenate([dqkv[i, one] for one in rows], axis=0) for i in range(2))
            block = dot3(x_parts[layer, 0], x_parts[layer, 1], high, low, right_t=True)
            for number, (part, pair) in enumerate(group):
                put(layer, AT_PAIR + pair * PAIR_ROWS + part * WIDTH, block[:, number * 128:(number + 1) * 128])

    def sum_lanes(layer):
        lane_small = lax.broadcasted_iota(jnp.int32, (WIDTH, 128), 1)
        packed = jnp.zeros((WIDTH, 128), F32)
        for index in range(10):
            packed = jnp.where(lane_small == index, jnp.sum(sums[index], axis=1, keepdims=True), packed)
        small[layer] = packed.T[:SMALL_ROWS]

    def steps(*sums_of):
        def run():
            for one in sums_of:
                one.step()
        return run

    one_a = row_sum(0, 1, AT_BACK, 2048, "yzx")
    one_b = row_sum(1, 1, AT_OUT, 2048, "zyx")
    zero_a = row_sum(2, 0, AT_BACK, AT_PAIR, "zyx")
    zero_b = row_sum(3, 0, AT_PAIR, PAIR_ROWS, "zxy")
    zero_c = row_sum(4, 0, AT_PAIR + PAIR_ROWS, PAIR_ROWS, "xyz")

    def nothing():
        pass

    sums[...] = jnp.zeros_like(sums)
    finish_back(1, range(BLOCKS))
    finish_grads(1)
    one_a.step()
    attend_back(1, [one_a.step, nothing, one_a.step])
    project_grads(1, (0, 1))
    one_b.step()
    one_a.step()
    project_back(1)
    sum_lanes(1)

    sums[...] = jnp.zeros_like(sums)
    one_b.step()
    finish_back(0, range(BLOCKS))
    one_a.step()
    finish_grads(0)
    zero_a.step()

    def after_second():
        project_grads(0, (0,))
        zero_b.step()
        one_b.step()

    attend_back(0, [
        steps(zero_a, one_b, one_a), after_second, steps(zero_b, zero_a, one_a), one_b.step,
    ])
    project_grads(0, (1,))
    zero_c.step()
    zero_a.step()
    project_back(0)
    zero_c.step()
    zero_b.step()
    one_b.step()
    sum_lanes(0)
    small_copy = remote(small.at[1 - core], small_far, torus.sibling)
    small_copy.start()
    y_own.wait()
    y_send.wait()
    x_in[1] = x_now[:, HALF:].T
    d_send = remote(x_in.at[1], grad_ref.at[half], torus.partner)
    d_send.start()
    x_in[0] = x_now[:, :HALF].T
    d_own = pltpu.make_async_copy(x_in.at[0], grad_ref.at[half], local_sem.at[8])
    d_own.start()
    rounds = ((zero_a, zero_b), (one_b, zero_a, zero_b), (), (zero_b,), (zero_a, zero_b))
    copies = [small_copy]
    for number, others in enumerate(rounds):
        zero_c.step()
        if number < 4:
            for copy in copies:
                copy.wait()
            if number == 0:
                small_now = small[core] + small_far[...]
            else:
                small_now = (small_slots[number - 1, 0] + small_slots[number - 1, 1]) + (
                    small_slots[number - 1, 2] + small_slots[number - 1, 3])
        if number == 3:
            small_far[...] = small_now
            small_out = pltpu.make_async_copy(small_far, small_ref, local_sem.at[19])
            small_out.start()
        if number < 3:
            axis = "yzx"[number]
            place = small_slots.at[number, torus.axes[axis][0]]
            place[...] = small_now
            copies = [remote(place, place, device) for _, device in torus.peers(axis)]
            for copy in copies:
                copy.start()
        for one in others:
            one.step()
    small_out.wait()
    d_own.wait()
    d_send.wait()
    assert [one.next for one in (one_a, one_b, zero_a, zero_b, zero_c)] == [7, 7, 7, 7, 7]


def relay(*operands):
    anywhere = pl.BlockSpec(memory_space=pl.ANY)
    shape = jax.ShapeDtypeStruct
    f32 = lambda *dims: pltpu.VMEM(dims, F32)
    bf16 = lambda *dims: pltpu.VMEM(dims, BF16)
    copies = 4 + 5 + 2 + 5 * (1 + 12 + 8) + 1 + 9
    return pl.pallas_call(
        relay_kernel,
        out_shape=(
            shape((2, HALF, WIDTH), F32),
            shape((2, HALF, WIDTH), F32),
            shape((PACKED_ROWS, 128), F32),
            shape((SMALL_ROWS, WIDTH), F32),
        ),
        in_specs=[anywhere] * 15,
        out_specs=(anywhere,) * 4,
        scratch_shapes=[
            f32(2, HALF, WIDTH), pltpu.SMEM((3, 1, 4), jnp.int32),
            f32(2, 1, INNER), f32(6, 1, WIDTH), f32(2, SMALL_ROWS, WIDTH),
            bf16(2, 2, WIDTH, 3 * WIDTH), bf16(2, 2, WIDTH, WIDTH), bf16(2, 2, WIDTH, INNER), bf16(2, 2, INNER, WIDTH),
            f32(2, WIDTH, 128),
            f32(16, SLOT), f32(8, SLOT), f32(HEADS, 2, 1, HALF), f32(WIDTH, SLOT), bf16(2, 2, WIDTH, SLOT),
            bf16(2, HEADS, DEEP, SLOT), bf16(2, HEADS, DEEP, SLOT), bf16(2, HEADS, DEEP, SLOT),
            bf16(2, 2, WIDTH, SLOT),
            f32(2, WIDTH, SLOT), f32(2, 1, SLOT), f32(2, INNER, SLOT), bf16(2, 2, INNER, SLOT),
            f32(2, WIDTH, SLOT), f32(2, 1, SLOT),
            bf16(2, WIDTH, SLOT), bf16(2, WIDTH, SLOT),
            bf16(HEADS, DEEP, SLOT), f32(2 * HEAD, SLOT), bf16(2, 3 * WIDTH, SLOT), f32(10, WIDTH, 128),
            f32(2, PACKED_ROWS, 128), f32(2, PACKED_ROWS // 2, 128),
            f32(3, 2, PACKED_ROWS // 8, 128), f32(3, 2, PACKED_ROWS // 32, 128),
            f32(2, PACKED_ROWS // 8, 128), f32(4, 2, PACKED_ROWS // 32, 128), f32(2, PACKED_ROWS // 8, 128),
            f32(2, SMALL_ROWS, WIDTH), f32(SMALL_ROWS, WIDTH), f32(3, 4, SMALL_ROWS, WIDTH),
            pltpu.SemaphoreType.DMA((20,)),
            pltpu.SemaphoreType.DMA((5,)),
            pltpu.SemaphoreType.DMA((copies,)),
            pltpu.SemaphoreType.DMA((copies,)),
        ],
        compiler_params=pltpu.CompilerParams(
            collective_id=0, has_side_effects=True, vmem_limit_bytes=VMEM_BYTES),
        name="relay",
    )(*operands)


def unpack_kernel(
    final_in, grad_in, total_in, small_in,
    final_out, grad_out, w_qkv, b_qv, w_out, b_out, gain_one, shift_one, w_in, b_in, w_back, b_back, gain_two, shift_two,
    final_now, grad_now, total_now, small_now, wide, narrow, in_sem, sem,
):
    pairs = [(small_in, small_now)]
    groups = ((AT_BACK, 1024), (AT_IN, 1024), (AT_OUT, 512), (AT_PAIR, PAIR_ROWS), (AT_PAIR + PAIR_ROWS, PAIR_ROWS))
    pairs += [(total_in.at[pl.ds(*group)], total_now.at[pl.ds(*group)]) for group in groups]
    pairs += [(final_in.at[part], final_now.at[part]) for part in range(2)]
    pairs += [(grad_in.at[part], grad_now.at[part]) for part in range(2)]
    arrivals = [pltpu.make_async_copy(src, dst, in_sem.at[i]) for i, (src, dst) in enumerate(pairs)]
    for copy in arrivals:
        copy.start()
    copies = []

    def send(src, dst):
        copy = pltpu.make_async_copy(src, dst, sem.at[len(copies)])
        copy.start()
        copies.append(copy)

    def block(first, rows):
        return total_now.at[pl.ds(first, rows)]

    def lanes(ref, part):
        return ref.at[0, :, pl.ds(part * 128, 128)]

    arrivals[0].wait()
    for number, (ref, first) in enumerate(((b_qv, V_Q), (b_in, V_IN))):
        wide[number, :, :WIDTH] = small_now[first:first + 1, :]
        wide[number, :, WIDTH:] = small_now[first + 1:first + 2, :]
        send(wide.at[number], ref)
    for number, (ref, first) in enumerate((
        (b_out, V_OUT), (gain_one, V_GAIN1), (shift_one, V_SHIFT1), (b_back, V_BACK), (gain_two, V_GAIN2),
        (shift_two, V_SHIFT2),
    )):
        narrow[number] = small_now[first:first + 1, :]
        send(narrow.at[number], ref)
    arrivals[1].wait()
    for part in range(2):
        send(block(AT_BACK + 512 * part, 512), lanes(w_back, part))
    arrivals[2].wait()
    for part in range(4):
        send(block(AT_IN + 256 * part, 256), lanes(w_in, part))
    arrivals[3].wait()
    for part in range(2):
        send(block(AT_OUT + 256 * part, 256), lanes(w_out, part))
    for pair in range(2):
        arrivals[4 + pair].wait()
        for part in range(3):
            send(block(AT_PAIR + PAIR_ROWS * pair + 256 * part, 256), lanes(w_qkv, 2 * part + pair))
    for part in range(2):
        arrivals[6 + part].wait()
        send(final_now.at[part], final_out.at[part])
    for part in range(2):
        arrivals[8 + part].wait()
        send(grad_now.at[part], grad_out.at[part])
    for copy in copies:
        copy.wait()


def unpack(final_output, input_grad, total, small):
    anywhere = pl.BlockSpec(memory_space=pl.ANY)
    shapes = [
        (2, HALF, WIDTH), (2, HALF, WIDTH), (1, WIDTH, 3 * WIDTH), (1, 2 * WIDTH), (1, WIDTH, WIDTH), (1, WIDTH),
        (1, WIDTH), (1, WIDTH), (1, WIDTH, INNER), (1, INNER), (1, INNER, WIDTH), (1, WIDTH), (1, WIDTH), (1, WIDTH),
    ]
    return pl.pallas_call(
        unpack_kernel,
        out_shape=tuple(jax.ShapeDtypeStruct(dims, F32) for dims in shapes),
        in_specs=[anywhere] * 4,
        out_specs=tuple(anywhere for dims in shapes),
        scratch_shapes=[
            pltpu.VMEM((2, HALF, WIDTH), F32), pltpu.VMEM((2, HALF, WIDTH), F32), pltpu.VMEM((PACKED_ROWS, 128), F32),
            pltpu.VMEM((SMALL_ROWS, WIDTH), F32), pltpu.VMEM((2, 1, INNER), F32), pltpu.VMEM((6, 1, WIDTH), F32),
            pltpu.SemaphoreType.DMA((10,)), pltpu.SemaphoreType.DMA((26,)),
        ],
        compiler_params=pltpu.CompilerParams(vmem_limit_bytes=VMEM_BYTES),
        name="unpack",
    )(final_output, input_grad, total, small)


def body(
    activations, cotangent, cell_lengths, w_qkv, b_qv, w_out, b_out, gain_one, shift_one,
    w_in, b_in, w_back, b_back, gain_two, shift_two,
):
    return unpack(*relay(
        activations, cotangent, jnp.transpose(cell_lengths, (2, 1, 0)), w_qkv, w_out, w_in, w_back,
        b_qv, b_out, gain_one, shift_one, b_in, b_back, gain_two, shift_two))


def solution(mesh):
    rows = P(None, ("dp", "seq"), None)
    matrix = P("pipe", None, None)
    vector = P("pipe", None)
    in_specs = (
        rows, rows, P(None, "dp", None), matrix, vector, matrix, vector, vector, vector,
        matrix, vector, matrix, vector, vector, vector,
    )
    out_rows = P("pipe", ("dp", "seq"), None)
    out_specs = (
        out_rows, out_rows, matrix, vector, matrix, vector, vector, vector,
        matrix, vector, matrix, vector, vector, vector,
    )
    return jax.shard_map(body, mesh=mesh, in_specs=in_specs, out_specs=out_specs, check_vma=False)
```

```python
import math

import jax
import jax.numpy as jnp
from jax import lax
from jax.experimental import pallas as pl
from jax.experimental.pallas import tpu as pltpu
from jax.sharding import PartitionSpec as P

MESH = pl.DeviceIdType.MESH
F32 = jnp.float32
BF16 = jnp.bfloat16

HEADS = 4
HEAD = 64
WIDTH = 256
INNER = 512
HALF = 512
SLOT = 1024
BLOCK = 256
BLOCKS = SLOT // BLOCK
DEEP = 3 * HEAD + 16
EPSILON = 1e-06
APART = -1e30
LOG2E = math.log2(math.e)
LN2 = math.log(2.0)
QUERY_SCALE = LOG2E / math.sqrt(HEAD)
KEY_SCALE = 1.0 / math.sqrt(HEAD)

AT_BACK, AT_IN, AT_OUT, AT_PAIR, PAIR_ROWS, PACKED_ROWS = 0, 1024, 2048, 2560, 768, 4096
SMALL_ROWS = 16
VMEM_BYTES = 64 * 2 ** 20 - 2 ** 18
V_Q, V_V, V_OUT, V_GAIN1, V_SHIFT1, V_IN, V_BACK, V_GAIN2, V_SHIFT2 = 0, 1, 2, 3, 4, 5, 7, 8, 9


def dot(left, right, left_t=False, right_t=False):
    dims = (((0 if left_t else 1,), (1 if right_t else 0,)), ((), ()))
    return lax.dot_general(left, right, dims, preferred_element_type=F32)


def split(values):
    high = values.astype(BF16)
    return high, (values - high.astype(F32)).astype(BF16)


def dot3(left_high, left_low, right_high, right_low, left_t=False, right_t=False):
    return (
        dot(left_high, right_high, left_t, right_t)
        + dot(left_high, right_low, left_t, right_t)
        + dot(left_low, right_high, left_t, right_t)
    )


def skewed(tasks):
    waiting, running = list(tasks), []
    while waiting or running:
        if waiting:
            running.insert(0, waiting.pop(0))
        for task in list(running):
            if next(task, "end") == "end":
                running.remove(task)


def staged(count, first, second, third):
    first(0)
    for index in range(count + 1):
        if index + 1 < count:
            first(index + 1)
        if index > 0:
            third(index - 1)
        if index < count:
            second(index)


def col_mean(values):
    return jnp.mean(values, axis=0, keepdims=True)


def norm_rows(values):
    center = values - col_mean(values)
    spread = col_mean(center * center)
    inverse = lax.rsqrt(spread + EPSILON)
    return center * inverse, inverse


def norm_back(grad, normed, inverse):
    return (grad - col_mean(grad) - normed * col_mean(grad * normed)) * inverse


def feature_tile(base, values, first):
    high = values.astype(BF16).astype(F32)
    rest = values - high
    middle = rest.astype(BF16).astype(F32)
    low = rest - middle
    row = lax.broadcasted_iota(jnp.int32, base.shape, 0)
    tile = jnp.where(row == first, high, base)
    tile = jnp.where(row == first + 1, middle, tile)
    return jnp.where(row == first + 2, low, tile).astype(BF16)


def lane_fold(values):
    folded = values[:, :128]
    for first in range(128, values.shape[1], 128):
        folded = folded + values[:, first:first + 128]
    return folded


class Torus:
    def __init__(self):
        self.core = lax.axis_index("pipe")
        self.half = lax.axis_index("seq")
        dp = lax.axis_index("dp")
        x_high, z, y = dp // 16, (dp // 4) % 4, dp % 4
        self.sibling = {"pipe": 1 - self.core}
        self.partner = {"seq": 1 - self.half}
        self.axes = {
            "x": (x_high * 2 + self.half, lambda i: {"dp": (i // 2) * 16 + dp % 16, "seq": i % 2}),
            "y": (y, lambda i: {"dp": dp - y + i}),
            "z": (z, lambda i: {"dp": x_high * 16 + i * 4 + y}),
        }

        self.near = {
            axis: [((index + step) % 4, where((index + step) % 4)) for step in (1, 2, 3)]
            for axis, (index, where) in self.axes.items()
        }

    def peer(self, axis, step):
        return self.near[axis][step - 1]

    def peers(self, axis):
        return self.near[axis]


class Sender:
    def __init__(self, send_sem, recv_sem):
        self.send_sem, self.recv_sem, self.used = send_sem, recv_sem, 0

    def take(self, count=1):
        self.used += count
        return self.used - count

    def __call__(self, src, dst, device):
        return self.build(self.take(), src, dst, device)

    def build(self, index, src, dst, device):
        return pltpu.make_async_remote_copy(
            src_ref=src, dst_ref=dst, send_sem=self.send_sem.at[index], recv_sem=self.recv_sem.at[index],
            device_id=device, device_id_type=MESH,
        )


def span(first, size):
    return pl.ds(pl.multiple_of(first, size), size)


def rows_at(first, size):
    return pl.ds(pl.multiple_of(first, 8), size)


class RowSum:
    def __init__(self, torus, remote, bufs, total_ref, own_sem, layer, first, count, order):
        self.torus, self.remote, self.bufs = torus, remote, bufs
        self.total_ref, self.own_sem = total_ref, own_sem
        self.layer, self.first, self.order = layer, first, order
        self.half, self.quarter, self.part = count // 2, count // 8, count // 32
        self.pending = []
        self.next = 0

    def send(self, makers):
        self.pending = [(self.remote.take(), maker) for maker in makers]
        for index, maker in self.pending:
            self.remote.build(index, *maker()).start()

    def settle(self):
        for index, maker in self.pending:
            self.remote.build(index, *maker()).wait()
        self.pending = []

    def place(self, level):
        return self.torus.axes[self.order[level]][0]

    def step(self):
        getattr(self, "step_%d" % self.next)()
        self.next += 1

    def half_rows(self, core):
        return rows_at(self.first + core * self.half, self.half)

    def quarter_rows(self, index):
        return rows_at(self.first + self.torus.core * self.half + index * self.quarter, self.quarter)

    def part_rows(self, index):
        return rows_at(self.first // 8 + index * self.part, self.part)

    def quarters(self):
        return pl.ds(self.first // 8, self.quarter)

    def parts(self):
        return pl.ds(self.first // 32, self.part)

    def step_0(self):
        self.send([lambda: (
            self.bufs["grads"].at[self.layer, self.half_rows(1 - self.torus.core)],
            self.bufs["cores"].at[self.layer, pl.ds(self.first // 2, self.half)], self.torus.sibling)])

    def to_peers(self, level, make):
        def maker(step):
            def made():
                peer, device = self.torus.peer(self.order[level], step)
                return (*make(step, peer), device)
            return made

        self.send([maker(step) for step in (1, 2, 3)])

    def step_1(self):
        self.settle()
        grads, cores, slots = self.bufs["grads"], self.bufs["cores"], self.bufs["slots"][0]
        grads[self.layer, self.half_rows(self.torus.core), :] += cores[self.layer, pl.ds(self.first // 2, self.half), :]
        self.to_peers(0, lambda step, peer: (
            grads.at[self.layer, self.quarter_rows(peer)], slots.at[step - 1, self.layer, self.quarters()]))

    def gathered(self, slots, own, rows):
        return (own + slots[0, self.layer, rows, :]) + (slots[1, self.layer, rows, :] + slots[2, self.layer, rows, :])

    def step_2(self):
        self.settle()
        partial, slots = self.bufs["partial"], self.bufs["slots"][1]
        own = self.bufs["grads"][self.layer, self.quarter_rows(self.place(0)), :]
        partial[self.layer, self.quarters(), :] = self.gathered(self.bufs["slots"][0], own, self.quarters())
        self.to_peers(1, lambda step, peer: (
            partial.at[self.layer, self.part_rows(peer)], slots.at[step - 1, self.layer, self.parts()]))

    def step_3(self):
        self.settle()
        cross = self.bufs["cross"]
        own = self.bufs["partial"][self.layer, self.part_rows(self.place(1)), :]
        cross[self.place(2), self.layer, self.parts(), :] = self.gathered(self.bufs["slots"][1], own, self.parts())

        def chunk():
            return cross.at[self.place(2), self.layer, self.parts()]

        self.to_peers(2, lambda step, peer: (chunk(), chunk()))

    def step_4(self):
        self.settle()
        cross, ring = self.bufs["cross"], self.bufs["ring"]
        one, two, three, four = (cross[index, self.layer, self.parts(), :] for index in range(4))
        ring[self.layer, self.part_rows(self.place(1)), :] = (one + two) + (three + four)

        def chunk():
            return ring.at[self.layer, self.part_rows(self.place(1))]

        self.to_peers(1, lambda step, peer: (chunk(), chunk()))

    def last(self, step, across):
        device = dict(self.torus.peer(self.order[0], step)[1]) if step else {}
        if across:
            device.update(self.torus.sibling)
        return self.remote.build(
            self.first_index + step + 4 * across, self.bufs["ring"].at[self.layer, self.quarters()],
            self.total_ref.at[self.quarter_rows(self.place(0))], device)

    def own_copy(self):
        return pltpu.make_async_copy(
            self.bufs["ring"].at[self.layer, self.quarters()], self.total_ref.at[self.quarter_rows(self.place(0))],
            self.own_sem)

    def step_5(self):
        self.settle()
        self.first_index = self.remote.take(8)

        @pl.when(self.torus.core == self.layer)
        def _():
            for step in (1, 2, 3):
                self.last(step, 0).start()
            self.own_copy().start()

        @pl.when(self.torus.core != self.layer)
        def _():
            for step in (1, 2, 3, 0):
                self.last(step, 1).start()

    def step_6(self):
        @pl.when(self.torus.core == self.layer)
        def _():
            for step in (1, 2, 3):
                self.last(step, 0).wait()
            for step in (0, 1, 2, 3):
                self.last(step, 1).wait_recv()
            self.own_copy().wait()

        @pl.when(self.torus.core != self.layer)
        def _():
            for step in (1, 2, 3, 0):
                self.last(step, 1).wait_send()


def relay_kernel(
    act_ref, cot_ref, len_ref, w_qkv_ref, w_out_ref, w_in_ref, w_back_ref,
    b_qv_ref, b_out_ref, gain_one_ref, shift_one_ref, b_in_ref, b_back_ref, gain_two_ref, shift_two_ref,
    final_ref, grad_ref, total_ref, small_ref,
    x_in, lengths, wide, narrow, vecs, p_qkv, p_out, p_in, p_back, cols,
    marks, live, tops, x_now, x_parts, q_all, k_all, v_all, ctx_parts,
    n_one, r_one, slope, inner_parts, n_two, r_two,
    dl_parts, du_parts, do_all, dkv, dqkv, sums,
    grads, cores, slots_0, slots_1, partial, cross, ring, small, small_far, small_slots,
    local_sem, out_sem, send_sem, recv_sem,
):
    torus = Torus()
    core, half = torus.core, torus.half
    remote = Sender(send_sem, recv_sem)

    barrier = pltpu.get_barrier_semaphore()
    pl.semaphore_signal(barrier, inc=1, device_id=torus.sibling, device_id_type=MESH)
    for axis in "xyz":
        for _, device in torus.peers(axis):
            pl.semaphore_signal(barrier, inc=1, device_id=device, device_id_type=MESH)
            if axis != "x":
                pl.semaphore_signal(barrier, inc=1, device_id={**device, **torus.sibling}, device_id_type=MESH)

    mine = 2 * core + half
    theirs = 2 * core + 1 - half

    def weight_pairs(layer):
        return (
            (w_qkv_ref.at[0], slope.at[layer, 0:WIDTH, 0:768]),
            (w_out_ref.at[0], slope.at[layer, WIDTH:INNER, 0:WIDTH]),
            (w_in_ref.at[0], slope.at[layer, WIDTH:INNER, WIDTH:768]),
            (w_back_ref.at[0], slope.at[layer, 0:INNER, 768:SLOT]),
        )

    len_own = pltpu.make_async_copy(len_ref, lengths, local_sem.at[0])
    x_own = pltpu.make_async_copy(act_ref.at[mine], x_in.at[0], local_sem.at[1])
    c_owns = [
        pltpu.make_async_copy(cot_ref.at[mine, :, pl.ds(part * 128, 128)], cores.at[0, pl.ds(part * HALF, HALF)], local_sem.at[9 + part])
        for part in range(2)
    ]
    w_owns = [
        pltpu.make_async_copy(src, dst, local_sem.at[3 + i])
        for i, (src, dst) in enumerate(weight_pairs(core))
    ]
    len_own.start()
    x_own.start()
    for copy in w_owns:
        copy.start()
    v_owns = [
        pltpu.make_async_copy(src, dst, local_sem.at[11 + i])
        for i, (src, dst) in enumerate((
            (b_qv_ref, wide.at[0]), (b_in_ref, wide.at[1]), (b_out_ref, narrow.at[0]), (gain_one_ref, narrow.at[1]),
            (shift_one_ref, narrow.at[2]), (b_back_ref, narrow.at[3]), (gain_two_ref, narrow.at[4]),
            (shift_two_ref, narrow.at[5]),
        ))
    ]
    for copy in v_owns:
        copy.start()
    pl.semaphore_wait(barrier, 16)

    x_sends = [
        remote(act_ref.at[theirs, pl.ds(part * BLOCK, BLOCK)], x_in.at[1, pl.ds(part * BLOCK, BLOCK)], torus.partner)
        for part in range(2)
    ]
    c_sends = [
        remote(cot_ref.at[theirs, :, pl.ds(part * 128, 128)], cores.at[0, pl.ds((2 + part) * HALF, HALF)], torus.partner) for part in range(2)
    ]
    w_sends = [remote(src, dst, torus.sibling) for src, dst in weight_pairs(core)]
    w_sends.append(remote(vecs.at[core], vecs.at[core], torus.sibling))
    for copy in x_sends + w_sends[:-1]:
        copy.start()
    for copy in v_owns:
        copy.wait()
    vecs[core] = jnp.concatenate([
        wide[0, :, :WIDTH], wide[0, :, WIDTH:], narrow[0], narrow[1], narrow[2], wide[1, :, :WIDTH], wide[1, :, WIDTH:],
        narrow[3], narrow[4], narrow[5], jnp.zeros((6, WIDTH), F32)], axis=0)
    w_sends[-1].start()
    for copy in c_owns:
        copy.start()

    len_own.wait()
    lane = lax.broadcasted_iota(jnp.int32, (16, SLOT), 1)
    row = lax.broadcasted_iota(jnp.int32, (16, SLOT), 0)
    place = jnp.where(lane < HALF, half * HALF + lane, (1 - half) * HALF + lane - HALF)
    end_0 = lengths[0, 0, mine]
    end_1 = end_0 + lengths[1, 0, mine]
    end_2 = end_1 + lengths[2, 0, mine]
    one = jnp.ones_like(place)
    none = jnp.zeros_like(place)
    cell = (
        jnp.where(place >= end_0, one, none)
        + jnp.where(place >= end_1, one, none)
        + jnp.where(place >= end_2, one, none)
    )
    same = jnp.where(cell == row, 1.0, 0.0)
    marks[...] = same
    live[...] = jnp.where(cell < 3, 1.0, 0.0)[:8]
    key_marks = jnp.where(row < 4, (1.0 - same) * APART, jnp.where(row < 7, 1.0, 0.0)).astype(BF16)
    value_marks = jnp.where(row < 3, 1.0, 0.0).astype(BF16)
    query_marks = same.astype(BF16)
    for layer in range(2):
        for head in range(HEADS):
            q_all[layer, head, 192:208, :] = query_marks
            k_all[layer, head, 192:208, :] = key_marks
            v_all[layer, head, 192:208, :] = value_marks

    def load_weights(layer):
        cols[layer] = jnp.concatenate([vecs[layer].T, jnp.zeros((WIDTH, 128 - SMALL_ROWS), F32)], axis=1)
        p_qkv[layer, 0], p_qkv[layer, 1] = split(slope[layer, 0:WIDTH, 0:768])
        p_out[layer, 0], p_out[layer, 1] = split(slope[layer, WIDTH:INNER, 0:WIDTH])
        p_in[layer, 0], p_in[layer, 1] = split(slope[layer, WIDTH:INNER, WIDTH:768])
        p_back[layer, 0], p_back[layer, 1] = split(slope[layer, 0:INNER, 768:SLOT])

    def col(layer, index):
        return cols[layer, :, index:index + 1]

    def block_at(block):
        return slice(block * BLOCK, (block + 1) * BLOCK)

    def project_block(layer, block):
        at = block_at(block)
        x_high, x_low = split(x_now[:, at])
        x_parts[layer, 0, :, at] = x_high
        x_parts[layer, 1, :, at] = x_low
        queries, key_rows, value_rows = (
            dot3(p_qkv[layer, 0, :, part * WIDTH:(part + 1) * WIDTH], p_qkv[layer, 1, :, part * WIDTH:(part + 1) * WIDTH],
                 x_high, x_low, left_t=True)
            for part in range(3))
        yield
        q_high, q_low = split((queries + col(layer, V_Q)) * QUERY_SCALE)
        k_high, k_low = split(key_rows)
        v_high, v_low = split(value_rows + col(layer, V_V))
        for head in range(HEADS):
            rows = slice(head * HEAD, (head + 1) * HEAD)
            q_all[layer, head, 0:64, at] = q_high[rows]
            q_all[layer, head, 64:128, at] = q_high[rows]
            q_all[layer, head, 128:192, at] = q_low[rows]
            k_all[layer, head, 0:64, at] = k_high[rows]
            k_all[layer, head, 64:128, at] = k_low[rows]
            k_all[layer, head, 128:192, at] = k_high[rows]
            v_all[layer, head, 0:64, at] = v_high[rows]
            v_all[layer, head, 64:128, at] = v_low[rows]
            v_all[layer, head, 128:192, at] = v_high[rows]

    def project(layer, blocks):
        skewed(project_block(layer, block) for block in blocks)

    def weigh_values(layer, head, at, keys, top_before):
        scores = dot(k_all[layer, head, :, keys], q_all[layer, head, :, at], left_t=True)
        yield
        top = jnp.max(scores, axis=0, keepdims=True)
        if top_before is not None:
            top = jnp.maximum(top, top_before())
        weights = jnp.exp2(scores - top)
        total = jnp.sum(weights, axis=0, keepdims=True)
        high, low = split(weights)
        both = dot(v_all[layer, head, 0:128, keys], high)
        return top, total, both[:64] + both[64:] + dot(v_all[layer, head, 0:64, keys], low)

    own, other, every = slice(0, HALF), slice(HALF, SLOT), slice(0, SLOT)

    def attend_own():
        def one_block(head, block):
            at = block_at(block)
            top, total, mixed = yield from weigh_values(0, head, at, own, None)
            tops[head, 0, :, at] = top
            tops[head, 1, :, at] = total
            n_two[0, head * HEAD:(head + 1) * HEAD, at] = mixed

        skewed(one_block(head, block) for head in range(HEADS) for block in range(2))

    def attend(layer):
        def two_heads(pair, inside):
            def one_block(index):
                head, block = pair * 2 + index // BLOCKS, index % BLOCKS
                rows = span(head * HEAD, HEAD)
                at = block_at(block)
                begun = layer == 0 and block < 2
                top, total, context = yield from weigh_values(
                    layer, head, at, other if begun else every, (lambda: tops[head, 0, :, at]) if begun else None)
                if begun:
                    scale = jnp.exp2(tops[head, 0, :, at] - top)
                    total = total + tops[head, 1, :, at] * scale
                    context = context + n_two[0, rows, at] * scale
                context = context / total
                ctx_parts[layer, 0, rows, at], ctx_parts[layer, 1, rows, at] = split(context)
                log_total = top + jnp.log(total) * LOG2E
                q_all[layer, head, 192:208, at] = feature_tile(marks[:, at], -log_total, 4)

            skewed(one_block(index) for index in range(2 * BLOCKS))
            return inside

        lax.fori_loop(0, HEADS // 2, two_heads, 0)

    def feed_block(layer, block):
        at = block_at(block)
        upper = x_now[:, at] + dot3(
            p_out[layer, 0], p_out[layer, 1], ctx_parts[layer, 0, :, at], ctx_parts[layer, 1, :, at], left_t=True
        ) + col(layer, V_OUT)
        normed, inverse = norm_rows(upper)
        n_one[layer, :, at] = normed
        r_one[layer, :, at] = inverse
        hidden = normed * col(layer, V_GAIN1) + col(layer, V_SHIFT1)
        hid_high, hid_low = split(hidden)
        yield
        in_bias = jnp.concatenate([col(layer, V_IN), col(layer, V_IN + 1)], axis=0)
        pre = dot3(p_in[layer, 0], p_in[layer, 1], hid_high, hid_low, left_t=True) + in_bias
        share = 0.5 + 0.5 * lax.erf(pre * math.sqrt(0.5))
        slope[layer, :, at] = share + pre * (jnp.exp(pre * pre * -0.5) * (1.0 / math.sqrt(2.0 * math.pi)))
        inner_high, inner_low = split(pre * share)
        inner_parts[layer, 0, :, at] = inner_high
        inner_parts[layer, 1, :, at] = inner_low
        yield
        lower = hidden + dot3(p_back[layer, 0], p_back[layer, 1], inner_high, inner_low, left_t=True) + col(layer, V_BACK)
        normed, inverse = norm_rows(lower)
        n_two[layer, :, at] = normed
        r_two[layer, :, at] = inverse
        x_now[:, at] = live[0:1, at] * (normed * col(layer, V_GAIN2) + col(layer, V_SHIFT2))

    def feed_forward(layer):
        skewed(feed_block(layer, block) for block in range(BLOCKS))

    for copy in w_owns:
        copy.wait()
    for copy in w_sends:
        copy.wait()
    load_weights(0)
    x_own.wait()
    x_now[:, :HALF] = x_in[0].T
    project(0, (0, 1))
    attend_own()
    load_weights(1)
    for part in range(2):
        x_sends[part].wait()
        if part == 1:
            for copy in c_sends:
                copy.start()
        x_now[:, block_at(2 + part)] = x_in[1, part * BLOCK:(part + 1) * BLOCK].T
        project(0, (2 + part,))
    attend(0)
    feed_forward(0)
    project(1, (0, 1, 2, 3))
    attend(1)
    feed_forward(1)

    x_in[0] = x_now[:, :HALF].T
    x_in[1] = x_now[:, HALF:].T
    y_send = remote(x_in.at[1], final_ref.at[half], torus.partner)
    y_own = pltpu.make_async_copy(x_in.at[0], final_ref.at[half], local_sem.at[7])
    for copy in c_owns + c_sends:
        copy.wait()
    y_send.start()
    y_own.start()
    for part in range(2):
        x_now[part * 128:(part + 1) * 128, :HALF] = cores[0, part * HALF:(part + 1) * HALF].T
        x_now[part * 128:(part + 1) * 128, HALF:] = cores[0, (2 + part) * HALF:(3 + part) * HALF].T

    bufs = {
        "grads": grads, "cores": cores, "slots": (slots_0, slots_1),
        "partial": partial, "cross": cross, "ring": ring,
    }

    def row_sum(number, layer, first, count, order):
        return RowSum(torus, remote, bufs, total_ref, out_sem.at[number], layer, first, count, order)

    dp_parts = dqkv.at[:, 0:INNER]
    hid_parts = dqkv.at[:, INNER:INNER + WIDTH]

    def add_sum(index, values):
        sums[index] += lane_fold(values)

    def back_block(layer, block):
        at = block_at(block)
        grad = live[0:1, at] * x_now[:, at]
        normed = n_two[layer, :, at]
        add_sum(V_GAIN2, grad * normed)
        add_sum(V_SHIFT2, grad)
        d_lower = norm_back(grad * col(layer, V_GAIN2), normed, r_two[layer, :, at])
        add_sum(V_BACK, d_lower)
        high, low = split(d_lower)
        dl_parts[0, :, at] = high
        dl_parts[1, :, at] = low
        yield
        d_pre = dot3(p_back[layer, 0], p_back[layer, 1], high, low) * slope[layer, :, at]
        add_sum(V_IN, d_pre[:WIDTH])
        add_sum(V_IN + 1, d_pre[WIDTH:])
        high, low = split(d_pre)
        dp_parts[0, :, at] = high
        dp_parts[1, :, at] = low
        yield
        d_hidden = d_lower + dot3(p_in[layer, 0], p_in[layer, 1], high, low)
        normed = n_one[layer, :, at]
        hid_parts[0, :, at], hid_parts[1, :, at] = split(normed * col(layer, V_GAIN1) + col(layer, V_SHIFT1))
        add_sum(V_GAIN1, d_hidden * normed)
        add_sum(V_SHIFT1, d_hidden)
        d_upper = norm_back(d_hidden * col(layer, V_GAIN1), normed, r_one[layer, :, at])
        add_sum(V_OUT, d_upper)
        x_now[:, at] = d_upper
        high, low = split(d_upper)
        du_parts[0, :, at] = high
        du_parts[1, :, at] = low
        yield
        d_context = dot3(p_out[layer, 0], p_out[layer, 1], high, low)
        high, low = split(d_context)
        context = ctx_parts[layer, 0, :, at].astype(F32) + ctx_parts[layer, 1, :, at].astype(F32)
        product = d_context * context
        for head in range(HEADS):
            rows = slice(head * HEAD, (head + 1) * HEAD)
            do_all[head, 0:64, at] = high[rows]
            do_all[head, 64:128, at] = high[rows]
            do_all[head, 128:192, at] = low[rows]
            row_dot = jnp.sum(product[rows], axis=0, keepdims=True)
            do_all[head, 192:208, at] = feature_tile(jnp.zeros((16, BLOCK), F32), -row_dot, 0)

    def finish_back(layer, blocks):
        skewed(back_block(layer, block) for block in blocks)

    def put(layer, first, values):
        rows = values.shape[0]
        for part in range(values.shape[1] // 128):
            grads[layer, first + part * rows:first + (part + 1) * rows, :] = values[:, part * 128:(part + 1) * 128]

    def finish_grads(layer):
        put(layer, AT_BACK, dot3(
            inner_parts[layer, 0], inner_parts[layer, 1], dl_parts[0], dl_parts[1], right_t=True))
        put(layer, AT_IN, dot3(hid_parts[0], hid_parts[1], dp_parts[0], dp_parts[1], right_t=True))
        put(layer, AT_OUT, dot3(ctx_parts[layer, 0], ctx_parts[layer, 1], du_parts[0], du_parts[1], right_t=True))

    def attend_back(layer, after_head):
        def one_head(head, inside):
            rows = span(head * HEAD, HEAD)
            products, parts = {}, {}
            key_cols = k_all[layer, head, 0:128, :].T

            def scores(block):
                at = block_at(block)
                products[block] = (
                    dot(q_all[layer, head, :, at], k_all[layer, head], left_t=True),
                    dot(do_all[head, :, at], v_all[layer, head], left_t=True),
                )

            def weigh(block):
                exponent, d_probs = products.pop(block)
                probs = jnp.exp2(exponent)
                parts[block] = split(probs) + split(probs * d_probs)

            def multiply(block):
                at = block_at(block)
                p_high, p_low, s_high, s_low = parts.pop(block)
                both = dot(s_high, key_cols)
                d_query = (both[:, :64] + both[:, 64:] + dot(s_low, key_cols[:, :64])).T * KEY_SCALE
                sums[V_Q, rows, :] += lane_fold(d_query)
                dqkv[0, rows, at], dqkv[1, rows, at] = split(d_query)
                both = dot(q_all[layer, head, 64:192, at], s_high)
                d_key = both[:64] + both[64:] + dot(q_all[layer, head, 64:128, at], s_low)
                both = dot(do_all[head, 64:192, at], p_high)
                d_value = both[:64] + both[64:] + dot(do_all[head, 64:128, at], p_low)
                if block > 0:
                    d_key = dkv[0:64, :] + d_key
                    d_value = dkv[64:128, :] + d_value
                if block < BLOCKS - 1:
                    dkv[0:64, :] = d_key
                    dkv[64:128, :] = d_value
                    return
                k_rows = span(WIDTH + head * HEAD, HEAD)
                v_rows = span(2 * WIDTH + head * HEAD, HEAD)
                dqkv[0, k_rows, :], dqkv[1, k_rows, :] = split(d_key * LN2)
                dqkv[0, v_rows, :], dqkv[1, v_rows, :] = split(d_value)
                sums[V_V, rows, :] += lane_fold(d_value)

            staged(BLOCKS, scores, weigh, multiply)
            for number, todo in enumerate(after_head):

                @pl.when(head == number)
                def _():
                    todo()

            return inside

        lax.fori_loop(0, HEADS, one_head, 0)

    def project_back(layer):
        for block in range(BLOCKS):
            at = block_at(block)
            total = x_now[:, at]
            for part in range(3):
                rows = slice(part * WIDTH, (part + 1) * WIDTH)
                total = total + dot3(
                    p_qkv[layer, 0, :, rows], p_qkv[layer, 1, :, rows], dqkv[0, rows, at], dqkv[1, rows, at])
            x_now[:, at] = total

    def project_grads(layer, pairs):
        spans = [(part, pair) for part in range(3) for pair in pairs]
        for first in range(0, len(spans), 2 if len(pairs) == 2 else 3):
            group = spans[first:first + (2 if len(pairs) == 2 else 3)]
            rows = [slice(part * WIDTH + pair * 128, part * WIDTH + (pair + 1) * 128) for part, pair in group]
            high, low = (jnp.concatenate([dqkv[i, one] for one in rows], axis=0) for i in range(2))
            block = dot3(x_parts[layer, 0], x_parts[layer, 1], high, low, right_t=True)
            for number, (part, pair) in enumerate(group):
                put(layer, AT_PAIR + pair * PAIR_ROWS + part * WIDTH, block[:, number * 128:(number + 1) * 128])

    def sum_lanes(layer):
        lane_small = lax.broadcasted_iota(jnp.int32, (WIDTH, 128), 1)
        packed = jnp.zeros((WIDTH, 128), F32)
        for index in range(10):
            packed = jnp.where(lane_small == index, jnp.sum(sums[index], axis=1, keepdims=True), packed)
        small[layer] = packed.T[:SMALL_ROWS]

    def steps(*sums_of):
        def run():
            for one in sums_of:
                one.step()
        return run

    one_a = row_sum(0, 1, AT_BACK, 2048, "yzx")
    one_b = row_sum(1, 1, AT_OUT, 2048, "zyx")
    zero_a = row_sum(2, 0, AT_BACK, AT_PAIR, "zyx")
    zero_b = row_sum(3, 0, AT_PAIR, PAIR_ROWS, "zxy")
    zero_c = row_sum(4, 0, AT_PAIR + PAIR_ROWS, PAIR_ROWS, "xyz")

    def nothing():
        pass

    sums[...] = jnp.zeros_like(sums)
    finish_back(1, range(BLOCKS))
    finish_grads(1)
    one_a.step()
    attend_back(1, [one_a.step, nothing, one_a.step])
    project_grads(1, (0, 1))
    one_b.step()
    one_a.step()
    project_back(1)
    sum_lanes(1)

    sums[...] = jnp.zeros_like(sums)
    one_b.step()
    finish_back(0, range(BLOCKS))
    one_a.step()
    finish_grads(0)
    zero_a.step()

    def after_second():
        project_grads(0, (0,))
        zero_b.step()
        one_b.step()

    attend_back(0, [
        steps(zero_a, one_b, one_a), after_second, steps(zero_b, zero_a, one_a), one_b.step,
    ])
    project_grads(0, (1,))
    zero_c.step()
    zero_a.step()
    project_back(0)
    zero_c.step()
    zero_b.step()
    one_b.step()
    sum_lanes(0)
    small_copy = remote(small.at[1 - core], small_far, torus.sibling)
    small_copy.start()
    y_own.wait()
    y_send.wait()
    x_in[1] = x_now[:, HALF:].T
    d_send = remote(x_in.at[1], grad_ref.at[half], torus.partner)
    d_send.start()
    x_in[0] = x_now[:, :HALF].T
    d_own = pltpu.make_async_copy(x_in.at[0], grad_ref.at[half], local_sem.at[8])
    d_own.start()
    rounds = ((zero_a, zero_b), (one_b, zero_a, zero_b), (), (zero_b,), (zero_a, zero_b))
    copies = [small_copy]
    for number, others in enumerate(rounds):
        zero_c.step()
        if number < 4:
            for copy in copies:
                copy.wait()
            if number == 0:
                small_now = small[core] + small_far[...]
            else:
                small_now = (small_slots[number - 1, 0] + small_slots[number - 1, 1]) + (
                    small_slots[number - 1, 2] + small_slots[number - 1, 3])
        if number == 3:
            small_far[...] = small_now
            small_out = pltpu.make_async_copy(small_far, small_ref, local_sem.at[19])
            small_out.start()
        if number < 3:
            axis = "yzx"[number]
            place = small_slots.at[number, torus.axes[axis][0]]
            place[...] = small_now
            copies = [remote(place, place, device) for _, device in torus.peers(axis)]
            for copy in copies:
                copy.start()
        for one in others:
            one.step()
    small_out.wait()
    d_own.wait()
    d_send.wait()
    assert [one.next for one in (one_a, one_b, zero_a, zero_b, zero_c)] == [7, 7, 7, 7, 7]


def relay(*operands):
    anywhere = pl.BlockSpec(memory_space=pl.ANY)
    shape = jax.ShapeDtypeStruct
    f32 = lambda *dims: pltpu.VMEM(dims, F32)
    bf16 = lambda *dims: pltpu.VMEM(dims, BF16)
    copies = 4 + 5 + 2 + 5 * (1 + 12 + 8) + 1 + 9
    return pl.pallas_call(
        relay_kernel,
        out_shape=(
            shape((2, HALF, WIDTH), F32),
            shape((2, HALF, WIDTH), F32),
            shape((PACKED_ROWS, 128), F32),
            shape((SMALL_ROWS, WIDTH), F32),
        ),
        in_specs=[anywhere] * 15,
        out_specs=(anywhere,) * 4,
        scratch_shapes=[
            f32(2, HALF, WIDTH), pltpu.SMEM((3, 1, 4), jnp.int32),
            f32(2, 1, INNER), f32(6, 1, WIDTH), f32(2, SMALL_ROWS, WIDTH),
            bf16(2, 2, WIDTH, 3 * WIDTH), bf16(2, 2, WIDTH, WIDTH), bf16(2, 2, WIDTH, INNER), bf16(2, 2, INNER, WIDTH),
            f32(2, WIDTH, 128),
            f32(16, SLOT), f32(8, SLOT), f32(HEADS, 2, 1, HALF), f32(WIDTH, SLOT), bf16(2, 2, WIDTH, SLOT),
            bf16(2, HEADS, DEEP, SLOT), bf16(2, HEADS, DEEP, SLOT), bf16(2, HEADS, DEEP, SLOT),
            bf16(2, 2, WIDTH, SLOT),
            f32(2, WIDTH, SLOT), f32(2, 1, SLOT), f32(2, INNER, SLOT), bf16(2, 2, INNER, SLOT),
            f32(2, WIDTH, SLOT), f32(2, 1, SLOT),
            bf16(2, WIDTH, SLOT), bf16(2, WIDTH, SLOT),
            bf16(HEADS, DEEP, SLOT), f32(2 * HEAD, SLOT), bf16(2, 3 * WIDTH, SLOT), f32(10, WIDTH, 128),
            f32(2, PACKED_ROWS, 128), f32(2, PACKED_ROWS // 2, 128),
            f32(3, 2, PACKED_ROWS // 8, 128), f32(3, 2, PACKED_ROWS // 32, 128),
            f32(2, PACKED_ROWS // 8, 128), f32(4, 2, PACKED_ROWS // 32, 128), f32(2, PACKED_ROWS // 8, 128),
            f32(2, SMALL_ROWS, WIDTH), f32(SMALL_ROWS, WIDTH), f32(3, 4, SMALL_ROWS, WIDTH),
            pltpu.SemaphoreType.DMA((20,)),
            pltpu.SemaphoreType.DMA((5,)),
            pltpu.SemaphoreType.DMA((copies,)),
            pltpu.SemaphoreType.DMA((copies,)),
        ],
        compiler_params=pltpu.CompilerParams(
            collective_id=0, has_side_effects=True, vmem_limit_bytes=VMEM_BYTES),
        name="relay",
    )(*operands)


def unpack_kernel(
    final_in, grad_in, total_in, small_in,
    final_out, grad_out, w_qkv, b_qv, w_out, b_out, gain_one, shift_one, w_in, b_in, w_back, b_back, gain_two, shift_two,
    final_now, grad_now, total_now, small_now, wide, narrow, in_sem, sem,
):
    pairs = [(small_in, small_now)]
    groups = ((AT_BACK, 1024), (AT_IN, 1024), (AT_OUT, 512), (AT_PAIR, PAIR_ROWS), (AT_PAIR + PAIR_ROWS, PAIR_ROWS))
    pairs += [(total_in.at[pl.ds(*group)], total_now.at[pl.ds(*group)]) for group in groups]
    pairs += [(final_in.at[part], final_now.at[part]) for part in range(2)]
    pairs += [(grad_in.at[part], grad_now.at[part]) for part in range(2)]
    arrivals = [pltpu.make_async_copy(src, dst, in_sem.at[i]) for i, (src, dst) in enumerate(pairs)]
    for copy in arrivals:
        copy.start()
    copies = []

    def send(src, dst):
        copy = pltpu.make_async_copy(src, dst, sem.at[len(copies)])
        copy.start()
        copies.append(copy)

    def block(first, rows):
        return total_now.at[pl.ds(first, rows)]

    def lanes(ref, part):
        return ref.at[0, :, pl.ds(part * 128, 128)]

    arrivals[0].wait()
    for number, (ref, first) in enumerate(((b_qv, V_Q), (b_in, V_IN))):
        wide[number, :, :WIDTH] = small_now[first:first + 1, :]
        wide[number, :, WIDTH:] = small_now[first + 1:first + 2, :]
        send(wide.at[number], ref)
    for number, (ref, first) in enumerate((
        (b_out, V_OUT), (gain_one, V_GAIN1), (shift_one, V_SHIFT1), (b_back, V_BACK), (gain_two, V_GAIN2),
        (shift_two, V_SHIFT2),
    )):
        narrow[number] = small_now[first:first + 1, :]
        send(narrow.at[number], ref)
    arrivals[1].wait()
    for part in range(2):
        send(block(AT_BACK + 512 * part, 512), lanes(w_back, part))
    arrivals[2].wait()
    for part in range(4):
        send(block(AT_IN + 256 * part, 256), lanes(w_in, part))
    arrivals[3].wait()
    for part in range(2):
        send(block(AT_OUT + 256 * part, 256), lanes(w_out, part))
    for pair in range(2):
        arrivals[4 + pair].wait()
        for part in range(3):
            send(block(AT_PAIR + PAIR_ROWS * pair + 256 * part, 256), lanes(w_qkv, 2 * part + pair))
    for part in range(2):
        arrivals[6 + part].wait()
        send(final_now.at[part], final_out.at[part])
    for part in range(2):
        arrivals[8 + part].wait()
        send(grad_now.at[part], grad_out.at[part])
    for copy in copies:
        copy.wait()


def unpack(final_output, input_grad, total, small):
    anywhere = pl.BlockSpec(memory_space=pl.ANY)
    shapes = [
        (2, HALF, WIDTH), (2, HALF, WIDTH), (1, WIDTH, 3 * WIDTH), (1, 2 * WIDTH), (1, WIDTH, WIDTH), (1, WIDTH),
        (1, WIDTH), (1, WIDTH), (1, WIDTH, INNER), (1, INNER), (1, INNER, WIDTH), (1, WIDTH), (1, WIDTH), (1, WIDTH),
    ]
    return pl.pallas_call(
        unpack_kernel,
        out_shape=tuple(jax.ShapeDtypeStruct(dims, F32) for dims in shapes),
        in_specs=[anywhere] * 4,
        out_specs=tuple(anywhere for dims in shapes),
        scratch_shapes=[
            pltpu.VMEM((2, HALF, WIDTH), F32), pltpu.VMEM((2, HALF, WIDTH), F32), pltpu.VMEM((PACKED_ROWS, 128), F32),
            pltpu.VMEM((SMALL_ROWS, WIDTH), F32), pltpu.VMEM((2, 1, INNER), F32), pltpu.VMEM((6, 1, WIDTH), F32),
            pltpu.SemaphoreType.DMA((10,)), pltpu.SemaphoreType.DMA((26,)),
        ],
        compiler_params=pltpu.CompilerParams(vmem_limit_bytes=VMEM_BYTES),
        name="unpack",
    )(final_output, input_grad, total, small)


def body(
    activations, cotangent, cell_lengths, w_qkv, b_qv, w_out, b_out, gain_one, shift_one,
    w_in, b_in, w_back, b_back, gain_two, shift_two,
):
    return unpack(*relay(
        activations, cotangent, jnp.transpose(cell_lengths, (2, 1, 0)), w_qkv, w_out, w_in, w_back,
        b_qv, b_out, gain_one, shift_one, b_in, b_back, gain_two, shift_two))


def solution(mesh):
    rows = P(None, ("dp", "seq"), None)
    matrix = P("pipe", None, None)
    vector = P("pipe", None)
    in_specs = (
        rows, rows, P(None, "dp", None), matrix, vector, matrix, vector, vector, vector,
        matrix, vector, matrix, vector, vector, vector,
    )
    out_rows = P("pipe", ("dp", "seq"), None)
    out_specs = (
        out_rows, out_rows, matrix, vector, matrix, vector, vector, vector,
        matrix, vector, matrix, vector, vector, vector,
    )
    return jax.shard_map(body, mesh=mesh, in_specs=in_specs, out_specs=out_specs, check_vma=False)
```
